32 devices in a mesh: seq: 8 (over y, x, core), chan: 4 (over z).
Axes of the slice: x: 2, y: 2, z: 4, core: 2. Of those that a mesh axis runs over, the one named last changes fastest.
Arguments:
- outer_gate: bfloat16 [1024, 8192], P('chan', 'seq'), may hold values from -6 to 6
- inner_gate: bfloat16 [1024, 8192], P('chan', 'seq'), may hold values from -6 to 6
- signal: bfloat16 [1024, 8192], P('chan', 'seq'), may hold values from -6 to 6
- long_filter: bfloat16 [1024, 8192], P('chan', 'seq'), may hold values from -2 to 2
- grad_output: bfloat16 [8192, 8192], P('chan', 'seq'), may hold values from -6 to 6
- out_proj: bfloat16 [1024, 8192], P(None, 'chan'), may hold values from -0.0625 to 0.0625
Outputs:
- grad_outer: bfloat16 [1024, 8192], P('chan', 'seq')
- grad_inner: bfloat16 [1024, 8192], P('chan', 'seq')
- grad_signal: bfloat16 [1024, 8192], P('chan', 'seq')
- grad_filter: float32 [1024, 8192], P('chan', 'seq')
- grad_proj: float32 [1024, 8192], P('seq', 'chan')
The draws below stay inside these ranges and needn't reach their ends.
All inputs are finite; a program needn't handle non-finite values.
Results may differ from the reference program's by a relative error of at most 0.025.
Values may be sent and summed in bfloat16 or wider, within the bound.
No kernel may reach another device: no remote copies, remote signals or barrier semaphores. Data moves between devices by JAX's collectives and lax.ppermute only.
A program may use at most 128 MiB of HBM per device.

```python
import math
import jax
import jax.numpy as jnp
from jax import lax

C = 1024
D = 8192
TOKENS = 8192
N_CHAN = 4


def draw_long_filter(key, part):
    key = jax.random.fold_in(key, 7)
    rate_key, rough_key = jax.random.split(key, 2)
    lags = lax.broadcasted_iota(jnp.float32, (C, TOKENS), 1)
    log_rate = jax.random.uniform(rate_key, (C, 1), jnp.float32, math.log(0.5 / TOKENS), math.log(1.0 / 20.0))
    rough = jnp.clip(jax.random.normal(rough_key, (C, TOKENS), jnp.float32), -6.0, 6.0)
    rate = jnp.exp(log_rate)
    return (rough * jnp.exp(-rate * lags) * jnp.sqrt(2.0 * rate)).astype(jnp.bfloat16)


def steps_of(rng, extent, cuts, least, high):
    loudness = 1.0
    for position, parts in cuts:
        heights = jax.random.uniform(jax.random.fold_in(jax.random.fold_in(rng, 6), position), (parts,), jnp.float32, least / len(cuts), high / len(cuts))
        loudness = loudness * jnp.repeat(jnp.exp(heights), extent[position] // parts).reshape((-1,) + (1,) * (len(extent) - 1 - position))
    return loudness


def centred(key, dims, deviation, most, cuts=(), held_as=jnp.bfloat16):
    array = jax.random.normal(key, dims, jnp.float32) * deviation
    if len(cuts) > 0:
        array = steps_of(key, dims, cuts, -0.22, 0.18) * array
    return jnp.clip(array, min=-most, max=most).astype(held_as)


def setup_inputs(seed: int = 0) -> dict:
    streams_of = jax.random.split(jax.random.key(seed), 7)
    outer_gate = centred(streams_of[0], (C, TOKENS), 1.0, 6.0, ((0, 4), (1, 8)))
    inner_gate = centred(streams_of[1], (C, TOKENS), 1.0, 6.0, ((0, 4), (1, 8)))
    signal = centred(streams_of[2], (C, TOKENS), 1.0, 6.0, ((0, 4), (1, 8)))
    long_filter = draw_long_filter(jax.random.fold_in(streams_of[6], 71), 0)
    grad_output = centred(streams_of[4], (D, TOKENS), 1.0, 6.0, ((0, 4), (1, 8)))
    out_proj = centred(streams_of[5], (C, D), D ** -0.5, 0.0625, ((1, 4),))
    return dict(outer_gate=outer_gate, inner_gate=inner_gate, signal=signal, long_filter=long_filter, grad_output=grad_output, out_proj=out_proj)


def conv_block(blocks):
    mixed_in, kernel, grad_conv = blocks
    full_len = 2 * TOKENS
    sig_f = jnp.fft.rfft(mixed_in.astype(jnp.float32), n=full_len, axis=-1)
    ker_f = jnp.fft.rfft(kernel.astype(jnp.float32), n=full_len, axis=-1)
    grad_f = jnp.fft.rfft(grad_conv.astype(jnp.float32), n=full_len, axis=-1)
    conv_out = jnp.fft.irfft(ker_f * sig_f, n=full_len, axis=-1)[:, :TOKENS]
    grad_prod = jnp.fft.irfft(jnp.conj(ker_f) * grad_f, n=full_len, axis=-1)[:, :TOKENS]
    grad_kernel = jnp.fft.irfft(jnp.conj(sig_f) * grad_f, n=full_len, axis=-1)[:, :TOKENS]
    return conv_out.astype(jnp.float32), grad_prod.astype(jnp.float32), grad_kernel.astype(jnp.float32)


def reference(outer_gate, inner_gate, signal, long_filter, grad_output, out_proj):
    mixed_in = (inner_gate.astype(jnp.float32) * signal.astype(jnp.float32)).astype(jnp.bfloat16)
    group_size = D // N_CHAN

    def add_group(index, total):
        start = (index * group_size).astype(jnp.int32)
        cols = lax.dynamic_slice_in_dim(out_proj, start, group_size, 1)
        rows = lax.dynamic_slice_in_dim(grad_output, start, group_size, 0)
        partial_sum = jnp.dot(cols, rows, preferred_element_type=jnp.float32).astype(jnp.bfloat16)
        partial_sum = lax.optimization_barrier(partial_sum)
        return total + partial_sum.astype(jnp.float32)

    grad_mix = lax.fori_loop(0, N_CHAN, add_group, jnp.zeros((C, TOKENS), jnp.float32))
    grad_conv = (grad_mix * outer_gate.astype(jnp.float32)).astype(jnp.bfloat16)
    block_rows = 64
    shaped = (C // block_rows, block_rows, TOKENS)
    conv_out, grad_prod, grad_filter = lax.map(
        conv_block, (mixed_in.reshape(shaped), long_filter.reshape(shaped), grad_conv.reshape(shaped)))
    conv_out = conv_out.reshape(C, TOKENS)
    grad_prod = grad_prod.reshape(C, TOKENS)
    grad_filter = grad_filter.reshape(C, TOKENS)
    mixed = (outer_gate.astype(jnp.float32) * conv_out).astype(jnp.bfloat16)
    grad_proj = lax.dot_general(mixed, grad_output, (((1,), (1,)), ((), ())), preferred_element_type=jnp.float32)
    grad_outer = (grad_mix * conv_out).astype(jnp.bfloat16)
    grad_inner = (grad_prod * signal.astype(jnp.float32)).astype(jnp.bfloat16)
    grad_signal = (grad_prod * inner_gate.astype(jnp.float32)).astype(jnp.bfloat16)
    return grad_outer, grad_inner, grad_signal, grad_filter, grad_proj
```

```python
import functools
import math

import jax
import jax.numpy as jnp
import numpy as np
from jax import lax
from jax.experimental import pallas as pl
from jax.experimental.pallas import tpu as pltpu
from jax.sharding import PartitionSpec as P

LANES = 128
VMEM_BYTES = 48 * 1024 * 1024


def high_low(table, axis):
    high = table.astype(jnp.bfloat16)
    low = (table - high.astype(np.float64)).astype(jnp.bfloat16)
    return np.concatenate([high, low], axis=axis)


def dft_tables(tokens, blocks):
    outer = tokens // LANES
    per = outer // blocks
    freq = np.arange(outer) + 0.25
    angle = 2.0 * math.pi / outer * np.outer(freq, np.arange(outer))
    first = np.zeros((2, 2, outer, blocks, 2, per))
    last = np.zeros((blocks, 2, per, 2, 2, outer))
    for pair in range(2):
        first[pair, 0, :, :, pair, :] = np.cos(angle).reshape(outer, blocks, per)
        first[pair, 1, :, :, pair, :] = -np.sin(angle).reshape(outer, blocks, per)
        last[:, pair, :, pair, 0, :] = np.cos(angle.T).reshape(blocks, per, outer) / tokens
        last[:, pair, :, pair, 1, :] = -np.sin(angle.T).reshape(blocks, per, outer) / tokens
    first = high_low(first.reshape(4 * outer, 2 * outer), 1)
    last = high_low(last.reshape(2 * outer, 4 * outer), 1)
    turn = 2.0 * math.pi / tokens * np.outer(freq, np.arange(LANES))
    twiddle = np.stack([np.cos(turn), np.sin(turn)]).astype(np.float32)
    lane = 2.0 * math.pi / LANES * np.outer(np.arange(LANES), np.arange(LANES))
    cos, sin = np.cos(lane), np.sin(lane)
    forward = high_low(np.block([[cos, -sin], [sin, cos]]), 0)
    inverse = high_low(np.block([[cos, sin], [-sin, cos]]), 0)
    return first, forward, inverse, last, twiddle


def mxu(left, right):
    return jnp.dot(left, right, preferred_element_type=jnp.float32)


def forward_pair(pair_block, first, twiddle):
    outer = twiddle.shape[1]
    rows = pair_block.reshape(2 * outer, LANES)
    part = mxu(first, jnp.concatenate([rows, rows], axis=0))
    cos, sin = twiddle[0], twiddle[1]
    turned = []
    for pair in range(2):
        real = part[2 * pair * outer : (2 * pair + 1) * outer]
        imag = part[(2 * pair + 1) * outer : (2 * pair + 2) * outer]
        turned.append(
            jnp.concatenate([real * cos + imag * sin, imag * cos - real * sin], axis=1).astype(
                jnp.bfloat16
            )
        )
    return turned


def inverse_pair(spread, last, twiddle):
    cos, sin = twiddle[0], twiddle[1]
    parts = []
    for item in spread:
        real, imag = item[:, :LANES], item[:, LANES:]
        parts.append((real * cos - imag * sin).astype(jnp.bfloat16))
        parts.append((real * sin + imag * cos).astype(jnp.bfloat16))
    return mxu(last, jnp.concatenate(parts + parts, axis=0))


def lanes_dft(rows, table):
    return mxu(jnp.concatenate([rows, rows], axis=1), table)


def convolve_kernel(pairs_ref, first_ref, forward_ref, inverse_ref, last_ref, twiddle_ref,
                    conv_ref, signal_ref, filter_ref, turned, spread):
    outer = twiddle_ref.shape[1]
    step = pairs_ref.shape[1]
    twiddle = twiddle_ref[...]
    for chan in range(step):
        pieces = forward_pair(pairs_ref[:, chan], first_ref[...], twiddle)
        for pair in range(2):
            turned[pl.ds((pair * step + chan) * outer, outer), :] = pieces[pair]
    half = step * outer
    signal = lanes_dft(turned[pl.ds(0, half), :], forward_ref[...])
    kernel = lanes_dft(turned[pl.ds(half, half), :], forward_ref[...])
    signal_ref[...] = signal.reshape(signal_ref.shape)
    filter_ref[...] = kernel.reshape(filter_ref.shape)
    sr, si = signal[:, :LANES], signal[:, LANES:]
    kr, ki = kernel[:, :LANES], kernel[:, LANES:]
    product = jnp.concatenate([kr * sr - ki * si, kr * si + ki * sr], axis=1).astype(jnp.bfloat16)
    spread[...] = lanes_dft(product, inverse_ref[...])
    for pair in range(step // 2):
        items = [spread[pl.ds((2 * pair + one) * outer, outer), :] for one in range(2)]
        out = inverse_pair(items, last_ref[...], twiddle)
        conv_ref[:, pair] = out.reshape(conv_ref.shape[0], -1, LANES).astype(jnp.bfloat16)


def correlate_kernel(pairs_ref, signal_ref, filter_ref, first_ref, forward_ref, inverse_ref,
                     last_ref, twiddle_ref, out_ref, turned, spread):
    outer = twiddle_ref.shape[1]
    step = signal_ref.shape[0]
    twiddle = twiddle_ref[...]
    for pair in range(step // 2):
        pieces = forward_pair(pairs_ref[:, pair], first_ref[...], twiddle)
        for one in range(2):
            turned[pl.ds((2 * pair + one) * outer, outer), :] = pieces[one]
    half = step * outer
    grad = lanes_dft(turned[...], forward_ref[...])
    gr, gi = grad[:, :LANES], grad[:, LANES:]
    for place, ref in enumerate((filter_ref, signal_ref)):
        other = ref[...].reshape(half, 2 * LANES)
        kr, ki = other[:, :LANES], other[:, LANES:]
        product = jnp.concatenate([kr * gr + ki * gi, kr * gi - ki * gr], axis=1)
        spread[place] = lanes_dft(product.astype(jnp.bfloat16), inverse_ref[...])
    for chan in range(step):
        items = [spread[place, pl.ds(chan * outer, outer), :] for place in range(2)]
        out = inverse_pair(items, last_ref[...], twiddle)
        out_ref[:, chan] = out.reshape(out_ref.shape[0], -1, LANES).astype(jnp.bfloat16)


def whole(table):
    zeros = (0,) * table.ndim
    return pl.BlockSpec(table.shape, lambda i: zeros)


def convolve(pairs, tables, step=8):
    blocks, chans, rows, _ = pairs.shape
    outer = blocks * rows // 2
    spec = jax.ShapeDtypeStruct((chans, outer, 2 * LANES), jnp.float32)
    spec_block = pl.BlockSpec((step, outer, 2 * LANES), lambda i: (i, 0, 0))
    return pl.pallas_call(
        convolve_kernel,
        grid=(chans // step,),
        in_specs=[pl.BlockSpec((blocks, step, rows, LANES), lambda i: (0, i, 0, 0))]
        + [whole(table) for table in tables],
        out_specs=[
            pl.BlockSpec((blocks, step // 2, rows, LANES), lambda i: (0, i, 0, 0)),
            spec_block,
            spec_block,
        ],
        out_shape=[jax.ShapeDtypeStruct((blocks, chans // 2, rows, LANES), jnp.bfloat16), spec, spec],
        scratch_shapes=[
            pltpu.VMEM((2 * step * outer, 2 * LANES), jnp.bfloat16),
            pltpu.VMEM((step * outer, 2 * LANES), jnp.float32),
        ],
        compiler_params=pltpu.CompilerParams(vmem_limit_bytes=VMEM_BYTES),
        name="convolve",
    )(pairs, *tables)


def correlate(pairs, signal, kernel, tables, step=8):
    blocks, half, rows, _ = pairs.shape
    chans = 2 * half
    outer = blocks * rows // 2
    spec_block = pl.BlockSpec((step, outer, 2 * LANES), lambda i: (i, 0, 0))
    return pl.pallas_call(
        correlate_kernel,
        grid=(chans // step,),
        in_specs=[
            pl.BlockSpec((blocks, step // 2, rows, LANES), lambda i: (0, i, 0, 0)),
            spec_block,
            spec_block,
        ]
        + [whole(table) for table in tables],
        out_specs=pl.BlockSpec((blocks, step, rows, LANES), lambda i: (0, i, 0, 0)),
        out_shape=jax.ShapeDtypeStruct((blocks, chans, rows, LANES), jnp.bfloat16),
        scratch_shapes=[
            pltpu.VMEM((step * outer, 2 * LANES), jnp.bfloat16),
            pltpu.VMEM((2, step * outer, 2 * LANES), jnp.float32),
        ],
        compiler_params=pltpu.CompilerParams(vmem_limit_bytes=VMEM_BYTES),
        name="correlate",
    )(pairs, signal, kernel, *tables)


def body(outer_gate, inner_gate, signal, long_filter, grad_output, out_proj):
    seq_count = lax.axis_size("seq")
    chan_rows, block_len = outer_gate.shape
    owned = chan_rows // seq_count
    per = block_len // LANES
    tables = [jnp.asarray(t) for t in dft_tables(block_len * seq_count, seq_count)]

    def exchange(blocks):
        return lax.all_to_all(blocks, "seq", split_axis=0, concat_axis=0, tiled=True)

    def wide(x):
        return x.astype(jnp.float32)

    mixed_in = (wide(inner_gate) * wide(signal)).astype(jnp.bfloat16)
    pair = jnp.concatenate(
        [mixed_in.reshape(chan_rows, per, LANES), long_filter.reshape(chan_rows, per, LANES)], axis=1
    )
    pair = exchange(pair.reshape(seq_count, owned, 2 * per, LANES))
    conv, spec_signal, spec_filter = convolve(pair, tables)
    conv_out = wide(exchange(conv).reshape(chan_rows, block_len))
    mixed = (wide(outer_gate) * conv_out).astype(jnp.bfloat16)

    grad_mix = wide(
        lax.psum_scatter(
            jnp.dot(out_proj, grad_output, preferred_element_type=jnp.float32).astype(jnp.bfloat16),
            "chan",
            scatter_dimension=0,
            tiled=True,
        )
    )
    grad_conv = (grad_mix * wide(outer_gate)).astype(jnp.bfloat16)
    grad_outer = (grad_mix * conv_out).astype(jnp.bfloat16)
    corr = correlate(
        exchange(grad_conv.reshape(seq_count, owned // 2, 2 * per, LANES)),
        spec_signal,
        spec_filter,
        tables,
    )
    corr = exchange(corr).reshape(chan_rows, 2, block_len)
    grad_prod, grad_filter = wide(corr[:, 0]), wide(corr[:, 1])
    grad_inner = (grad_prod * wide(signal)).astype(jnp.bfloat16)
    grad_signal = (grad_prod * wide(inner_gate)).astype(jnp.bfloat16)

    mixed_all = lax.all_gather(mixed, "chan", axis=0, tiled=True)
    grad_proj = wide(
        lax.psum_scatter(
            lax.dot_general(
                mixed_all, grad_output, (((1,), (1,)), ((), ())), preferred_element_type=jnp.float32
            ).astype(jnp.bfloat16),
            "seq",
            scatter_dimension=0,
            tiled=True,
        )
    )
    return (grad_outer, grad_inner, grad_signal, grad_filter, grad_proj)


def solution(mesh):
    tokens = P("chan", "seq")
    in_specs = (tokens, tokens, tokens, tokens, tokens, P(None, "chan"))
    out_specs = (tokens, tokens, tokens, tokens, P("seq", "chan"))
    return jax.shard_map(body, mesh=mesh, in_specs=in_specs, out_specs=out_specs, check_vma=False)
```

```python
import functools
import math

import jax
import jax.numpy as jnp
import numpy as np
from jax import lax
from jax.experimental import pallas as pl
from jax.experimental.pallas import tpu as pltpu
from jax.sharding import PartitionSpec as P

LANES = 128
CHUNKS = 2
VMEM_BYTES = 48 * 1024 * 1024


def wide(x):
    return x.astype(jnp.float32)


def short(x):
    return x.astype(jnp.bfloat16)


def high_low(table, axis):
    high = table.astype(jnp.bfloat16)
    low = (table - high.astype(np.float64)).astype(jnp.bfloat16)
    return np.concatenate([high, low], axis=axis)


def dft_tables(tokens, blocks):
    outer = tokens // LANES
    per = outer // blocks
    freq = np.arange(outer) + 0.25
    angle = 2.0 * math.pi / outer * np.outer(freq, np.arange(outer))
    first = np.zeros((2, 2, outer, blocks, 2, per))
    last = np.zeros((blocks, 2, per, 2, 2, outer))
    for pair in range(2):
        first[pair, 0, :, :, pair, :] = np.cos(angle).reshape(outer, blocks, per)
        first[pair, 1, :, :, pair, :] = -np.sin(angle).reshape(outer, blocks, per)
        last[:, pair, :, pair, 0, :] = np.cos(angle.T).reshape(blocks, per, outer) / tokens
        last[:, pair, :, pair, 1, :] = -np.sin(angle.T).reshape(blocks, per, outer) / tokens
    first = high_low(first.reshape(4 * outer, 2 * outer), 1)
    last = high_low(last.reshape(2 * outer, 4 * outer), 1)
    turn = 2.0 * math.pi / tokens * np.outer(freq, np.arange(LANES))
    twiddle = np.stack([np.cos(turn), np.sin(turn)]).astype(np.float32)
    lane = 2.0 * math.pi / LANES * np.outer(np.arange(LANES), np.arange(LANES))
    cos, sin = np.cos(lane), np.sin(lane)
    forward = high_low(np.block([[cos, -sin], [sin, cos]]), 0)
    inverse = high_low(np.block([[cos, sin], [-sin, cos]]), 0)
    return first, forward, inverse, last, twiddle


def mxu(left, right):
    return jnp.dot(left, right, preferred_element_type=jnp.float32)


def forward_pair(pair_block, first, twiddle):
    outer = twiddle.shape[1]
    rows = pair_block.reshape(2 * outer, LANES)
    part = mxu(first, jnp.concatenate([rows, rows], axis=0))
    cos, sin = twiddle[0], twiddle[1]
    turned = []
    for pair in range(2):
        real = part[2 * pair * outer : (2 * pair + 1) * outer]
        imag = part[(2 * pair + 1) * outer : (2 * pair + 2) * outer]
        turned.append(
            jnp.concatenate([real * cos + imag * sin, imag * cos - real * sin], axis=1).astype(
                jnp.bfloat16
            )
        )
    return turned


def inverse_pair(spread, last, twiddle):
    cos, sin = twiddle[0], twiddle[1]
    parts = []
    for item in spread:
        real, imag = item[:, :LANES], item[:, LANES:]
        parts.append((real * cos - imag * sin).astype(jnp.bfloat16))
        parts.append((real * sin + imag * cos).astype(jnp.bfloat16))
    return mxu(last, jnp.concatenate(parts + parts, axis=0))


def lanes_dft(rows, table):
    return mxu(jnp.concatenate([rows, rows], axis=1), table)


def convolve_kernel(pairs_ref, first_ref, forward_ref, inverse_ref, last_ref, twiddle_ref,
                    conv_ref, signal_ref, filter_ref, turned, spread):
    outer = twiddle_ref.shape[1]
    step = pairs_ref.shape[1]
    twiddle = twiddle_ref[...]
    for chan in range(step):
        pieces = forward_pair(pairs_ref[:, chan], first_ref[...], twiddle)
        for pair in range(2):
            turned[pl.ds((pair * step + chan) * outer, outer), :] = pieces[pair]
    half = step * outer
    signal = lanes_dft(turned[pl.ds(0, half), :], forward_ref[...])
    kernel = lanes_dft(turned[pl.ds(half, half), :], forward_ref[...])
    signal_ref[...] = signal.reshape(signal_ref.shape)
    filter_ref[...] = kernel.reshape(filter_ref.shape)
    sr, si = signal[:, :LANES], signal[:, LANES:]
    kr, ki = kernel[:, :LANES], kernel[:, LANES:]
    product = jnp.concatenate([kr * sr - ki * si, kr * si + ki * sr], axis=1).astype(jnp.bfloat16)
    spread[...] = lanes_dft(product, inverse_ref[...])
    for pair in range(step // 2):
        items = [spread[pl.ds((2 * pair + one) * outer, outer), :] for one in range(2)]
        out = inverse_pair(items, last_ref[...], twiddle)
        conv_ref[:, pair] = out.reshape(conv_ref.shape[0], -1, LANES).astype(jnp.bfloat16)


def correlate_kernel(pairs_ref, signal_ref, filter_ref, first_ref, forward_ref, inverse_ref,
                     last_ref, twiddle_ref, out_ref, turned, spread):
    outer = twiddle_ref.shape[1]
    step = signal_ref.shape[0]
    twiddle = twiddle_ref[...]
    for pair in range(step // 2):
        pieces = forward_pair(pairs_ref[:, pair], first_ref[...], twiddle)
        for one in range(2):
            turned[pl.ds((2 * pair + one) * outer, outer), :] = pieces[one]
    half = step * outer
    grad = lanes_dft(turned[...], forward_ref[...])
    gr, gi = grad[:, :LANES], grad[:, LANES:]
    for place, ref in enumerate((filter_ref, signal_ref)):
        other = ref[...].reshape(half, 2 * LANES)
        kr, ki = other[:, :LANES], other[:, LANES:]
        product = jnp.concatenate([kr * gr + ki * gi, kr * gi - ki * gr], axis=1)
        spread[place] = lanes_dft(product.astype(jnp.bfloat16), inverse_ref[...])
    for chan in range(step):
        items = [spread[place, pl.ds(chan * outer, outer), :] for place in range(2)]
        out = inverse_pair(items, last_ref[...], twiddle)
        out_ref[:, chan] = out.reshape(out_ref.shape[0], -1, LANES).astype(jnp.bfloat16)


def whole(table):
    zeros = (0,) * table.ndim
    return pl.BlockSpec(table.shape, lambda i: zeros)


def convolve(pairs, tables):
    blocks, chans, rows, _ = pairs.shape
    step = min(8, chans)
    outer = blocks * rows // 2
    spec = jax.ShapeDtypeStruct((chans, outer, 2 * LANES), jnp.float32)
    spec_block = pl.BlockSpec((step, outer, 2 * LANES), lambda i: (i, 0, 0))
    return pl.pallas_call(
        convolve_kernel,
        grid=(chans // step,),
        in_specs=[pl.BlockSpec((blocks, step, rows, LANES), lambda i: (0, i, 0, 0))]
        + [whole(table) for table in tables],
        out_specs=[
            pl.BlockSpec((blocks, step // 2, rows, LANES), lambda i: (0, i, 0, 0)),
            spec_block,
            spec_block,
        ],
        out_shape=[jax.ShapeDtypeStruct((blocks, chans // 2, rows, LANES), jnp.bfloat16), spec, spec],
        scratch_shapes=[
            pltpu.VMEM((2 * step * outer, 2 * LANES), jnp.bfloat16),
            pltpu.VMEM((step * outer, 2 * LANES), jnp.float32),
        ],
        compiler_params=pltpu.CompilerParams(vmem_limit_bytes=VMEM_BYTES),
        name="convolve",
    )(pairs, *tables)


def correlate(pairs, signal, kernel, tables):
    blocks, _, rows, _ = pairs.shape
    chans = signal.shape[0]
    step = min(8, chans)
    outer = blocks * rows // 2
    spec_block = pl.BlockSpec((step, outer, 2 * LANES), lambda i: (i, 0, 0))
    return pl.pallas_call(
        correlate_kernel,
        grid=(chans // step,),
        in_specs=[
            pl.BlockSpec((blocks, step // 2, rows, LANES), lambda i: (0, i, 0, 0)),
            spec_block,
            spec_block,
        ]
        + [whole(table) for table in tables],
        out_specs=pl.BlockSpec((blocks, step, rows, LANES), lambda i: (0, i, 0, 0)),
        out_shape=jax.ShapeDtypeStruct((blocks, chans, rows, LANES), jnp.bfloat16),
        scratch_shapes=[
            pltpu.VMEM((step * outer, 2 * LANES), jnp.bfloat16),
            pltpu.VMEM((2, step * outer, 2 * LANES), jnp.float32),
        ],
        compiler_params=pltpu.CompilerParams(vmem_limit_bytes=VMEM_BYTES),
        name="correlate",
    )(pairs, signal, kernel, *tables)


def params():
    return pltpu.CompilerParams(vmem_limit_bytes=VMEM_BYTES)


def spread_lanes(target, rows, first, stride):
    count = rows.shape[0]
    for lane in range(rows.shape[1] // LANES):
        target[pl.ds(first + lane, count, stride=stride), :] = rows[:, lane * LANES : (lane + 1) * LANES]


def prepare_kernel(gate_ref, signal_ref, filter_ref, pair_ref, lines):
    per = gate_ref.shape[1] // LANES
    spread_lanes(lines, short(wide(gate_ref[...]) * wide(signal_ref[...])).astype(jnp.float32), 0, 2 * per)
    spread_lanes(lines, wide(filter_ref[...]), per, 2 * per)
    pair_ref[...] = short(lines[...]).reshape(pair_ref.shape)


def prepare(inner_gate, signal, long_filter):
    rows, length = signal.shape
    per = length // LANES
    step = rows // 4
    block = pl.BlockSpec((step, length), lambda i: (i, 0))
    return pl.pallas_call(
        prepare_kernel,
        grid=(4,),
        in_specs=[block] * 3,
        out_specs=pl.BlockSpec((step, 2 * per, LANES), lambda i: (i, 0, 0)),
        out_shape=jax.ShapeDtypeStruct((rows, 2 * per, LANES), jnp.bfloat16),
        scratch_shapes=[pltpu.VMEM((step * 2 * per, LANES), jnp.float32)],
        compiler_params=params(),
        name="prepare",
    )(inner_gate, signal, long_filter)


def mix_kernel(conv_ref, gate_ref, *refs):
    mixed_refs, out_ref, lines = refs[:CHUNKS], refs[CHUNKS], refs[CHUNKS + 1]
    rows, length = gate_ref.shape
    per = length // LANES
    lines[...] = wide(conv_ref[...].reshape(rows * per, LANES))
    small = rows // CHUNKS
    for lane in range(per):
        cols = slice(lane * LANES, (lane + 1) * LANES)
        conv = lines[pl.ds(lane, rows, stride=per), :]
        out_ref[:, cols] = short(conv)
        mixed = short(conv * wide(gate_ref[:, cols]))
        for cut in range(CHUNKS):
            mixed_refs[cut][:, cols] = mixed[cut * small : (cut + 1) * small]


def mix(conv, outer_gate):
    rows, length = outer_gate.shape
    per = length // LANES
    conv = conv.reshape(rows * per // 16, 16, LANES)
    step = rows // 2
    token_rows = pl.BlockSpec((step, length), lambda i: (i, 0))
    cut_rows = pl.BlockSpec((step // CHUNKS, length), lambda i: (i, 0))
    return pl.pallas_call(
        mix_kernel,
        grid=(2,),
        in_specs=[pl.BlockSpec((step * per // 16, 16, LANES), lambda i: (i, 0, 0)), token_rows],
        out_specs=[cut_rows] * CHUNKS + [token_rows],
        out_shape=[jax.ShapeDtypeStruct((rows // CHUNKS, length), jnp.bfloat16)] * CHUNKS
        + [jax.ShapeDtypeStruct((rows, length), jnp.bfloat16)],
        scratch_shapes=[pltpu.VMEM((step * per, LANES), jnp.float32)],
        compiler_params=params(),
        name="mix",
    )(conv, outer_gate)


def regard_kernel(*refs):
    *share_refs, gate_ref, conv_ref, outer_ref, grad_ref, lines = refs
    per = gate_ref.shape[1] // LANES
    grad_mix = wide(share_refs[0][...])
    for ref in share_refs[1:]:
        grad_mix = grad_mix + wide(ref[...])
    outer_ref[...] = short(grad_mix * wide(conv_ref[...]))
    spread_lanes(lines, grad_mix * wide(gate_ref[...]), 0, per)
    grad_ref[...] = short(lines[...]).reshape(grad_ref.shape)


def regard(shares, outer_gate, conv_out):
    rows, length = outer_gate.shape
    per = length // LANES
    step = rows // 2
    block = pl.BlockSpec((step, length), lambda i: (i, 0))
    return pl.pallas_call(
        regard_kernel,
        grid=(2,),
        in_specs=[block] * (len(shares) + 2),
        out_specs=[block, pl.BlockSpec((step * per // 16, 16, LANES), lambda i: (i, 0, 0))],
        out_shape=[
            jax.ShapeDtypeStruct((rows, length), jnp.bfloat16),
            jax.ShapeDtypeStruct((rows * per // 16, 16, LANES), jnp.bfloat16),
        ],
        scratch_shapes=[pltpu.VMEM((step * per, LANES), jnp.float32)],
        compiler_params=params(),
        name="regard",
    )(*shares, outer_gate, conv_out)


def finish_kernel(corr_ref, signal_ref, gate_ref, inner_ref, signal_out_ref, filter_ref, lines):
    rows, length = signal_ref.shape
    per = length // LANES
    lines[...] = wide(corr_ref[...].reshape(rows * 2 * per, LANES))
    for lane in range(per):
        cols = slice(lane * LANES, (lane + 1) * LANES)
        grad_prod = lines[pl.ds(lane, rows, stride=2 * per), :]
        filter_ref[:, cols] = lines[pl.ds(per + lane, rows, stride=2 * per), :]
        inner_ref[:, cols] = short(grad_prod * wide(signal_ref[:, cols]))
        signal_out_ref[:, cols] = short(grad_prod * wide(gate_ref[:, cols]))


def finish(corr, signal, inner_gate):
    rows, length = signal.shape
    per = length // LANES
    step = rows // 2
    block = pl.BlockSpec((step, length), lambda i: (i, 0))
    return pl.pallas_call(
        finish_kernel,
        grid=(2,),
        in_specs=[pl.BlockSpec((step, 2 * per, LANES), lambda i: (i, 0, 0)), block, block],
        out_specs=[block] * 3,
        out_shape=[jax.ShapeDtypeStruct((rows, length), jnp.bfloat16)] * 2
        + [jax.ShapeDtypeStruct((rows, length), jnp.float32)],
        scratch_shapes=[pltpu.VMEM((step * 2 * per, LANES), jnp.float32)],
        compiler_params=params(),
        name="finish",
    )(corr.reshape(rows, 2 * per, LANES), signal, inner_gate)


def unproject_kernel(count, place_ref, *refs):
    grad_ref = refs[count]
    for row in range(count):
        refs[count + 1 + row][...] = short(mxu(refs[row][...], grad_ref[...]))


def unproject(out_proj, grad_output, offsets, place, count):
    width, length = grad_output.shape
    rows = out_proj.shape[0] // count
    step = 256
    in_specs = [
        pl.BlockSpec((rows, width), lambda i, at, by=by: (lax.rem(at[0] + by, count), 0))
        for by in offsets
    ]
    return pl.pallas_call(
        functools.partial(unproject_kernel, len(offsets)),
        grid_spec=pltpu.PrefetchScalarGridSpec(
            num_scalar_prefetch=1,
            grid=(length // step,),
            in_specs=in_specs + [pl.BlockSpec((width, step), lambda i, at: (0, i))],
            out_specs=[pl.BlockSpec((rows, step), lambda i, at: (0, i))] * len(offsets),
        ),
        out_shape=[jax.ShapeDtypeStruct((rows, length), jnp.bfloat16)] * len(offsets),
        compiler_params=params(),
        name="unproject",
    )(place.reshape(1), *[out_proj] * len(offsets), grad_output)


def project_kernel(core_ref, *refs):
    *piece_refs, grad_ref, other_ref, mine_ref = refs
    small = mine_ref.shape[1]
    for ref, which in ((other_ref, 1 - core_ref[0]), (mine_ref, core_ref[0])):
        first = pl.multiple_of(which * small, small)
        rows = jnp.concatenate([piece[pl.ds(first, small), :] for piece in piece_refs], axis=0)
        out = lax.dot_general(
            rows, grad_ref[...], (((1,), (1,)), ((), ())), preferred_element_type=jnp.float32
        )
        ref[...] = short(out).reshape(ref.shape)


def project(pieces, grad_output, core):
    width, length = grad_output.shape
    small = pieces[0].shape[0] // 2
    step = 512
    out_block = pl.BlockSpec((len(pieces), small, step), lambda i, at: (0, 0, i))
    out = jax.ShapeDtypeStruct((len(pieces), small, width), jnp.bfloat16)
    return pl.pallas_call(
        project_kernel,
        grid_spec=pltpu.PrefetchScalarGridSpec(
            num_scalar_prefetch=1,
            grid=(width // step,),
            in_specs=[pl.BlockSpec(pieces[0].shape, lambda i, at: (0, 0))] * len(pieces)
            + [pl.BlockSpec((step, length), lambda i, at: (i, 0))],
            out_specs=[out_block, out_block],
        ),
        out_shape=[out, out],
        compiler_params=params(),
        name="project",
    )(core.reshape(1), *pieces, grad_output)


def pick_kernel(order_ref, mine_ref, got_ref, *out_refs):
    for slot, ref in enumerate(out_refs):
        at = order_ref[slot]
        ref[...] = short(wide(mine_ref[at]) + wide(got_ref[at]))


def pick(mine, got, order):
    count, small, width = mine.shape
    step = width // 2
    block = pl.BlockSpec((count, small, step), lambda i, at: (0, 0, i))
    return pl.pallas_call(
        pick_kernel,
        grid_spec=pltpu.PrefetchScalarGridSpec(
            num_scalar_prefetch=1,
            grid=(2,),
            in_specs=[block, block],
            out_specs=[pl.BlockSpec((small, step), lambda i, at: (0, i))] * count,
        ),
        out_shape=[jax.ShapeDtypeStruct((small, width), jnp.bfloat16)] * count,
        compiler_params=params(),
        name="pick",
    )(order, mine, got)


def swaps(count, bit):
    return [(place, place ^ bit) for place in range(count)]


def exchange(blocks):
    return lax.all_to_all(blocks, "seq", split_axis=0, concat_axis=0, tiled=True)


def tie(first, *others):
    return lax.optimization_barrier((first,) + others)[0]


def shift(block, by):
    count = lax.axis_size("chan")
    return lax.ppermute(block, "chan", [(i, (i + by) % count) for i in range(count)])


def gather_first(shard):
    count, place = lax.axis_size("chan"), lax.axis_index("chan")
    if count != 4:
        return [shard] + [shift(shard, by) for by in range(1, count)]
    low, high = shift(shard, 1), shift(shard, 3)
    return [lax.select_n(place, shard, high, low, shard), shard, low, high]


def gather_second(held):
    if lax.axis_size("chan") == 4:
        passed, shard, low, high = held
        return [shard, low, lax.ppermute(passed, "chan", [(0, 2), (3, 1), (2, 3), (1, 0)]), high]
    return held


def scatter_seq(other, mine):
    count, chips = lax.axis_size("seq"), lax.axis_size("chan")
    line, chip = lax.axis_index("chan"), lax.axis_index("seq") // 2
    got = lax.ppermute(other, "seq", swaps(count, 1))
    bits = sorted(range(1, chips), key=lambda bit: (-bin(bit).count("1"), bit)) + [0]
    order = jnp.stack([lax.rem(line - (chip ^ bit) + chips, chips) for bit in bits])
    blocks = pick(mine, got, order.astype(jnp.int32))
    return [
        lax.ppermute(block, "seq", swaps(count, 2 * bit)) for block, bit in zip(blocks, bits[:-1])
    ] + [blocks[-1]]


def sum_of(parts):
    total = wide(parts[0])
    for part in parts[1:]:
        total = total + wide(part)
    return total


def body(outer_gate, inner_gate, signal, long_filter, grad_output, out_proj):
    seq_count, chan_count = lax.axis_size("seq"), lax.axis_size("chan")
    chan_rows, block_len = outer_gate.shape
    owned = chan_rows // seq_count
    per = block_len // LANES
    line = lax.axis_index("chan")
    core = lax.axis_index("seq") % 2
    tables = [jnp.asarray(t) for t in dft_tables(block_len * seq_count, seq_count)]

    pair = prepare(inner_gate, signal, long_filter).reshape(seq_count, owned, 2 * per, LANES)
    sent = exchange(pair)

    weights = tie(out_proj, pair)
    if chan_count == 4:
        far = unproject(weights, grad_output, [2], line, chan_count)[0]
        near = unproject(tie(weights, far), grad_output, [0, 1, 3], line, chan_count)
        far = lax.ppermute(far, "chan", [(2, 0), (1, 3), (3, 2), (0, 1)])
        sent = tie(sent, *near)
        none = jnp.zeros_like(far)
        up = shift(short(wide(near[1]) + wide(jnp.where(line == 1, far, none))), 1)
        down = shift(short(wide(near[2]) + wide(jnp.where(line == 2, far, none))), 3)
        ends = jnp.where((line == 0) | (line == 3), far, none)
        shares = [near[0], up, down, ends]
    else:
        blocks = unproject(weights, grad_output, list(range(chan_count)), line, chan_count)
        shares = [blocks[0]] + [shift(block, by) for by, block in enumerate(blocks) if by > 0]

    conv, spec_signal, spec_filter = convolve(sent, tables)
    *mixed, conv_out = mix(exchange(conv), outer_gate)
    held = [gather_first(part) for part in mixed]
    held, shares = lax.optimization_barrier((held, shares))

    grad_outer, grad_conv = regard(shares, outer_gate, conv_out)
    grad_conv = grad_conv.reshape(seq_count, owned // 2, 2 * per, LANES)
    pieces = [gather_second(part) for part in held]
    pieces[0] = tie(pieces[0], grad_conv)
    projs = [scatter_seq(*project(pieces[0], grad_output, core))]
    corr = correlate(exchange(grad_conv), spec_signal, spec_filter, tables)
    pieces[1] = tie(pieces[1], corr)
    projs.append(scatter_seq(*project(pieces[1], grad_output, core)))

    grad_inner, grad_signal, grad_filter = finish(exchange(corr), signal, inner_gate)
    grad_proj = jnp.concatenate([sum_of(parts) for parts in projs], axis=0)
    return (grad_outer, grad_inner, grad_signal, grad_filter, grad_proj)


def solution(mesh):
    tokens = P("chan", "seq")
    in_specs = (tokens, tokens, tokens, tokens, tokens, P(None, "chan"))
    out_specs = (tokens, tokens, tokens, tokens, P("seq", "chan"))
    return jax.shard_map(body, mesh=mesh, in_specs=in_specs, out_specs=out_specs, check_vma=False)
```

```python
import functools
import math

import jax
import jax.numpy as jnp
import numpy as np
from jax import lax
from jax.experimental import pallas as pl
from jax.experimental.pallas import tpu as pltpu
from jax.sharding import PartitionSpec as P

LANES = 128
CHUNKS = 2
VMEM_BYTES = 48 * 1024 * 1024


def wide(x):
    return x.astype(jnp.float32)


def short(x):
    return x.astype(jnp.bfloat16)


def held_in_hbm(*arrays):
    return [pltpu.with_memory_space_constraint(array, pltpu.HBM) for array in arrays]


def in_hbm(shape, dtype=jnp.bfloat16):
    return pltpu.HBM(shape, dtype)


def high_low(table, axis):
    high = table.astype(jnp.bfloat16)
    low = (table - high.astype(np.float64)).astype(jnp.bfloat16)
    return np.concatenate([high, low], axis=axis)


def dft_tables(tokens, blocks):
    outer = tokens // LANES
    per = outer // blocks
    freq = np.arange(outer) + 0.25
    angle = 2.0 * math.pi / outer * np.outer(freq, np.arange(outer))
    first = np.zeros((2, 2, outer, blocks, 2, per))
    last = np.zeros((blocks, 2, per, 2, 2, outer))
    for pair in range(2):
        first[pair, 0, :, :, pair, :] = np.cos(angle).reshape(outer, blocks, per)
        first[pair, 1, :, :, pair, :] = -np.sin(angle).reshape(outer, blocks, per)
        last[:, pair, :, pair, 0, :] = np.cos(angle.T).reshape(blocks, per, outer) / tokens
        last[:, pair, :, pair, 1, :] = -np.sin(angle.T).reshape(blocks, per, outer) / tokens
    first = high_low(first.reshape(4 * outer, 2 * outer), 1)
    last = high_low(last.reshape(2 * outer, 4 * outer), 1)
    turn = 2.0 * math.pi / tokens * np.outer(freq, np.arange(LANES))
    twiddle = np.stack([np.cos(turn), np.sin(turn)]).astype(np.float32)
    lane = 2.0 * math.pi / LANES * np.outer(np.arange(LANES), np.arange(LANES))
    cos, sin = np.cos(lane), np.sin(lane)
    forward = high_low(np.block([[cos, -sin], [sin, cos]]), 0)
    inverse = high_low(np.block([[cos, sin], [-sin, cos]]), 0)
    return first, forward, inverse, last, twiddle


def mxu(left, right):
    return jnp.dot(left, right, preferred_element_type=jnp.float32)


def forward_pair(pair_block, first, twiddle):
    outer = twiddle.shape[1]
    rows = pair_block.reshape(2 * outer, LANES)
    part = mxu(first, jnp.concatenate([rows, rows], axis=0))
    cos, sin = twiddle[0], twiddle[1]
    turned = []
    for pair in range(2):
        real = part[2 * pair * outer : (2 * pair + 1) * outer]
        imag = part[(2 * pair + 1) * outer : (2 * pair + 2) * outer]
        turned.append(
            jnp.concatenate([real * cos + imag * sin, imag * cos - real * sin], axis=1).astype(
                jnp.bfloat16
            )
        )
    return turned


def inverse_pair(spread, last, twiddle):
    cos, sin = twiddle[0], twiddle[1]
    parts = []
    for item in spread:
        real, imag = item[:, :LANES], item[:, LANES:]
        parts.append((real * cos - imag * sin).astype(jnp.bfloat16))
        parts.append((real * sin + imag * cos).astype(jnp.bfloat16))
    return mxu(last, jnp.concatenate(parts + parts, axis=0))


def lanes_dft(rows, table):
    return mxu(jnp.concatenate([rows, rows], axis=1), table)


def convolve_kernel(pairs_ref, first_ref, forward_ref, inverse_ref, last_ref, twiddle_ref,
                    conv_ref, signal_ref, filter_ref, turned, spread):
    outer = twiddle_ref.shape[1]
    step = pairs_ref.shape[1]
    twiddle = twiddle_ref[...]
    for chan in range(step):
        pieces = forward_pair(pairs_ref[:, chan], first_ref[...], twiddle)
        for pair in range(2):
            turned[pl.ds((pair * step + chan) * outer, outer), :] = pieces[pair]
    half = step * outer
    signal = lanes_dft(turned[pl.ds(0, half), :], forward_ref[...])
    kernel = lanes_dft(turned[pl.ds(half, half), :], forward_ref[...])
    signal_ref[...] = signal.reshape(signal_ref.shape)
    filter_ref[...] = kernel.reshape(filter_ref.shape)
    sr, si = signal[:, :LANES], signal[:, LANES:]
    kr, ki = kernel[:, :LANES], kernel[:, LANES:]
    product = jnp.concatenate([kr * sr - ki * si, kr * si + ki * sr], axis=1).astype(jnp.bfloat16)
    spread[...] = lanes_dft(product, inverse_ref[...])
    for pair in range(step // 2):
        items = [spread[pl.ds((2 * pair + one) * outer, outer), :] for one in range(2)]
        out = inverse_pair(items, last_ref[...], twiddle)
        conv_ref[:, pair] = out.reshape(conv_ref.shape[0], -1, LANES).astype(jnp.bfloat16)


def correlate_kernel(pairs_ref, signal_ref, filter_ref, first_ref, forward_ref, inverse_ref,
                     last_ref, twiddle_ref, out_ref, turned, spread):
    outer = twiddle_ref.shape[1]
    step = signal_ref.shape[0]
    twiddle = twiddle_ref[...]
    for pair in range(step // 2):
        pieces = forward_pair(pairs_ref[:, pair], first_ref[...], twiddle)
        for one in range(2):
            turned[pl.ds((2 * pair + one) * outer, outer), :] = pieces[one]
    half = step * outer
    grad = lanes_dft(turned[...], forward_ref[...])
    gr, gi = grad[:, :LANES], grad[:, LANES:]
    for place, ref in enumerate((filter_ref, signal_ref)):
        other = ref[...].reshape(half, 2 * LANES)
        kr, ki = other[:, :LANES], other[:, LANES:]
        product = jnp.concatenate([kr * gr + ki * gi, kr * gi - ki * gr], axis=1)
        spread[place] = lanes_dft(product.astype(jnp.bfloat16), inverse_ref[...])
    for chan in range(step):
        items = [spread[place, pl.ds(chan * outer, outer), :] for place in range(2)]
        out = inverse_pair(items, last_ref[...], twiddle)
        out_ref[:, chan] = out.reshape(out_ref.shape[0], -1, LANES).astype(jnp.bfloat16)


def whole(table):
    zeros = (0,) * table.ndim
    return pl.BlockSpec(table.shape, lambda i: zeros)


def convolve(pairs, tables):
    blocks, chans, rows, _ = pairs.shape
    step = min(8, chans)
    outer = blocks * rows // 2
    spec = in_hbm((chans, outer, 2 * LANES), jnp.float32)
    spec_block = pl.BlockSpec((step, outer, 2 * LANES), lambda i: (i, 0, 0))
    return pl.pallas_call(
        convolve_kernel,
        grid=(chans // step,),
        in_specs=[pl.BlockSpec((blocks, step, rows, LANES), lambda i: (0, i, 0, 0))]
        + [whole(table) for table in tables],
        out_specs=[
            pl.BlockSpec((blocks, step // 2, rows, LANES), lambda i: (0, i, 0, 0)),
            spec_block,
            spec_block,
        ],
        out_shape=[in_hbm((blocks, chans // 2, rows, LANES)), spec, spec],
        scratch_shapes=[
            pltpu.VMEM((2 * step * outer, 2 * LANES), jnp.bfloat16),
            pltpu.VMEM((step * outer, 2 * LANES), jnp.float32),
        ],
        compiler_params=pltpu.CompilerParams(vmem_limit_bytes=VMEM_BYTES),
        name="convolve",
    )(*held_in_hbm(pairs, *tables))


def correlate(pairs, signal, kernel, tables):
    blocks, _, rows, _ = pairs.shape
    chans = signal.shape[0]
    step = min(8, chans)
    outer = blocks * rows // 2
    spec_block = pl.BlockSpec((step, outer, 2 * LANES), lambda i: (i, 0, 0))
    return pl.pallas_call(
        correlate_kernel,
        grid=(chans // step,),
        in_specs=[
            pl.BlockSpec((blocks, step // 2, rows, LANES), lambda i: (0, i, 0, 0)),
            spec_block,
            spec_block,
        ]
        + [whole(table) for table in tables],
        out_specs=pl.BlockSpec((blocks, step, rows, LANES), lambda i: (0, i, 0, 0)),
        out_shape=in_hbm((blocks, chans, rows, LANES)),
        scratch_shapes=[
            pltpu.VMEM((step * outer, 2 * LANES), jnp.bfloat16),
            pltpu.VMEM((2, step * outer, 2 * LANES), jnp.float32),
        ],
        compiler_params=pltpu.CompilerParams(vmem_limit_bytes=VMEM_BYTES),
        name="correlate",
    )(*held_in_hbm(pairs, signal, kernel, *tables))


def params():
    return pltpu.CompilerParams(vmem_limit_bytes=VMEM_BYTES)


def spread_lanes(target, rows, first, stride):
    count = rows.shape[0]
    for lane in range(rows.shape[1] // LANES):
        target[pl.ds(first + lane, count, stride=stride), :] = rows[:, lane * LANES : (lane + 1) * LANES]


def prepare_kernel(gate_ref, signal_ref, filter_ref, pair_ref, lines):
    per = gate_ref.shape[1] // LANES
    spread_lanes(lines, short(wide(gate_ref[...]) * wide(signal_ref[...])).astype(jnp.float32), 0, 2 * per)
    spread_lanes(lines, wide(filter_ref[...]), per, 2 * per)
    pair_ref[...] = short(lines[...]).reshape(pair_ref.shape)


def prepare(inner_gate, signal, long_filter):
    rows, length = signal.shape
    per = length // LANES
    step = rows // 4
    block = pl.BlockSpec((step, length), lambda i: (i, 0))
    return pl.pallas_call(
        prepare_kernel,
        grid=(4,),
        in_specs=[block] * 3,
        out_specs=pl.BlockSpec((step, 2 * per, LANES), lambda i: (i, 0, 0)),
        out_shape=in_hbm((rows, 2 * per, LANES)),
        scratch_shapes=[pltpu.VMEM((step * 2 * per, LANES), jnp.float32)],
        compiler_params=params(),
        name="prepare",
    )(*held_in_hbm(inner_gate, signal, long_filter))


def mix_kernel(conv_ref, gate_ref, *refs):
    mixed_refs, out_ref, lines = refs[:CHUNKS], refs[CHUNKS], refs[CHUNKS + 1]
    rows, length = gate_ref.shape
    per = length // LANES
    lines[...] = wide(conv_ref[...].reshape(rows * per, LANES))
    small = rows // CHUNKS
    for lane in range(per):
        cols = slice(lane * LANES, (lane + 1) * LANES)
        conv = lines[pl.ds(lane, rows, stride=per), :]
        out_ref[:, cols] = short(conv)
        mixed = short(conv * wide(gate_ref[:, cols]))
        for cut in range(CHUNKS):
            mixed_refs[cut][:, cols] = mixed[cut * small : (cut + 1) * small]


def mix(conv, outer_gate):
    rows, length = outer_gate.shape
    per = length // LANES
    conv = conv.reshape(rows * per // 16, 16, LANES)
    step = rows // 2
    token_rows = pl.BlockSpec((step, length), lambda i: (i, 0))
    cut_rows = pl.BlockSpec((step // CHUNKS, length), lambda i: (i, 0))
    return pl.pallas_call(
        mix_kernel,
        grid=(2,),
        in_specs=[pl.BlockSpec((step * per // 16, 16, LANES), lambda i: (i, 0, 0)), token_rows],
        out_specs=[cut_rows] * CHUNKS + [token_rows],
        out_shape=[in_hbm((rows // CHUNKS, length))] * CHUNKS + [in_hbm((rows, length))],
        scratch_shapes=[pltpu.VMEM((step * per, LANES), jnp.float32)],
        compiler_params=params(),
        name="mix",
    )(conv, outer_gate)


def regard_kernel(flag_ref, *refs):
    *share_refs, gate_ref, conv_ref, outer_ref, grad_ref, lines = refs
    per = gate_ref.shape[1] // LANES
    grad_mix = wide(share_refs[0][...])
    for ref in share_refs[1:-1]:
        grad_mix = grad_mix + wide(ref[...])
    last = wide(share_refs[-1][...])
    grad_mix = grad_mix + jnp.where(flag_ref[0] != 0, last, jnp.zeros_like(last))
    outer_ref[...] = short(grad_mix * wide(conv_ref[...]))
    spread_lanes(lines, grad_mix * wide(gate_ref[...]), 0, per)
    grad_ref[...] = short(lines[...]).reshape(grad_ref.shape)


def regard(shares, flag, outer_gate, conv_out):
    rows, length = outer_gate.shape
    per = length // LANES
    step = rows // 2
    block = pl.BlockSpec((step, length), lambda i, at: (i, 0))
    return pl.pallas_call(
        regard_kernel,
        grid_spec=pltpu.PrefetchScalarGridSpec(
            num_scalar_prefetch=1,
            grid=(2,),
            in_specs=[block] * (len(shares) + 2),
            out_specs=[block, pl.BlockSpec((step * per // 16, 16, LANES), lambda i, at: (i, 0, 0))],
            scratch_shapes=[pltpu.VMEM((step * per, LANES), jnp.float32)],
        ),
        out_shape=[in_hbm((rows, length)), in_hbm((rows * per // 16, 16, LANES))],
        compiler_params=params(),
        name="regard",
    )(flag.astype(jnp.int32).reshape(1), *held_in_hbm(*shares, outer_gate, conv_out))


def finish_kernel(corr_ref, signal_ref, gate_ref, inner_ref, signal_out_ref, filter_ref, lines):
    rows, length = signal_ref.shape
    per = length // LANES
    lines[...] = wide(corr_ref[...].reshape(rows * 2 * per, LANES))
    for lane in range(per):
        cols = slice(lane * LANES, (lane + 1) * LANES)
        grad_prod = lines[pl.ds(lane, rows, stride=2 * per), :]
        filter_ref[:, cols] = lines[pl.ds(per + lane, rows, stride=2 * per), :]
        inner_ref[:, cols] = short(grad_prod * wide(signal_ref[:, cols]))
        signal_out_ref[:, cols] = short(grad_prod * wide(gate_ref[:, cols]))


def finish(corr, signal, inner_gate):
    rows, length = signal.shape
    per = length // LANES
    step = rows // 2
    block = pl.BlockSpec((step, length), lambda i: (i, 0))
    return pl.pallas_call(
        finish_kernel,
        grid=(2,),
        in_specs=[pl.BlockSpec((step, 2 * per, LANES), lambda i: (i, 0, 0)), block, block],
        out_specs=[block] * 3,
        out_shape=[jax.ShapeDtypeStruct((rows, length), jnp.bfloat16)] * 2
        + [jax.ShapeDtypeStruct((rows, length), jnp.float32)],
        scratch_shapes=[pltpu.VMEM((step * 2 * per, LANES), jnp.float32)],
        compiler_params=params(),
        name="finish",
    )(*held_in_hbm(corr.reshape(rows, 2 * per, LANES), signal, inner_gate))


def unproject_kernel(count, place_ref, *refs):
    rows, width = refs[0].shape
    grad_ref, weights = refs[count], refs[-1]

    @pl.when(pl.program_id(0) == 0)
    def _():
        for row in range(count):
            weights[pl.ds(row * rows, rows), :] = refs[row][...]

    out = short(mxu(weights[...], grad_ref[...]))
    for row in range(count):
        refs[count + 1 + row][...] = out[row * rows : (row + 1) * rows]


def unproject(out_proj, grad_output, offsets, place, count):
    width, length = grad_output.shape
    rows = out_proj.shape[0] // count
    step = 256
    in_specs = [
        pl.BlockSpec((rows, width), lambda i, at, by=by: (lax.rem(at[0] + by, count), 0))
        for by in offsets
    ]
    return pl.pallas_call(
        functools.partial(unproject_kernel, len(offsets)),
        grid_spec=pltpu.PrefetchScalarGridSpec(
            num_scalar_prefetch=1,
            grid=(length // step,),
            in_specs=in_specs + [pl.BlockSpec((width, step), lambda i, at: (0, i))],
            out_specs=[pl.BlockSpec((rows, step), lambda i, at: (0, i))] * len(offsets),
            scratch_shapes=[pltpu.VMEM((len(offsets) * rows, width), jnp.bfloat16)],
        ),
        out_shape=[in_hbm((rows, length))] * len(offsets),
        compiler_params=params(),
        name="unproject",
    )(place.reshape(1), *held_in_hbm(*[out_proj] * len(offsets), grad_output))


def project_kernel(core_ref, *refs):
    *piece_refs, grad_ref, other_ref, mine_ref, rows = refs
    count, small, _ = mine_ref.shape

    @pl.when(pl.program_id(0) == 0)
    def _():
        for place, which in enumerate((1 - core_ref[0], core_ref[0])):
            first = pl.multiple_of(which * small, small)
            for slot, piece in enumerate(piece_refs):
                rows[pl.ds((place * count + slot) * small, small), :] = piece[pl.ds(first, small), :]

    out = lax.dot_general(
        rows[...], grad_ref[...], (((1,), (1,)), ((), ())), preferred_element_type=jnp.float32
    )
    out = short(out).reshape(2, count, small, -1)
    other_ref[...] = out[0]
    mine_ref[...] = out[1]


def project(pieces, grad_output, core):
    width, length = grad_output.shape
    small = pieces[0].shape[0] // 2
    step = 512
    out_block = pl.BlockSpec((len(pieces), small, step), lambda i, at: (0, 0, i))
    out = in_hbm((len(pieces), small, width))
    return pl.pallas_call(
        project_kernel,
        grid_spec=pltpu.PrefetchScalarGridSpec(
            num_scalar_prefetch=1,
            grid=(width // step,),
            in_specs=[pl.BlockSpec(pieces[0].shape, lambda i, at: (0, 0))] * len(pieces)
            + [pl.BlockSpec((step, length), lambda i, at: (i, 0))],
            out_specs=[out_block, out_block],
            scratch_shapes=[pltpu.VMEM((2 * len(pieces) * small, length), jnp.bfloat16)],
        ),
        out_shape=[out, out],
        compiler_params=params(),
        name="project",
    )(core.reshape(1), *held_in_hbm(*pieces, grad_output))


def pick_kernel(order_ref, mine_ref, got_ref, *out_refs):
    for slot, ref in enumerate(out_refs):
        at = order_ref[slot]
        ref[...] = short(wide(mine_ref[at]) + wide(got_ref[at]))


def pick(mine, got, order):
    count, small, width = mine.shape
    step = width // 2
    block = pl.BlockSpec((count, small, step), lambda i, at: (0, 0, i))
    return pl.pallas_call(
        pick_kernel,
        grid_spec=pltpu.PrefetchScalarGridSpec(
            num_scalar_prefetch=1,
            grid=(2,),
            in_specs=[block, block],
            out_specs=[pl.BlockSpec((small, step), lambda i, at: (0, i))] * count,
        ),
        out_shape=[in_hbm((small, width))] * count,
        compiler_params=params(),
        name="pick",
    )(order, *held_in_hbm(mine, got))


def swaps(count, bit):
    return [(place, place ^ bit) for place in range(count)]


def exchange(blocks):
    return lax.all_to_all(blocks, "seq", split_axis=0, concat_axis=0, tiled=True)


def tie(first, *others):
    return lax.optimization_barrier((first,) + others)[0]


def shift(block, by):
    count = lax.axis_size("chan")
    return lax.ppermute(block, "chan", [(i, (i + by) % count) for i in range(count)])


def gather_first(shard):
    count, place = lax.axis_size("chan"), lax.axis_index("chan")
    if count != 4:
        return [shard] + [shift(shard, by) for by in range(1, count)]
    low, high = shift(shard, 1), shift(shard, 3)
    return [lax.select_n(place, shard, high, low, shard), shard, low, high]


def gather_second(held):
    if lax.axis_size("chan") == 4:
        passed, shard, low, high = held
        return [shard, low, lax.ppermute(passed, "chan", [(0, 2), (3, 1), (2, 3), (1, 0)]), high]
    return held


def scatter_seq(other, mine, *before):
    count, chips = lax.axis_size("seq"), lax.axis_size("chan")
    line, chip = lax.axis_index("chan"), lax.axis_index("seq") // 2
    got = lax.ppermute(other, "seq", swaps(count, 1))
    bits = sorted(range(1, chips), key=lambda bit: (-bin(bit).count("1"), bit)) + [0]
    order = jnp.stack([lax.rem(line - (chip ^ bit) + chips, chips) for bit in bits])
    blocks = pick(tie(mine, *before), got, order.astype(jnp.int32))
    return [
        lax.ppermute(block, "seq", swaps(count, 2 * bit)) for block, bit in zip(blocks, bits[:-1])
    ] + [blocks[-1]]


def sum_of(parts):
    total = wide(parts[0])
    for part in parts[1:]:
        total = total + wide(part)
    return total


def body(outer_gate, inner_gate, signal, long_filter, grad_output, out_proj):
    seq_count, chan_count = lax.axis_size("seq"), lax.axis_size("chan")
    chan_rows, block_len = outer_gate.shape
    owned = chan_rows // seq_count
    per = block_len // LANES
    line = lax.axis_index("chan")
    core = lax.axis_index("seq") % 2
    tables = [jnp.asarray(t) for t in dft_tables(block_len * seq_count, seq_count)]

    if chan_count == 4:
        far = unproject(out_proj, grad_output, [2], line, chan_count)[0]
        pair = prepare(inner_gate, signal, tie(long_filter, far))
        pair = pair.reshape(seq_count, owned, 2 * per, LANES)
        sent = exchange(pair)
        near = unproject(tie(out_proj, pair), grad_output, [0, 1, 3], line, chan_count)
        far = lax.ppermute(far, "chan", [(2, 0), (1, 3), (3, 2), (0, 1)])
        none = jnp.zeros_like(far)
        rising = short(wide(near[1]) + wide(jnp.where(line == 1, far, none)))
        falling = short(wide(near[2]) + wide(jnp.where(line == 2, far, none)))
        sent = tie(sent, rising, falling)
        up, down = shift(rising, 1), shift(falling, 3)
        shares, flag = [near[0], up, down, far], (line == 0) | (line == 3)
    else:
        pair = prepare(inner_gate, signal, long_filter)
        pair = pair.reshape(seq_count, owned, 2 * per, LANES)
        sent = exchange(pair)
        blocks = unproject(out_proj, grad_output, list(range(chan_count)), line, chan_count)
        shares = [blocks[0]] + [shift(block, by) for by, block in enumerate(blocks) if by > 0]
        flag = line >= 0

    conv, spec_signal, spec_filter = convolve(sent, tables)
    *mixed, conv_out = mix(tie(exchange(conv), *shares), outer_gate)
    held = [gather_first(part) for part in mixed]
    grad_outer, grad_conv = regard(shares, flag, outer_gate, conv_out)
    grad_conv = grad_conv.reshape(seq_count, owned // 2, 2 * per, LANES)
    corr = correlate(exchange(grad_conv), spec_signal, spec_filter, tables)
    pieces = [gather_second(part) for part in held]
    pieces[0] = tie(pieces[0], corr)
    partials = [project(part, grad_output, core) for part in pieces]
    projs = [scatter_seq(*partials[0])]
    projs.append(scatter_seq(*partials[1], *projs[0][-1:]))

    grad_inner, grad_signal, grad_filter = finish(tie(exchange(corr), projs[1][-1]), signal, inner_gate)
    grad_proj = jnp.concatenate([sum_of(parts) for parts in projs], axis=0)
    return (grad_outer, grad_inner, grad_signal, grad_filter, grad_proj)


def solution(mesh):
    tokens = P("chan", "seq")
    in_specs = (tokens, tokens, tokens, tokens, tokens, P(None, "chan"))
    out_specs = (tokens, tokens, tokens, tokens, P("seq", "chan"))
    return jax.shard_map(body, mesh=mesh, in_specs=in_specs, out_specs=out_specs, check_vma=False)
```

```python
import functools
import math

import jax
import jax.numpy as jnp
import numpy as np
from jax import lax
from jax.experimental import pallas as pl
from jax.experimental.pallas import tpu as pltpu
from jax.sharding import PartitionSpec as P

LANES = 128
CHUNKS = 2
VMEM_BYTES = 48 * 1024 * 1024


def wide(x):
    return x.astype(jnp.float32)


def short(x):
    return x.astype(jnp.bfloat16)


def held_in_hbm(*arrays):
    return [pltpu.with_memory_space_constraint(array, pltpu.HBM) for array in arrays]


def in_hbm(shape, dtype=jnp.bfloat16):
    return pltpu.HBM(shape, dtype)


def high_low(table, axis):
    high = table.astype(jnp.bfloat16)
    low = (table - high.astype(np.float64)).astype(jnp.bfloat16)
    return np.concatenate([high, low], axis=axis)


def dft_tables(tokens, blocks):
    outer = tokens // LANES
    per = outer // blocks
    freq = np.arange(outer) + 0.25
    angle = 2.0 * math.pi / outer * np.outer(freq, np.arange(outer))
    first = np.zeros((2, 2, outer, blocks, 2, per))
    last = np.zeros((blocks, 2, per, 2, 2, outer))
    for pair in range(2):
        first[pair, 0, :, :, pair, :] = np.cos(angle).reshape(outer, blocks, per)
        first[pair, 1, :, :, pair, :] = -np.sin(angle).reshape(outer, blocks, per)
        last[:, pair, :, pair, 0, :] = np.cos(angle.T).reshape(blocks, per, outer) / tokens
        last[:, pair, :, pair, 1, :] = -np.sin(angle.T).reshape(blocks, per, outer) / tokens
    first = high_low(first.reshape(4 * outer, 2 * outer), 1)
    last = high_low(last.reshape(2 * outer, 4 * outer), 1)
    turn = 2.0 * math.pi / tokens * np.outer(freq, np.arange(LANES))
    twiddle = np.stack([np.cos(turn), np.sin(turn)]).astype(np.float32)
    lane = 2.0 * math.pi / LANES * np.outer(np.arange(LANES), np.arange(LANES))
    cos, sin = np.cos(lane), np.sin(lane)
    forward = high_low(np.block([[cos, -sin], [sin, cos]]), 0)
    inverse = high_low(np.block([[cos, sin], [-sin, cos]]), 0)
    return first, forward, inverse, last, twiddle


def mxu(left, right):
    return jnp.dot(left, right, preferred_element_type=jnp.float32)


def forward_pair(pair_block, first, twiddle):
    outer = twiddle.shape[1]
    rows = pair_block.reshape(2 * outer, LANES)
    part = mxu(first, jnp.concatenate([rows, rows], axis=0))
    cos, sin = twiddle[0], twiddle[1]
    turned = []
    for pair in range(2):
        real = part[2 * pair * outer : (2 * pair + 1) * outer]
        imag = part[(2 * pair + 1) * outer : (2 * pair + 2) * outer]
        turned.append(
            jnp.concatenate([real * cos + imag * sin, imag * cos - real * sin], axis=1).astype(
                jnp.bfloat16
            )
        )
    return turned


def inverse_pair(spread, last, twiddle):
    cos, sin = twiddle[0], twiddle[1]
    parts = []
    for item in spread:
        real, imag = item[:, :LANES], item[:, LANES:]
        parts.append((real * cos - imag * sin).astype(jnp.bfloat16))
        parts.append((real * sin + imag * cos).astype(jnp.bfloat16))
    return mxu(last, jnp.concatenate(parts + parts, axis=0))


def lanes_dft(rows, table):
    return mxu(jnp.concatenate([rows, rows], axis=1), table)


def convolve_kernel(pairs_ref, first_ref, forward_ref, inverse_ref, last_ref, twiddle_ref,
                    conv_ref, signal_ref, filter_ref, turned, spread):
    outer = twiddle_ref.shape[1]
    step = pairs_ref.shape[1]
    twiddle = twiddle_ref[...]
    for chan in range(step):
        pieces = forward_pair(pairs_ref[:, chan], first_ref[...], twiddle)
        for pair in range(2):
            turned[pl.ds((pair * step + chan) * outer, outer), :] = pieces[pair]
    half = step * outer
    signal = lanes_dft(turned[pl.ds(0, half), :], forward_ref[...])
    kernel = lanes_dft(turned[pl.ds(half, half), :], forward_ref[...])
    signal_ref[...] = signal.reshape(signal_ref.shape)
    filter_ref[...] = kernel.reshape(filter_ref.shape)
    sr, si = signal[:, :LANES], signal[:, LANES:]
    kr, ki = kernel[:, :LANES], kernel[:, LANES:]
    product = jnp.concatenate([kr * sr - ki * si, kr * si + ki * sr], axis=1).astype(jnp.bfloat16)
    spread[...] = lanes_dft(product, inverse_ref[...])
    for pair in range(step // 2):
        items = [spread[pl.ds((2 * pair + one) * outer, outer), :] for one in range(2)]
        out = inverse_pair(items, last_ref[...], twiddle)
        conv_ref[:, pair] = out.reshape(conv_ref.shape[0], -1, LANES).astype(jnp.bfloat16)


def correlate_kernel(pairs_ref, signal_ref, filter_ref, first_ref, forward_ref, inverse_ref,
                     last_ref, twiddle_ref, out_ref, turned, spread):
    outer = twiddle_ref.shape[1]
    step = signal_ref.shape[0]
    twiddle = twiddle_ref[...]
    for pair in range(step // 2):
        pieces = forward_pair(pairs_ref[:, pair], first_ref[...], twiddle)
        for one in range(2):
            turned[pl.ds((2 * pair + one) * outer, outer), :] = pieces[one]
    half = step * outer
    grad = lanes_dft(turned[...], forward_ref[...])
    gr, gi = grad[:, :LANES], grad[:, LANES:]
    for place, ref in enumerate((filter_ref, signal_ref)):
        other = ref[...].reshape(half, 2 * LANES)
        kr, ki = other[:, :LANES], other[:, LANES:]
        product = jnp.concatenate([kr * gr + ki * gi, kr * gi - ki * gr], axis=1)
        spread[place] = lanes_dft(product.astype(jnp.bfloat16), inverse_ref[...])
    for chan in range(step):
        items = [spread[place, pl.ds(chan * outer, outer), :] for place in range(2)]
        out = inverse_pair(items, last_ref[...], twiddle)
        out_ref[:, chan] = out.reshape(out_ref.shape[0], -1, LANES).astype(jnp.bfloat16)


def whole(table):
    zeros = (0,) * table.ndim
    return pl.BlockSpec(table.shape, lambda i: zeros)


def convolve(pairs, tables):
    blocks, chans, rows, _ = pairs.shape
    step = min(8, chans)
    outer = blocks * rows // 2
    spec = in_hbm((chans, outer, 2 * LANES), jnp.float32)
    spec_block = pl.BlockSpec((step, outer, 2 * LANES), lambda i: (i, 0, 0))
    return pl.pallas_call(
        convolve_kernel,
        grid=(chans // step,),
        in_specs=[pl.BlockSpec((blocks, step, rows, LANES), lambda i: (0, i, 0, 0))]
        + [whole(table) for table in tables],
        out_specs=[
            pl.BlockSpec((blocks, step // 2, rows, LANES), lambda i: (0, i, 0, 0)),
            spec_block,
            spec_block,
        ],
        out_shape=[in_hbm((blocks, chans // 2, rows, LANES)), spec, spec],
        scratch_shapes=[
            pltpu.VMEM((2 * step * outer, 2 * LANES), jnp.bfloat16),
            pltpu.VMEM((step * outer, 2 * LANES), jnp.float32),
        ],
        compiler_params=pltpu.CompilerParams(vmem_limit_bytes=VMEM_BYTES),
        name="convolve",
    )(pairs, *held_in_hbm(*tables))


def correlate(pairs, signal, kernel, tables):
    blocks, _, rows, _ = pairs.shape
    chans = signal.shape[0]
    step = min(8, chans)
    outer = blocks * rows // 2
    spec_block = pl.BlockSpec((step, outer, 2 * LANES), lambda i: (i, 0, 0))
    return pl.pallas_call(
        correlate_kernel,
        grid=(chans // step,),
        in_specs=[
            pl.BlockSpec((blocks, step // 2, rows, LANES), lambda i: (0, i, 0, 0)),
            spec_block,
            spec_block,
        ]
        + [whole(table) for table in tables],
        out_specs=pl.BlockSpec((blocks, step, rows, LANES), lambda i: (0, i, 0, 0)),
        out_shape=in_hbm((blocks, chans, rows, LANES)),
        scratch_shapes=[
            pltpu.VMEM((step * outer, 2 * LANES), jnp.bfloat16),
            pltpu.VMEM((2, step * outer, 2 * LANES), jnp.float32),
        ],
        compiler_params=pltpu.CompilerParams(vmem_limit_bytes=VMEM_BYTES),
        name="correlate",
    )(pairs, *held_in_hbm(signal, kernel, *tables))


def params():
    return pltpu.CompilerParams(vmem_limit_bytes=VMEM_BYTES)


def spread_lanes(target, rows, first, stride):
    count = rows.shape[0]
    for lane in range(rows.shape[1] // LANES):
        target[pl.ds(first + lane, count, stride=stride), :] = rows[:, lane * LANES : (lane + 1) * LANES]


def prepare_kernel(gate_ref, signal_ref, filter_ref, pair_ref, lines):
    per = gate_ref.shape[1] // LANES
    spread_lanes(lines, short(wide(gate_ref[...]) * wide(signal_ref[...])).astype(jnp.float32), 0, 2 * per)
    spread_lanes(lines, wide(filter_ref[...]), per, 2 * per)
    pair_ref[...] = short(lines[...]).reshape(pair_ref.shape)


def prepare(inner_gate, signal, long_filter):
    rows, length = signal.shape
    per = length // LANES
    step = rows // 2
    block = pl.BlockSpec((step, length), lambda i: (i, 0))
    return pl.pallas_call(
        prepare_kernel,
        grid=(2,),
        in_specs=[block] * 3,
        out_specs=pl.BlockSpec((step, 2 * per, LANES), lambda i: (i, 0, 0)),
        out_shape=in_hbm((rows, 2 * per, LANES)),
        scratch_shapes=[pltpu.VMEM((step * 2 * per, LANES), jnp.float32)],
        compiler_params=params(),
        name="prepare",
    )(*held_in_hbm(inner_gate, signal, long_filter))


def mix_kernel(conv_ref, gate_ref, *refs):
    mixed_ref, out_ref, lines = refs
    rows, length = gate_ref.shape
    per = length // LANES
    lines[...] = wide(conv_ref[...].reshape(rows * per, LANES))
    small = rows // CHUNKS
    for lane in range(per):
        cols = slice(lane * LANES, (lane + 1) * LANES)
        conv = lines[pl.ds(lane, rows, stride=per), :]
        out_ref[:, cols] = short(conv)
        mixed = short(conv * wide(gate_ref[:, cols]))
        for cut in range(CHUNKS):
            mixed_ref[cut, :, cols] = mixed[cut * small : (cut + 1) * small]


def mix(conv, outer_gate):
    rows, length = outer_gate.shape
    per = length // LANES
    conv = conv.reshape(rows * per // 16, 16, LANES)
    step = rows // 2
    token_rows = pl.BlockSpec((step, length), lambda i: (i, 0))
    cut_rows = pl.BlockSpec((CHUNKS, step // CHUNKS, length), lambda i: (0, i, 0))
    return pl.pallas_call(
        mix_kernel,
        grid=(2,),
        in_specs=[pl.BlockSpec((step * per // 16, 16, LANES), lambda i: (i, 0, 0)), token_rows],
        out_specs=[cut_rows, token_rows],
        out_shape=[in_hbm((CHUNKS, rows // CHUNKS, length)), in_hbm((rows, length))],
        scratch_shapes=[pltpu.VMEM((step * per, LANES), jnp.float32)],
        compiler_params=params(),
        name="mix",
    )(conv, outer_gate)


def regard_kernel(flag_ref, *refs):
    *share_refs, gate_ref, conv_ref, outer_ref, grad_ref, lines = refs
    per = gate_ref.shape[1] // LANES
    grad_mix = wide(share_refs[0][...])
    for ref in share_refs[1:-1]:
        grad_mix = grad_mix + wide(ref[...])
    last = wide(share_refs[-1][...])
    grad_mix = grad_mix + jnp.where(flag_ref[0] != 0, last, jnp.zeros_like(last))
    outer_ref[...] = short(grad_mix * wide(conv_ref[...]))
    spread_lanes(lines, grad_mix * wide(gate_ref[...]), 0, per)
    grad_ref[...] = short(lines[...]).reshape(grad_ref.shape)


def regard(shares, flag, outer_gate, conv_out):
    rows, length = outer_gate.shape
    per = length // LANES
    step = rows // 2
    block = pl.BlockSpec((step, length), lambda i, at: (i, 0))
    return pl.pallas_call(
        regard_kernel,
        grid_spec=pltpu.PrefetchScalarGridSpec(
            num_scalar_prefetch=1,
            grid=(2,),
            in_specs=[block] * (len(shares) + 2),
            out_specs=[block, pl.BlockSpec((step * per // 16, 16, LANES), lambda i, at: (i, 0, 0))],
            scratch_shapes=[pltpu.VMEM((step * per, LANES), jnp.float32)],
        ),
        out_shape=[in_hbm((rows, length)), in_hbm((rows * per // 16, 16, LANES))],
        compiler_params=params(),
        name="regard",
    )(flag.astype(jnp.int32).reshape(1), *shares, *held_in_hbm(outer_gate, conv_out))


def finish_kernel(corr_ref, signal_ref, gate_ref, inner_ref, signal_out_ref, filter_ref, lines):
    rows, length = signal_ref.shape
    per = length // LANES
    lines[...] = wide(corr_ref[...].reshape(rows * 2 * per, LANES))
    for lane in range(per):
        cols = slice(lane * LANES, (lane + 1) * LANES)
        grad_prod = lines[pl.ds(lane, rows, stride=2 * per), :]
        filter_ref[:, cols] = lines[pl.ds(per + lane, rows, stride=2 * per), :]
        inner_ref[:, cols] = short(grad_prod * wide(signal_ref[:, cols]))
        signal_out_ref[:, cols] = short(grad_prod * wide(gate_ref[:, cols]))


def finish(corr, signal, inner_gate):
    rows, length = signal.shape
    per = length // LANES
    step = rows // 2
    block = pl.BlockSpec((step, length), lambda i: (i, 0))
    return pl.pallas_call(
        finish_kernel,
        grid=(2,),
        in_specs=[pl.BlockSpec((step, 2 * per, LANES), lambda i: (i, 0, 0)), block, block],
        out_specs=[block] * 3,
        out_shape=[jax.ShapeDtypeStruct((rows, length), jnp.bfloat16)] * 2
        + [jax.ShapeDtypeStruct((rows, length), jnp.float32)],
        scratch_shapes=[pltpu.VMEM((step * 2 * per, LANES), jnp.float32)],
        compiler_params=params(),
        name="finish",
    )(corr.reshape(rows, 2 * per, LANES), *held_in_hbm(signal, inner_gate))


def unproject_kernel(count, place_ref, *refs):
    rows, width = refs[0].shape
    grad_ref, weights = refs[count], refs[-1]

    @pl.when(pl.program_id(0) == 0)
    def _():
        for row in range(count):
            weights[pl.ds(row * rows, rows), :] = refs[row][...]

    out = short(mxu(weights[...], grad_ref[...]))
    for row in range(count):
        refs[count + 1 + row][...] = out[row * rows : (row + 1) * rows]


def unproject(out_proj, grad_output, offsets, place, count):
    width, length = grad_output.shape
    rows = out_proj.shape[0] // count
    step = 512
    in_specs = [
        pl.BlockSpec((rows, width), lambda i, at, by=by: (lax.rem(at[0] + by, count), 0))
        for by in offsets
    ]
    return pl.pallas_call(
        functools.partial(unproject_kernel, len(offsets)),
        grid_spec=pltpu.PrefetchScalarGridSpec(
            num_scalar_prefetch=1,
            grid=(length // step,),
            in_specs=in_specs + [pl.BlockSpec((width, step), lambda i, at: (0, i))],
            out_specs=[pl.BlockSpec((rows, step), lambda i, at: (0, i))] * len(offsets),
            scratch_shapes=[pltpu.VMEM((len(offsets) * rows, width), jnp.bfloat16)],
        ),
        out_shape=[in_hbm((rows, length))] * len(offsets),
        compiler_params=params(),
        name="unproject",
    )(place.reshape(1), *held_in_hbm(*[out_proj] * len(offsets), grad_output))


def swaps(count, bit):
    return [(place, place ^ bit) for place in range(count)]


def exchange(blocks):
    return lax.all_to_all(blocks, "seq", split_axis=0, concat_axis=0, tiled=True)


def tie(first, *others):
    return lax.optimization_barrier((first,) + others)[0]


def shift(block, by):
    count = lax.axis_size("chan")
    return lax.ppermute(block, "chan", [(i, (i + by) % count) for i in range(count)])


def gather_first(shard):
    count, place = lax.axis_size("chan"), lax.axis_index("chan")
    if count != 4:
        return [shard] + [shift(shard, by) for by in range(1, count)]
    return [shard, shift(shard, 1), shift(shard, 3)]


def gather_between(held):
    shard, low, high = held
    return [
        lax.select_n(lax.axis_index("chan"), shard[cut], high[cut], low[cut], shard[cut])
        for cut in range(CHUNKS)
    ]


def gather_second(held, passed, cut):
    if lax.axis_size("chan") != 4:
        return held
    shard, low, high = held
    passed = lax.ppermute(passed[cut], "chan", [(0, 2), (3, 1), (2, 3), (1, 0)])
    return [shard, low, passed[None], high]


def project(pieces, cut, grad_output):
    count, chips = lax.axis_size("seq"), lax.axis_size("chan")
    line, place = lax.axis_index("chan"), lax.axis_index("seq")
    core, chip = place % 2, place // 2
    rows = jnp.stack([piece[min(cut, len(piece) - 1)] for piece in pieces])
    rows = rows.reshape(chips, 2, -1, rows.shape[-1])

    def rows_of(which):
        chosen = lax.dynamic_index_in_dim(rows, which, 1, False)
        return jnp.einsum("zct,dt->zcd", chosen, grad_output, preferred_element_type=jnp.float32)

    got = lax.ppermute(short(rows_of(1 - core)), "seq", swaps(count, 1))
    total = short(rows_of(core) + wide(got))

    def block(bit):
        return lax.dynamic_index_in_dim(total, (line - (chip ^ bit)) % chips, 0, False)

    bits = sorted(range(1, chips), key=lambda bit: (-bin(bit).count("1"), bit))
    return [lax.ppermute(block(bit), "seq", swaps(count, 2 * bit)) for bit in bits] + [block(0)]


def sum_of(parts):
    total = wide(parts[0])
    for part in parts[1:]:
        total = total + wide(part)
    return total


def body(outer_gate, inner_gate, signal, long_filter, grad_output, out_proj):
    seq_count, chan_count = lax.axis_size("seq"), lax.axis_size("chan")
    chan_rows, block_len = outer_gate.shape
    owned = chan_rows // seq_count
    per = block_len // LANES
    line = lax.axis_index("chan")
    tables = [jnp.asarray(t) for t in dft_tables(block_len * seq_count, seq_count)]

    pair = prepare(inner_gate, signal, long_filter).reshape(seq_count, owned, 2 * per, LANES)
    sent = exchange(pair)
    weights = tie(out_proj, pair)
    if chan_count == 4:
        far = unproject(weights, grad_output, [2], line, chan_count)[0]
        near = unproject(tie(weights, far), grad_output, [0, 1, 3], line, chan_count)
        far = lax.ppermute(far, "chan", [(2, 0), (1, 3), (3, 2), (0, 1)])
        none = jnp.zeros_like(far)
        rising = short(wide(near[1]) + wide(jnp.where(line == 1, far, none)))
        falling = short(wide(near[2]) + wide(jnp.where(line == 2, far, none)))
        sent = tie(sent, rising, falling)
        up, down = shift(rising, 1), shift(falling, 3)
        shares, flag = [near[0], up, down, far], (line == 0) | (line == 3)
    else:
        blocks = unproject(weights, grad_output, list(range(chan_count)), line, chan_count)
        shares = [blocks[0]] + [shift(block, by) for by, block in enumerate(blocks) if by > 0]
        flag = line >= 0

    conv, spec_signal, spec_filter = convolve(sent, tables)
    mixed, conv_out = mix(tie(exchange(conv), *shares), outer_gate)
    held = gather_first(mixed)
    grad_outer, grad_conv = regard(shares, flag, outer_gate, conv_out)
    grad_conv = grad_conv.reshape(seq_count, owned // 2, 2 * per, LANES)
    corr = correlate(exchange(grad_conv), spec_signal, spec_filter, tables)
    held = tie(held, corr)
    passed = gather_between(held) if chan_count == 4 else held
    pieces = [gather_second(held, passed, cut) for cut in range(CHUNKS)]
    corr = exchange(tie(corr, passed))
    pieces = tie(pieces, corr)
    first = project(pieces[0], 0, grad_output)
    second = project(pieces[1], 1, grad_output)
    grads = finish(tie(corr, first[-1]), signal, inner_gate)
    grad_proj = jnp.concatenate([sum_of(first), sum_of(second)], axis=0)
    return (grad_outer, *grads, grad_proj)


def solution(mesh):
    tokens = P("chan", "seq")
    in_specs = (tokens, tokens, tokens, tokens, tokens, P(None, "chan"))
    out_specs = (tokens, tokens, tokens, tokens, P("seq", "chan"))
    return jax.shard_map(body, mesh=mesh, in_specs=in_specs, out_specs=out_specs, check_vma=False)
```

```python
import functools
import math

import jax
import jax.numpy as jnp
import numpy as np
from jax import lax
from jax.experimental import pallas as pl
from jax.experimental.pallas import tpu as pltpu
from jax.sharding import PartitionSpec as P

LANES = 128
CHUNKS = 1
VMEM_BYTES = 48 * 1024 * 1024


def wide(x):
    return x.astype(jnp.float32)


def short(x):
    return x.astype(jnp.bfloat16)


def held_in_hbm(*arrays):
    return [pltpu.with_memory_space_constraint(array, pltpu.HBM) for array in arrays]


def in_hbm(shape, dtype=jnp.bfloat16):
    return pltpu.HBM(shape, dtype)


def high_low(table, axis):
    high = table.astype(jnp.bfloat16)
    low = (table - high.astype(np.float64)).astype(jnp.bfloat16)
    return np.concatenate([high, low], axis=axis)


def dft_tables(tokens, blocks):
    outer = tokens // LANES
    per = outer // blocks
    freq = np.arange(outer) + 0.25
    angle = 2.0 * math.pi / outer * np.outer(freq, np.arange(outer))
    first = np.zeros((2, 2, outer, blocks, 2, per))
    last = np.zeros((blocks, 2, per, 2, 2, outer))
    for pair in range(2):
        first[pair, 0, :, :, pair, :] = np.cos(angle).reshape(outer, blocks, per)
        first[pair, 1, :, :, pair, :] = -np.sin(angle).reshape(outer, blocks, per)
        last[:, pair, :, pair, 0, :] = np.cos(angle.T).reshape(blocks, per, outer) / tokens
        last[:, pair, :, pair, 1, :] = -np.sin(angle.T).reshape(blocks, per, outer) / tokens
    first = high_low(first.reshape(4 * outer, 2 * outer), 1)
    last = high_low(last.reshape(2 * outer, 4 * outer), 1)
    turn = 2.0 * math.pi / tokens * np.outer(freq, np.arange(LANES))
    twiddle = np.stack([np.cos(turn), np.sin(turn)]).astype(np.float32)
    lane = 2.0 * math.pi / LANES * np.outer(np.arange(LANES), np.arange(LANES))
    cos, sin = np.cos(lane), np.sin(lane)
    forward = high_low(np.block([[cos, -sin], [sin, cos]]), 0)
    inverse = high_low(np.block([[cos, sin], [-sin, cos]]), 0)
    return first, forward, inverse, last, twiddle


def mxu(left, right):
    return jnp.dot(left, right, preferred_element_type=jnp.float32)


def forward_pair(pair_block, first, twiddle):
    outer = twiddle.shape[1]
    rows = pair_block.reshape(2 * outer, LANES)
    part = mxu(first, jnp.concatenate([rows, rows], axis=0))
    cos, sin = twiddle[0], twiddle[1]
    turned = []
    for pair in range(2):
        real = part[2 * pair * outer : (2 * pair + 1) * outer]
        imag = part[(2 * pair + 1) * outer : (2 * pair + 2) * outer]
        turned.append(
            jnp.concatenate([real * cos + imag * sin, imag * cos - real * sin], axis=1).astype(
                jnp.bfloat16
            )
        )
    return turned


def inverse_pair(spread, last, twiddle):
    cos, sin = twiddle[0], twiddle[1]
    parts = []
    for item in spread:
        real, imag = item[:, :LANES], item[:, LANES:]
        parts.append((real * cos - imag * sin).astype(jnp.bfloat16))
        parts.append((real * sin + imag * cos).astype(jnp.bfloat16))
    return mxu(last, jnp.concatenate(parts + parts, axis=0))


def lanes_dft(rows, table):
    return mxu(jnp.concatenate([rows, rows], axis=1), table)


def convolve_kernel(pairs_ref, first_ref, forward_ref, inverse_ref, last_ref, twiddle_ref,
                    conv_ref, signal_ref, filter_ref, turned, spread):
    outer = twiddle_ref.shape[1]
    step = pairs_ref.shape[1]
    twiddle = twiddle_ref[...]
    for chan in range(step):
        pieces = forward_pair(pairs_ref[:, chan], first_ref[...], twiddle)
        for pair in range(2):
            turned[pl.ds((pair * step + chan) * outer, outer), :] = pieces[pair]
    half = step * outer
    signal = lanes_dft(turned[pl.ds(0, half), :], forward_ref[...])
    kernel = lanes_dft(turned[pl.ds(half, half), :], forward_ref[...])
    signal_ref[...] = signal.reshape(signal_ref.shape)
    filter_ref[...] = kernel.reshape(filter_ref.shape)
    sr, si = signal[:, :LANES], signal[:, LANES:]
    kr, ki = kernel[:, :LANES], kernel[:, LANES:]
    product = jnp.concatenate([kr * sr - ki * si, kr * si + ki * sr], axis=1).astype(jnp.bfloat16)
    spread[...] = lanes_dft(product, inverse_ref[...])
    for pair in range(step // 2):
        items = [spread[pl.ds((2 * pair + one) * outer, outer), :] for one in range(2)]
        out = inverse_pair(items, last_ref[...], twiddle)
        conv_ref[:, pair] = out.reshape(conv_ref.shape[0], -1, LANES).astype(jnp.bfloat16)


def correlate_kernel(pairs_ref, signal_ref, filter_ref, first_ref, forward_ref, inverse_ref,
                     last_ref, twiddle_ref, out_ref, turned, spread):
    outer = twiddle_ref.shape[1]
    step = signal_ref.shape[0]
    twiddle = twiddle_ref[...]
    for pair in range(step // 2):
        pieces = forward_pair(pairs_ref[:, pair], first_ref[...], twiddle)
        for one in range(2):
            turned[pl.ds((2 * pair + one) * outer, outer), :] = pieces[one]
    half = step * outer
    grad = lanes_dft(turned[...], forward_ref[...])
    gr, gi = grad[:, :LANES], grad[:, LANES:]
    for place, ref in enumerate((filter_ref, signal_ref)):
        other = ref[...].reshape(half, 2 * LANES)
        kr, ki = other[:, :LANES], other[:, LANES:]
        product = jnp.concatenate([kr * gr + ki * gi, kr * gi - ki * gr], axis=1)
        spread[place] = lanes_dft(product.astype(jnp.bfloat16), inverse_ref[...])
    for chan in range(step):
        items = [spread[place, pl.ds(chan * outer, outer), :] for place in range(2)]
        out = inverse_pair(items, last_ref[...], twiddle)
        out_ref[:, chan] = out.reshape(out_ref.shape[0], -1, LANES).astype(jnp.bfloat16)


def whole(table):
    zeros = (0,) * table.ndim
    return pl.BlockSpec(table.shape, lambda i: zeros)


def convolve(pairs, tables):
    blocks, chans, rows, _ = pairs.shape
    step = min(32, chans)
    outer = blocks * rows // 2
    spec = in_hbm((chans, outer, 2 * LANES), jnp.float32)
    spec_block = pl.BlockSpec((step, outer, 2 * LANES), lambda i: (i, 0, 0))
    return pl.pallas_call(
        convolve_kernel,
        grid=(chans // step,),
        in_specs=[pl.BlockSpec((blocks, step, rows, LANES), lambda i: (0, i, 0, 0))]
        + [whole(table) for table in tables],
        out_specs=[
            pl.BlockSpec((blocks, step // 2, rows, LANES), lambda i: (0, i, 0, 0)),
            spec_block,
            spec_block,
        ],
        out_shape=[in_hbm((blocks, chans // 2, rows, LANES)), spec, spec],
        scratch_shapes=[
            pltpu.VMEM((2 * step * outer, 2 * LANES), jnp.bfloat16),
            pltpu.VMEM((step * outer, 2 * LANES), jnp.float32),
        ],
        compiler_params=pltpu.CompilerParams(vmem_limit_bytes=VMEM_BYTES),
        name="convolve",
    )(pairs, *held_in_hbm(*tables))


def correlate(pairs, signal, kernel, tables):
    blocks, _, rows, _ = pairs.shape
    chans = signal.shape[0]
    step = min(16, chans)
    outer = blocks * rows // 2
    spec_block = pl.BlockSpec((step, outer, 2 * LANES), lambda i: (i, 0, 0))
    return pl.pallas_call(
        correlate_kernel,
        grid=(chans // step,),
        in_specs=[
            pl.BlockSpec((blocks, step // 2, rows, LANES), lambda i: (0, i, 0, 0)),
            spec_block,
            spec_block,
        ]
        + [whole(table) for table in tables],
        out_specs=pl.BlockSpec((blocks, step, rows, LANES), lambda i: (0, i, 0, 0)),
        out_shape=in_hbm((blocks, chans, rows, LANES)),
        scratch_shapes=[
            pltpu.VMEM((step * outer, 2 * LANES), jnp.bfloat16),
            pltpu.VMEM((2, step * outer, 2 * LANES), jnp.float32),
        ],
        compiler_params=pltpu.CompilerParams(vmem_limit_bytes=VMEM_BYTES),
        name="correlate",
    )(pairs, *held_in_hbm(signal, kernel, *tables))


def params():
    return pltpu.CompilerParams(vmem_limit_bytes=VMEM_BYTES)


def spread_lanes(target, rows, first, stride):
    count = rows.shape[0]
    for lane in range(rows.shape[1] // LANES):
        target[pl.ds(first + lane, count, stride=stride), :] = rows[:, lane * LANES : (lane + 1) * LANES]


def prepare_kernel(gate_ref, signal_ref, filter_ref, pair_ref, lines):
    per = gate_ref.shape[1] // LANES
    spread_lanes(lines, short(wide(gate_ref[...]) * wide(signal_ref[...])).astype(jnp.float32), 0, 2 * per)
    spread_lanes(lines, wide(filter_ref[...]), per, 2 * per)
    pair_ref[...] = short(lines[...]).reshape(pair_ref.shape)


def prepare(inner_gate, signal, long_filter):
    rows, length = signal.shape
    per = length // LANES
    step = rows // 2
    block = pl.BlockSpec((step, length), lambda i: (i, 0))
    return pl.pallas_call(
        prepare_kernel,
        grid=(2,),
        in_specs=[block] * 3,
        out_specs=pl.BlockSpec((step, 2 * per, LANES), lambda i: (i, 0, 0)),
        out_shape=in_hbm((rows, 2 * per, LANES)),
        scratch_shapes=[pltpu.VMEM((step * 2 * per, LANES), jnp.float32)],
        compiler_params=params(),
        name="prepare",
    )(*held_in_hbm(inner_gate, signal, long_filter))


def mix_kernel(conv_ref, gate_ref, *refs):
    mixed_ref, out_ref, lines = refs
    rows, length = gate_ref.shape
    per = length // LANES
    lines[...] = wide(conv_ref[...].reshape(rows * per, LANES))
    small = rows // CHUNKS
    for lane in range(per):
        cols = slice(lane * LANES, (lane + 1) * LANES)
        conv = lines[pl.ds(lane, rows, stride=per), :]
        out_ref[:, cols] = short(conv)
        mixed = short(conv * wide(gate_ref[:, cols]))
        for cut in range(CHUNKS):
            mixed_ref[cut, :, cols] = mixed[cut * small : (cut + 1) * small]


def mix(conv, outer_gate):
    rows, length = outer_gate.shape
    per = length // LANES
    conv = conv.reshape(rows * per // 16, 16, LANES)
    step = rows // 2
    token_rows = pl.BlockSpec((step, length), lambda i: (i, 0))
    cut_rows = pl.BlockSpec((CHUNKS, step // CHUNKS, length), lambda i: (0, i, 0))
    return pl.pallas_call(
        mix_kernel,
        grid=(2,),
        in_specs=[pl.BlockSpec((step * per // 16, 16, LANES), lambda i: (i, 0, 0)), token_rows],
        out_specs=[cut_rows, token_rows],
        out_shape=[in_hbm((CHUNKS, rows // CHUNKS, length)), in_hbm((rows, length))],
        scratch_shapes=[pltpu.VMEM((step * per, LANES), jnp.float32)],
        compiler_params=params(),
        name="mix",
    )(conv, outer_gate)


def regard_kernel(flag_ref, *refs):
    *share_refs, gate_ref, conv_ref, outer_ref, grad_ref, lines = refs
    per = gate_ref.shape[1] // LANES
    grad_mix = wide(share_refs[0][...])
    for ref in share_refs[1:-1]:
        grad_mix = grad_mix + wide(ref[...])
    last = wide(share_refs[-1][...])
    grad_mix = grad_mix + jnp.where(flag_ref[0] != 0, last, jnp.zeros_like(last))
    outer_ref[...] = short(grad_mix * wide(conv_ref[...]))
    spread_lanes(lines, grad_mix * wide(gate_ref[...]), 0, per)
    grad_ref[...] = short(lines[...]).reshape(grad_ref.shape)


def regard(shares, flag, outer_gate, conv_out):
    rows, length = outer_gate.shape
    per = length // LANES
    step = rows // 2
    block = pl.BlockSpec((step, length), lambda i, at: (i, 0))
    return pl.pallas_call(
        regard_kernel,
        grid_spec=pltpu.PrefetchScalarGridSpec(
            num_scalar_prefetch=1,
            grid=(2,),
            in_specs=[block] * (len(shares) + 2),
            out_specs=[block, pl.BlockSpec((step * per // 16, 16, LANES), lambda i, at: (i, 0, 0))],
            scratch_shapes=[pltpu.VMEM((step * per, LANES), jnp.float32)],
        ),
        out_shape=[in_hbm((rows, length)), in_hbm((rows * per // 16, 16, LANES))],
        compiler_params=params(),
        name="regard",
    )(flag.astype(jnp.int32).reshape(1), *shares, *held_in_hbm(outer_gate, conv_out))


def finish_kernel(corr_ref, signal_ref, gate_ref, inner_ref, signal_out_ref, filter_ref, lines):
    rows, length = signal_ref.shape
    per = length // LANES
    lines[...] = wide(corr_ref[...].reshape(rows * 2 * per, LANES))
    for lane in range(per):
        cols = slice(lane * LANES, (lane + 1) * LANES)
        grad_prod = lines[pl.ds(lane, rows, stride=2 * per), :]
        filter_ref[:, cols] = lines[pl.ds(per + lane, rows, stride=2 * per), :]
        inner_ref[:, cols] = short(grad_prod * wide(signal_ref[:, cols]))
        signal_out_ref[:, cols] = short(grad_prod * wide(gate_ref[:, cols]))


def finish(corr, signal, inner_gate):
    rows, length = signal.shape
    per = length // LANES
    step = rows // 2
    block = pl.BlockSpec((step, length), lambda i: (i, 0))
    return pl.pallas_call(
        finish_kernel,
        grid=(2,),
        in_specs=[pl.BlockSpec((step, 2 * per, LANES), lambda i: (i, 0, 0)), block, block],
        out_specs=[block] * 3,
        out_shape=[jax.ShapeDtypeStruct((rows, length), jnp.bfloat16)] * 2
        + [jax.ShapeDtypeStruct((rows, length), jnp.float32)],
        scratch_shapes=[pltpu.VMEM((step * 2 * per, LANES), jnp.float32)],
        compiler_params=params(),
        name="finish",
    )(corr.reshape(rows, 2 * per, LANES), *held_in_hbm(signal, inner_gate))


def unproject_kernel(count, place_ref, *refs):
    rows, width = refs[0].shape
    grad_ref, weights = refs[count], refs[-1]

    @pl.when(pl.program_id(0) == 0)
    def _():
        for row in range(count):
            weights[pl.ds(row * rows, rows), :] = refs[row][...]

    out = short(mxu(weights[...], grad_ref[...]))
    for row in range(count):
        refs[count + 1 + row][...] = out[row * rows : (row + 1) * rows]


def unproject(out_proj, grad_output, offsets, place, count):
    width, length = grad_output.shape
    rows = out_proj.shape[0] // count
    step = 512
    in_specs = [
        pl.BlockSpec((rows, width), lambda i, at, by=by: (lax.rem(at[0] + by, count), 0))
        for by in offsets
    ]
    return pl.pallas_call(
        functools.partial(unproject_kernel, len(offsets)),
        grid_spec=pltpu.PrefetchScalarGridSpec(
            num_scalar_prefetch=1,
            grid=(length // step,),
            in_specs=in_specs + [pl.BlockSpec((width, step), lambda i, at: (0, i))],
            out_specs=[pl.BlockSpec((rows, step), lambda i, at: (0, i))] * len(offsets),
            scratch_shapes=[pltpu.VMEM((len(offsets) * rows, width), jnp.bfloat16)],
        ),
        out_shape=[in_hbm((rows, length))] * len(offsets),
        compiler_params=params(),
        name="unproject",
    )(place.reshape(1), *held_in_hbm(*[out_proj] * len(offsets), grad_output))


def project_kernel(core_ref, *refs):
    *piece_refs, grad_ref, other_ref, mine_ref, rows = refs
    count, small, _ = mine_ref.shape

    @pl.when(pl.program_id(0) == 0)
    def _():
        for place, which in enumerate((1 - core_ref[0], core_ref[0])):
            first = pl.multiple_of(which * small, small)
            for slot, piece in enumerate(piece_refs):
                rows[pl.ds((place * count + slot) * small, small), :] = piece[pl.ds(first, small), :]

    out = lax.dot_general(
        rows[...], grad_ref[...], (((1,), (1,)), ((), ())), preferred_element_type=jnp.float32
    )
    out = short(out).reshape(2, count, small, -1)
    other_ref[...] = out[0]
    mine_ref[...] = out[1]


def project(pieces, grad_output, core):
    width, length = grad_output.shape
    small = pieces[0].shape[0] // 2
    step = min(1024, width)
    out_block = pl.BlockSpec((len(pieces), small, step), lambda i, at: (0, 0, i))
    out = in_hbm((len(pieces), small, width))
    return pl.pallas_call(
        project_kernel,
        grid_spec=pltpu.PrefetchScalarGridSpec(
            num_scalar_prefetch=1,
            grid=(width // step,),
            in_specs=[pl.BlockSpec(pieces[0].shape, lambda i, at: (0, 0))] * len(pieces)
            + [pl.BlockSpec((step, length), lambda i, at: (i, 0))],
            out_specs=[out_block, out_block],
            scratch_shapes=[pltpu.VMEM((2 * len(pieces) * small, length), jnp.bfloat16)],
        ),
        out_shape=[out, out],
        compiler_params=params(),
        name="project",
    )(core.reshape(1), *held_in_hbm(*pieces, grad_output))


def swaps(count, bit):
    return [(place, place ^ bit) for place in range(count)]


def exchange(blocks):
    return lax.all_to_all(blocks, "seq", split_axis=0, concat_axis=0, tiled=True)


def tie(first, *others):
    return lax.optimization_barrier((first,) + others)[0]


def shift(block, by):
    count = lax.axis_size("chan")
    return lax.ppermute(block, "chan", [(i, (i + by) % count) for i in range(count)])


def gather_first(shard):
    count, place = lax.axis_size("chan"), lax.axis_index("chan")
    if count != 4:
        return [shard] + [shift(shard, by) for by in range(1, count)]
    return [shard, shift(shard, 1), shift(shard, 3)]


def both_cores(pieces, grad_output):
    count, core = lax.axis_size("seq"), lax.axis_index("seq") % 2
    rows = jnp.stack(pieces)
    sums = short(
        jnp.einsum("zct,dt->zcd", rows, grad_output, preferred_element_type=jnp.float32)
    ).reshape(len(pieces), 2, -1, grad_output.shape[0])
    got = lax.ppermute(lax.dynamic_index_in_dim(sums, 1 - core, 1, False), "seq", swaps(count, 1))
    return short(wide(lax.dynamic_index_in_dim(sums, core, 1, False)) + wide(got))


def scatter_chips(total):
    count, chips = lax.axis_size("seq"), lax.axis_size("chan")
    line, chip = lax.axis_index("chan"), lax.axis_index("seq") // 2

    def block(bit):
        return lax.dynamic_index_in_dim(total, (line - (chip ^ bit)) % chips, 0, False)

    bits = sorted(range(1, chips), key=lambda bit: (-bin(bit).count("1"), bit))
    return [lax.ppermute(block(bit), "seq", swaps(count, 2 * bit)) for bit in bits] + [block(0)]


def sum_of(parts):
    total = wide(parts[0])
    for part in parts[1:]:
        total = total + wide(part)
    return total


def body(outer_gate, inner_gate, signal, long_filter, grad_output, out_proj):
    seq_count, chan_count = lax.axis_size("seq"), lax.axis_size("chan")
    chan_rows, block_len = outer_gate.shape
    owned = chan_rows // seq_count
    per = block_len // LANES
    line = lax.axis_index("chan")
    tables = [jnp.asarray(t) for t in dft_tables(block_len * seq_count, seq_count)]

    pair = prepare(inner_gate, signal, long_filter).reshape(seq_count, owned, 2 * per, LANES)
    sent = exchange(pair)
    weights = tie(out_proj, pair)
    if chan_count == 4:
        far = unproject(weights, grad_output, [2], line, chan_count)[0]
        near = unproject(tie(weights, far), grad_output, [0, 1, 3], line, chan_count)
        far = lax.ppermute(far, "chan", [(2, 0), (1, 3), (3, 2), (0, 1)])
        none = jnp.zeros_like(far)
        rising = short(wide(near[1]) + wide(jnp.where(line == 1, far, none)))
        falling = short(wide(near[2]) + wide(jnp.where(line == 2, far, none)))
        sent = tie(sent, rising, falling)
        up, down = shift(rising, 1), shift(falling, 3)
        shares, flag = [near[0], up, down, far], (line == 0) | (line == 3)
    else:
        blocks = unproject(weights, grad_output, list(range(chan_count)), line, chan_count)
        shares = [blocks[0]] + [shift(block, by) for by, block in enumerate(blocks) if by > 0]
        flag = line >= 0

    conv, spec_signal, spec_filter = convolve(sent, tables)
    mixed, conv_out = mix(tie(exchange(conv), *shares), outer_gate)
    held = gather_first(mixed)
    grad_outer, grad_conv = regard(shares, flag, outer_gate, conv_out)
    grad_conv = grad_conv.reshape(seq_count, owned // 2, 2 * per, LANES)
    corr = correlate(exchange(grad_conv), spec_signal, spec_filter, tables)
    held = [part[0] for part in tie(held, corr)]
    if chan_count == 4:
        passed = lax.select_n(line, held[0], held[2], held[1], held[0])
        middle = lax.ppermute(passed, "chan", [(0, 2), (3, 1), (2, 3), (1, 0)])
        corr = exchange(tie(corr, passed))
        held = tie(held, passed)
        core = lax.axis_index("seq") % 2
        other, mine = project([held[0], held[1], held[0], held[2]], grad_output, core)
        middle, other = lax.optimization_barrier((middle, other, corr))[:2]
        got = lax.ppermute(other, "seq", swaps(seq_count, 1))
        middle = both_cores([middle], grad_output)
        total = short(wide(mine) + wide(got))
        total = lax.dynamic_update_slice(total, middle, (2, 0, 0))
    else:
        corr = exchange(corr)
        total = both_cores(held, grad_output)
    parts = scatter_chips(total)
    grads = finish(tie(corr, parts[-1]), signal, inner_gate)
    return (grad_outer, *grads, sum_of(tie(parts, grads)))


def solution(mesh):
    tokens = P("chan", "seq")
    in_specs = (tokens, tokens, tokens, tokens, tokens, P(None, "chan"))
    out_specs = (tokens, tokens, tokens, tokens, P("seq", "chan"))
    return jax.shard_map(body, mesh=mesh, in_specs=in_specs, out_specs=out_specs, check_vma=False)
```

```python
import functools
import math

import jax
import jax.numpy as jnp
import numpy as np
from jax import lax
from jax.experimental import pallas as pl
from jax.experimental.pallas import tpu as pltpu
from jax.sharding import PartitionSpec as P

LANES = 128
VMEM_BYTES = 48 * 1024 * 1024


def wide(x):
    return x.astype(jnp.float32)


def short(x):
    return x.astype(jnp.bfloat16)


def held_in_hbm(*arrays):
    return [pltpu.with_memory_space_constraint(array, pltpu.HBM) for array in arrays]


def in_hbm(shape, dtype=jnp.bfloat16):
    return pltpu.HBM(shape, dtype)


def high_low(table, axis):
    high = table.astype(jnp.bfloat16)
    low = (table - high.astype(np.float64)).astype(jnp.bfloat16)
    return np.concatenate([high, low], axis=axis)


def dft_tables(tokens, blocks):
    outer = tokens // LANES
    per = outer // blocks
    freq = np.arange(outer) + 0.25
    angle = 2.0 * math.pi / outer * np.outer(freq, np.arange(outer))
    first = np.zeros((2, 2, outer, blocks, 2, per))
    last = np.zeros((blocks, 2, per, 2, 2, outer))
    for pair in range(2):
        first[pair, 0, :, :, pair, :] = np.cos(angle).reshape(outer, blocks, per)
        first[pair, 1, :, :, pair, :] = -np.sin(angle).reshape(outer, blocks, per)
        last[:, pair, :, pair, 0, :] = np.cos(angle.T).reshape(blocks, per, outer) / tokens
        last[:, pair, :, pair, 1, :] = -np.sin(angle.T).reshape(blocks, per, outer) / tokens
    first = high_low(first.reshape(4 * outer, 2 * outer), 1)
    last = high_low(last.reshape(2 * outer, 4 * outer), 1)
    turn = 2.0 * math.pi / tokens * np.outer(freq, np.arange(LANES))
    twiddle = np.stack([np.cos(turn), np.sin(turn)]).astype(np.float32)
    lane = 2.0 * math.pi / LANES * np.outer(np.arange(LANES), np.arange(LANES))
    cos, sin = np.cos(lane), np.sin(lane)
    forward = high_low(np.block([[cos, -sin], [sin, cos]]), 0)
    inverse = high_low(np.block([[cos, sin], [-sin, cos]]), 0)
    return first, forward, inverse, last, twiddle


def mxu(left, right):
    return jnp.dot(left, right, preferred_element_type=jnp.float32)


def forward_pair(pair_block, first, twiddle):
    outer = twiddle.shape[1]
    rows = pair_block.reshape(2 * outer, LANES)
    part = mxu(first, jnp.concatenate([rows, rows], axis=0))
    cos, sin = twiddle[0], twiddle[1]
    turned = []
    for pair in range(2):
        real = part[2 * pair * outer : (2 * pair + 1) * outer]
        imag = part[(2 * pair + 1) * outer : (2 * pair + 2) * outer]
        turned.append(
            jnp.concatenate([real * cos + imag * sin, imag * cos - real * sin], axis=1).astype(
                jnp.bfloat16
            )
        )
    return turned


def inverse_pair(spread, last, twiddle):
    cos, sin = twiddle[0], twiddle[1]
    parts = []
    for item in spread:
        real, imag = item[:, :LANES], item[:, LANES:]
        parts.append((real * cos - imag * sin).astype(jnp.bfloat16))
        parts.append((real * sin + imag * cos).astype(jnp.bfloat16))
    return mxu(last, jnp.concatenate(parts + parts, axis=0))


def lanes_dft(rows, table):
    return mxu(jnp.concatenate([rows, rows], axis=1), table)


def convolve_kernel(pairs_ref, first_ref, forward_ref, inverse_ref, last_ref, twiddle_ref,
                    conv_ref, signal_ref, filter_ref, turned, spread):
    outer = twiddle_ref.shape[1]
    step = pairs_ref.shape[1]
    twiddle = twiddle_ref[...]
    for chan in range(step):
        pieces = forward_pair(pairs_ref[:, chan], first_ref[...], twiddle)
        for pair in range(2):
            turned[pl.ds((pair * step + chan) * outer, outer), :] = pieces[pair]
    half = step * outer
    signal = lanes_dft(turned[pl.ds(0, half), :], forward_ref[...])
    kernel = lanes_dft(turned[pl.ds(half, half), :], forward_ref[...])
    signal_ref[...] = signal.reshape(signal_ref.shape)
    filter_ref[...] = kernel.reshape(filter_ref.shape)
    sr, si = signal[:, :LANES], signal[:, LANES:]
    kr, ki = kernel[:, :LANES], kernel[:, LANES:]
    product = jnp.concatenate([kr * sr - ki * si, kr * si + ki * sr], axis=1).astype(jnp.bfloat16)
    spread[...] = lanes_dft(product, inverse_ref[...])
    for pair in range(step // 2):
        items = [spread[pl.ds((2 * pair + one) * outer, outer), :] for one in range(2)]
        out = inverse_pair(items, last_ref[...], twiddle)
        conv_ref[:, pair] = out.reshape(conv_ref.shape[0], -1, LANES).astype(jnp.bfloat16)


def correlate_kernel(pairs_ref, signal_ref, filter_ref, first_ref, forward_ref, inverse_ref,
                     last_ref, twiddle_ref, out_ref, turned, spread):
    outer = twiddle_ref.shape[1]
    step = signal_ref.shape[0]
    twiddle = twiddle_ref[...]
    for pair in range(step // 2):
        pieces = forward_pair(pairs_ref[:, pair], first_ref[...], twiddle)
        for one in range(2):
            turned[pl.ds((2 * pair + one) * outer, outer), :] = pieces[one]
    half = step * outer
    grad = lanes_dft(turned[...], forward_ref[...])
    gr, gi = grad[:, :LANES], grad[:, LANES:]
    for place, ref in enumerate((filter_ref, signal_ref)):
        other = ref[...].reshape(half, 2 * LANES)
        kr, ki = other[:, :LANES], other[:, LANES:]
        product = jnp.concatenate([kr * gr + ki * gi, kr * gi - ki * gr], axis=1)
        spread[place] = lanes_dft(product.astype(jnp.bfloat16), inverse_ref[...])
    for chan in range(step):
        items = [spread[place, pl.ds(chan * outer, outer), :] for place in range(2)]
        out = inverse_pair(items, last_ref[...], twiddle)
        out_ref[:, chan] = out.reshape(out_ref.shape[0], -1, LANES).astype(jnp.bfloat16)


def whole(table):
    zeros = (0,) * table.ndim
    return pl.BlockSpec(table.shape, lambda i: zeros)


def convolve(pairs, tables):
    blocks, chans, rows, _ = pairs.shape
    step = min(32, chans)
    outer = blocks * rows // 2
    spec = in_hbm((chans, outer, 2 * LANES), jnp.float32)
    spec_block = pl.BlockSpec((step, outer, 2 * LANES), lambda i: (i, 0, 0))
    return pl.pallas_call(
        convolve_kernel,
        grid=(chans // step,),
        in_specs=[pl.BlockSpec((blocks, step, rows, LANES), lambda i: (0, i, 0, 0))]
        + [whole(table) for table in tables],
        out_specs=[
            pl.BlockSpec((blocks, step // 2, rows, LANES), lambda i: (0, i, 0, 0)),
            spec_block,
            spec_block,
        ],
        out_shape=[in_hbm((blocks, chans // 2, rows, LANES)), spec, spec],
        scratch_shapes=[
            pltpu.VMEM((2 * step * outer, 2 * LANES), jnp.bfloat16),
            pltpu.VMEM((step * outer, 2 * LANES), jnp.float32),
        ],
        compiler_params=pltpu.CompilerParams(vmem_limit_bytes=VMEM_BYTES),
        name="convolve",
    )(pairs, *held_in_hbm(*tables))


def correlate(pairs, signal, kernel, tables):
    blocks, _, rows, _ = pairs.shape
    chans = signal.shape[0]
    step = min(16, chans)
    outer = blocks * rows // 2
    spec_block = pl.BlockSpec((step, outer, 2 * LANES), lambda i: (i, 0, 0))
    return pl.pallas_call(
        correlate_kernel,
        grid=(chans // step,),
        in_specs=[
            pl.BlockSpec((blocks, step // 2, rows, LANES), lambda i: (0, i, 0, 0)),
            spec_block,
            spec_block,
        ]
        + [whole(table) for table in tables],
        out_specs=pl.BlockSpec((blocks, step, rows, LANES), lambda i: (0, i, 0, 0)),
        out_shape=in_hbm((blocks, chans, rows, LANES)),
        scratch_shapes=[
            pltpu.VMEM((step * outer, 2 * LANES), jnp.bfloat16),
            pltpu.VMEM((2, step * outer, 2 * LANES), jnp.float32),
        ],
        compiler_params=pltpu.CompilerParams(vmem_limit_bytes=VMEM_BYTES),
        name="correlate",
    )(pairs, *held_in_hbm(signal, kernel, *tables))


def params():
    return pltpu.CompilerParams(vmem_limit_bytes=VMEM_BYTES)


def spread_lanes(target, rows, first, stride):
    count = rows.shape[0]
    for lane in range(rows.shape[1] // LANES):
        target[pl.ds(first + lane, count, stride=stride), :] = rows[:, lane * LANES : (lane + 1) * LANES]


def prepare_kernel(gate_ref, signal_ref, filter_ref, pair_ref, lines):
    per = gate_ref.shape[1] // LANES
    spread_lanes(lines, short(wide(gate_ref[...]) * wide(signal_ref[...])).astype(jnp.float32), 0, 2 * per)
    spread_lanes(lines, wide(filter_ref[...]), per, 2 * per)
    pair_ref[...] = short(lines[...]).reshape(pair_ref.shape)


def prepare(inner_gate, signal, long_filter):
    rows, length = signal.shape
    per = length // LANES
    step = rows // 2
    block = pl.BlockSpec((step, length), lambda i: (i, 0))
    return pl.pallas_call(
        prepare_kernel,
        grid=(2,),
        in_specs=[block] * 3,
        out_specs=pl.BlockSpec((step, 2 * per, LANES), lambda i: (i, 0, 0)),
        out_shape=in_hbm((rows, 2 * per, LANES)),
        scratch_shapes=[pltpu.VMEM((step * 2 * per, LANES), jnp.float32)],
        compiler_params=params(),
        name="prepare",
    )(*held_in_hbm(inner_gate, signal, long_filter))


def mix_kernel(flag_ref, conv_ref, gate_ref, *refs):
    *share_refs, mixed_ref, outer_ref, grad_ref, lines, grads = refs
    rows, length = gate_ref.shape
    per = length // LANES
    lines[...] = wide(conv_ref[...].reshape(rows * per, LANES))
    for lane in range(per):
        cols = slice(lane * LANES, (lane + 1) * LANES)
        conv = lines[pl.ds(lane, rows, stride=per), :]
        gate = wide(gate_ref[:, cols])
        mixed_ref[:, cols] = short(conv * gate)
        grad_mix = wide(share_refs[0][:, cols])
        for ref in share_refs[1:-1]:
            grad_mix = grad_mix + wide(ref[:, cols])
        last = wide(share_refs[-1][:, cols])
        grad_mix = grad_mix + jnp.where(flag_ref[0] != 0, last, jnp.zeros_like(last))
        outer_ref[:, cols] = short(grad_mix * conv)
        grads[pl.ds(lane, rows, stride=per), :] = grad_mix * gate
    grad_ref[...] = short(grads[...]).reshape(grad_ref.shape)


def mix(conv, outer_gate, shares, flag):
    rows, length = outer_gate.shape
    per = length // LANES
    conv = conv.reshape(rows * per // 16, 16, LANES)
    step = rows // 2
    token_rows = pl.BlockSpec((step, length), lambda i, at: (i, 0))
    lane_rows = pl.BlockSpec((step * per // 16, 16, LANES), lambda i, at: (i, 0, 0))
    return pl.pallas_call(
        mix_kernel,
        grid_spec=pltpu.PrefetchScalarGridSpec(
            num_scalar_prefetch=1,
            grid=(2,),
            in_specs=[lane_rows, token_rows] + [token_rows] * len(shares),
            out_specs=[token_rows, token_rows, lane_rows],
            scratch_shapes=[pltpu.VMEM((step * per, LANES), jnp.float32)] * 2,
        ),
        out_shape=[in_hbm((rows, length))] * 2 + [in_hbm((rows * per // 16, 16, LANES))],
        compiler_params=params(),
        name="mix",
    )(flag.astype(jnp.int32).reshape(1), conv, outer_gate, *shares)


def finish_kernel(corr_ref, signal_ref, gate_ref, inner_ref, signal_out_ref, filter_ref, lines):
    rows, length = signal_ref.shape
    per = length // LANES
    lines[...] = wide(corr_ref[...].reshape(rows * 2 * per, LANES))
    for lane in range(per):
        cols = slice(lane * LANES, (lane + 1) * LANES)
        grad_prod = lines[pl.ds(lane, rows, stride=2 * per), :]
        filter_ref[:, cols] = lines[pl.ds(per + lane, rows, stride=2 * per), :]
        inner_ref[:, cols] = short(grad_prod * wide(signal_ref[:, cols]))
        signal_out_ref[:, cols] = short(grad_prod * wide(gate_ref[:, cols]))


def finish(corr, signal, inner_gate):
    rows, length = signal.shape
    per = length // LANES
    step = rows // 2
    block = pl.BlockSpec((step, length), lambda i: (i, 0))
    return pl.pallas_call(
        finish_kernel,
        grid=(2,),
        in_specs=[pl.BlockSpec((step, 2 * per, LANES), lambda i: (i, 0, 0)), block, block],
        out_specs=[block] * 3,
        out_shape=[jax.ShapeDtypeStruct((rows, length), jnp.bfloat16)] * 2
        + [jax.ShapeDtypeStruct((rows, length), jnp.float32)],
        scratch_shapes=[pltpu.VMEM((step * 2 * per, LANES), jnp.float32)],
        compiler_params=params(),
        name="finish",
    )(corr.reshape(rows, 2 * per, LANES), *held_in_hbm(signal, inner_gate))


def unproject_kernel(count, add_from, place_ref, *refs):
    rows, width = refs[0].shape
    grad_ref, weights = refs[count], refs[-1]
    out_refs = refs[-1 - count : -1]

    @pl.when(pl.program_id(0) == 0)
    def _():
        for row in range(count):
            weights[pl.ds(row * rows, rows), :] = refs[row][...]

    out = short(mxu(weights[...], grad_ref[...]))
    for row in range(count):
        part = out[row * rows : (row + 1) * rows]
        if add_from is not None:
            more = wide(refs[count + 1][...])
            part = short(wide(part) + jnp.where(place_ref[0] == add_from[row], more, jnp.zeros_like(more)))
        out_refs[row][...] = part


def unproject(out_proj, grad_output, offsets, place, count, more=None, add_from=None):
    width, length = grad_output.shape
    rows = out_proj.shape[0] // count
    step = 512
    in_specs = [
        pl.BlockSpec((rows, width), lambda i, at, by=by: (lax.rem(at[0] + by, count), 0))
        for by in offsets
    ]
    out_block = pl.BlockSpec((rows, step), lambda i, at: (0, i))
    extra = [] if more is None else [more]
    return pl.pallas_call(
        functools.partial(unproject_kernel, len(offsets), add_from),
        grid_spec=pltpu.PrefetchScalarGridSpec(
            num_scalar_prefetch=1,
            grid=(length // step,),
            in_specs=in_specs
            + [pl.BlockSpec((width, step), lambda i, at: (0, i))]
            + [out_block] * len(extra),
            out_specs=[out_block] * len(offsets),
            scratch_shapes=[pltpu.VMEM((len(offsets) * rows, width), jnp.bfloat16)],
        ),
        out_shape=[in_hbm((rows, length))] * len(offsets),
        compiler_params=params(),
        cost_estimate=pl.CostEstimate(flops=40 * 10**9, bytes_accessed=10**8, transcendentals=0),
        name="unproject",
    )(place.reshape(1), *held_in_hbm(*[out_proj] * len(offsets), grad_output), *extra)


def project_kernel(core_ref, *refs):
    *piece_refs, grad_ref, other_ref, mine_ref, rows = refs
    count, small, _ = mine_ref.shape

    @pl.when(pl.program_id(0) == 0)
    def _():
        for place, which in enumerate((1 - core_ref[0], core_ref[0])):
            first = pl.multiple_of(which * small, small)
            for slot, piece in enumerate(piece_refs):
                rows[pl.ds((place * count + slot) * small, small), :] = piece[pl.ds(first, small), :]

    out = lax.dot_general(
        rows[...], grad_ref[...], (((1,), (1,)), ((), ())), preferred_element_type=jnp.float32
    )
    out = short(out).reshape(2, count, small, -1)
    other_ref[...] = out[0]
    mine_ref[...] = out[1]


def project(pieces, grad_output, core):
    width, length = grad_output.shape
    small = pieces[0].shape[0] // 2
    step = min(1024, width)
    out_block = pl.BlockSpec((len(pieces), small, step), lambda i, at: (0, 0, i))
    out = in_hbm((len(pieces), small, width))
    return pl.pallas_call(
        project_kernel,
        grid_spec=pltpu.PrefetchScalarGridSpec(
            num_scalar_prefetch=1,
            grid=(width // step,),
            in_specs=[pl.BlockSpec(pieces[0].shape, lambda i, at: (0, 0))] * len(pieces)
            + [pl.BlockSpec((step, length), lambda i, at: (i, 0))],
            out_specs=[out_block, out_block],
            scratch_shapes=[pltpu.VMEM((2 * len(pieces) * small, length), jnp.bfloat16)],
        ),
        out_shape=[out, out],
        compiler_params=params(),
        name="project",
    )(core.reshape(1), *pieces, *held_in_hbm(grad_output))


def swaps(count, bit):
    return [(place, place ^ bit) for place in range(count)]


def exchange(blocks):
    return lax.all_to_all(blocks, "seq", split_axis=0, concat_axis=0, tiled=True)


def tie(first, *others):
    return lax.optimization_barrier((first,) + others)[0]


def shift(block, by):
    count = lax.axis_size("chan")
    return lax.ppermute(block, "chan", [(i, (i + by) % count) for i in range(count)])


def gather_first(shard):
    count, place = lax.axis_size("chan"), lax.axis_index("chan")
    if count != 4:
        return [shard] + [shift(shard, by) for by in range(1, count)]
    return [shard, shift(shard, 1), shift(shard, 3)]


def both_cores(pieces, grad_output):
    count, core = lax.axis_size("seq"), lax.axis_index("seq") % 2
    rows = jnp.stack(pieces)
    sums = short(
        jnp.einsum("zct,dt->zcd", rows, grad_output, preferred_element_type=jnp.float32)
    ).reshape(len(pieces), 2, -1, grad_output.shape[0])
    got = lax.ppermute(lax.dynamic_index_in_dim(sums, 1 - core, 1, False), "seq", swaps(count, 1))
    return short(wide(lax.dynamic_index_in_dim(sums, core, 1, False)) + wide(got))


def scatter_chips(total):
    count, chips = lax.axis_size("seq"), lax.axis_size("chan")
    line, chip = lax.axis_index("chan"), lax.axis_index("seq") // 2

    def block(bit):
        return lax.dynamic_index_in_dim(total, (line - (chip ^ bit)) % chips, 0, False)

    bits = sorted(range(1, chips), key=lambda bit: (-bin(bit).count("1"), bit))
    return [lax.ppermute(block(bit), "seq", swaps(count, 2 * bit)) for bit in bits] + [block(0)]


def sum_of(parts):
    total = wide(parts[0])
    for part in parts[1:]:
        total = total + wide(part)
    return total


def body(outer_gate, inner_gate, signal, long_filter, grad_output, out_proj):
    seq_count, chan_count = lax.axis_size("seq"), lax.axis_size("chan")
    chan_rows, block_len = outer_gate.shape
    owned = chan_rows // seq_count
    per = block_len // LANES
    line = lax.axis_index("chan")
    tables = [jnp.asarray(t) for t in dft_tables(block_len * seq_count, seq_count)]

    if chan_count == 4:
        far = unproject(out_proj, grad_output, [2], line, chan_count)[0]
        pair = prepare(inner_gate, signal, tie(long_filter, far))
        pair = pair.reshape(seq_count, owned, 2 * per, LANES)
        far = lax.ppermute(far, "chan", [(2, 0), (1, 3), (3, 2), (0, 1)])
        sent = exchange(pair)
        near = unproject(tie(out_proj, pair), grad_output, [1, 3], line, chan_count, far, [1, 2])
        sent = tie(sent, *near)
        shares = [shift(near[0], 1), shift(near[1], 3), far]
        flag = (line == 0) | (line == 3)
    else:
        pair = prepare(inner_gate, signal, long_filter)
        pair = pair.reshape(seq_count, owned, 2 * per, LANES)
        sent = exchange(pair)
        offsets = list(range(1, chan_count))
        blocks = unproject(out_proj, grad_output, offsets, line, chan_count)
        shares = [shift(block, by) for by, block in zip(offsets, blocks)]
        flag = line >= 0

    conv, spec_signal, spec_filter = convolve(sent, tables)
    own = unproject(tie(out_proj, conv), grad_output, [0], line, chan_count)
    shares = [*held_in_hbm(*own), *shares]
    mixed, grad_outer, grad_conv = mix(exchange(conv), outer_gate, shares, flag)
    held = gather_first(mixed)
    grad_conv = grad_conv.reshape(seq_count, owned // 2, 2 * per, LANES)
    corr = correlate(exchange(grad_conv), spec_signal, spec_filter, tables)
    held = tie(held, corr)
    if chan_count == 4:
        passed = lax.select_n(line, held[0], held[2], held[1], held[0])
        middle = lax.ppermute(passed, "chan", [(0, 2), (3, 1), (2, 3), (1, 0)])
        corr = exchange(tie(corr, passed))
        held = tie(held, passed)
        core = lax.axis_index("seq") % 2
        other, mine = project([held[0], held[1], held[0], held[2]], grad_output, core)
        middle, other = lax.optimization_barrier((middle, other, corr))[:2]
        got = lax.ppermute(other, "seq", swaps(seq_count, 1))
        middle = both_cores([middle], grad_output)
        total = short(wide(mine) + wide(got))
        total = lax.dynamic_update_slice(total, middle, (2, 0, 0))
    else:
        corr = exchange(corr)
        total = both_cores(held, grad_output)
    parts = scatter_chips(total)
    grads = finish(tie(corr, parts[-1]), signal, inner_gate)
    return (grad_outer, *grads, sum_of(tie(parts, grads)))


def solution(mesh):
    tokens = P("chan", "seq")
    in_specs = (tokens, tokens, tokens, tokens, tokens, P(None, "chan"))
    out_specs = (tokens, tokens, tokens, tokens, P("seq", "chan"))
    return jax.shard_map(body, mesh=mesh, in_specs=in_specs, out_specs=out_specs, check_vma=False)
```

```python
import functools
import math

import jax
import jax.numpy as jnp
import numpy as np
from jax import lax
from jax.experimental import pallas as pl
from jax.experimental.pallas import tpu as pltpu
from jax.sharding import PartitionSpec as P

LANES = 128
VMEM_BYTES = 48 * 1024 * 1024


def wide(x):
    return x.astype(jnp.float32)


def short(x):
    return x.astype(jnp.bfloat16)


def held_in_hbm(*arrays):
    return [pltpu.with_memory_space_constraint(array, pltpu.HBM) for array in arrays]


def in_hbm(shape, dtype=jnp.bfloat16):
    return pltpu.HBM(shape, dtype)


def high_low(table, axis):
    high = table.astype(jnp.bfloat16)
    low = (table - high.astype(np.float64)).astype(jnp.bfloat16)
    return np.concatenate([high, low], axis=axis)


def dft_tables(tokens, blocks):
    outer = tokens // LANES
    per = outer // blocks
    freq = np.arange(outer) + 0.25
    angle = 2.0 * math.pi / outer * np.outer(freq, np.arange(outer))
    first = np.zeros((2, 2, outer, blocks, 2, per))
    last = np.zeros((blocks, 2, per, 2, 2, outer))
    for pair in range(2):
        first[pair, 0, :, :, pair, :] = np.cos(angle).reshape(outer, blocks, per)
        first[pair, 1, :, :, pair, :] = -np.sin(angle).reshape(outer, blocks, per)
        last[:, pair, :, pair, 0, :] = np.cos(angle.T).reshape(blocks, per, outer) / tokens
        last[:, pair, :, pair, 1, :] = -np.sin(angle.T).reshape(blocks, per, outer) / tokens
    first = high_low(first.reshape(4 * outer, 2 * outer), 1)
    last = high_low(last.reshape(2 * outer, 4 * outer), 1)
    turn = 2.0 * math.pi / tokens * np.outer(freq, np.arange(LANES))
    twiddle = np.stack([np.cos(turn), np.sin(turn)]).astype(np.float32)
    lane = 2.0 * math.pi / LANES * np.outer(np.arange(LANES), np.arange(LANES))
    cos, sin = np.cos(lane), np.sin(lane)
    forward = np.block([[cos, -sin], [sin, cos]]).astype(jnp.bfloat16)
    inverse = np.block([[cos, sin], [-sin, cos]]).astype(jnp.bfloat16)
    return first, forward, inverse, last, twiddle


def mxu(left, right):
    return jnp.dot(left, right, preferred_element_type=jnp.float32)


def forward_pair(pair_block, first, twiddle):
    outer = twiddle.shape[1]
    rows = pair_block.reshape(2 * outer, LANES)
    part = mxu(first, jnp.concatenate([rows, rows], axis=0))
    cos, sin = twiddle[0], twiddle[1]
    turned = []
    for pair in range(2):
        real = part[2 * pair * outer : (2 * pair + 1) * outer]
        imag = part[(2 * pair + 1) * outer : (2 * pair + 2) * outer]
        turned.append(
            jnp.concatenate([real * cos + imag * sin, imag * cos - real * sin], axis=1).astype(
                jnp.bfloat16
            )
        )
    return turned


def inverse_pair(spread, last, twiddle):
    cos, sin = twiddle[0], twiddle[1]
    parts = []
    for item in spread:
        real, imag = item[:, :LANES], item[:, LANES:]
        parts.append((real * cos - imag * sin).astype(jnp.bfloat16))
        parts.append((real * sin + imag * cos).astype(jnp.bfloat16))
    return mxu(last, jnp.concatenate(parts + parts, axis=0))


def lanes_dft(rows, table):
    return mxu(rows, table)


def convolve_kernel(pairs_ref, first_ref, forward_ref, inverse_ref, last_ref, twiddle_ref,
                    conv_ref, signal_ref, filter_ref, turned, spread):
    outer = twiddle_ref.shape[1]
    step = pairs_ref.shape[1]
    twiddle = twiddle_ref[...]
    for chan in range(step):
        pieces = forward_pair(pairs_ref[:, chan], first_ref[...], twiddle)
        for pair in range(2):
            turned[pl.ds((pair * step + chan) * outer, outer), :] = pieces[pair]
    half = step * outer
    signal = lanes_dft(turned[pl.ds(0, half), :], forward_ref[...])
    kernel = lanes_dft(turned[pl.ds(half, half), :], forward_ref[...])
    signal_ref[...] = signal.reshape(signal_ref.shape)
    filter_ref[...] = kernel.reshape(filter_ref.shape)
    sr, si = signal[:, :LANES], signal[:, LANES:]
    kr, ki = kernel[:, :LANES], kernel[:, LANES:]
    product = jnp.concatenate([kr * sr - ki * si, kr * si + ki * sr], axis=1).astype(jnp.bfloat16)
    spread[...] = lanes_dft(product, inverse_ref[...])
    for pair in range(step // 2):
        items = [spread[pl.ds((2 * pair + one) * outer, outer), :] for one in range(2)]
        out = inverse_pair(items, last_ref[...], twiddle)
        conv_ref[:, pair] = out.reshape(conv_ref.shape[0], -1, LANES).astype(jnp.bfloat16)


def correlate_kernel(pairs_ref, signal_ref, filter_ref, first_ref, forward_ref, inverse_ref,
                     last_ref, twiddle_ref, out_ref, turned, spread):
    outer = twiddle_ref.shape[1]
    step = signal_ref.shape[0]
    twiddle = twiddle_ref[...]
    for pair in range(step // 2):
        pieces = forward_pair(pairs_ref[:, pair], first_ref[...], twiddle)
        for one in range(2):
            turned[pl.ds((2 * pair + one) * outer, outer), :] = pieces[one]
    half = step * outer
    grad = lanes_dft(turned[...], forward_ref[...])
    gr, gi = grad[:, :LANES], grad[:, LANES:]
    for place, ref in enumerate((filter_ref, signal_ref)):
        other = ref[...].reshape(half, 2 * LANES)
        kr, ki = other[:, :LANES], other[:, LANES:]
        product = jnp.concatenate([kr * gr + ki * gi, kr * gi - ki * gr], axis=1)
        spread[place] = lanes_dft(product.astype(jnp.bfloat16), inverse_ref[...])
    for chan in range(step):
        items = [spread[place, pl.ds(chan * outer, outer), :] for place in range(2)]
        out = inverse_pair(items, last_ref[...], twiddle)
        out_ref[:, chan] = out.reshape(out_ref.shape[0], -1, LANES).astype(jnp.bfloat16)


def whole(table):
    zeros = (0,) * table.ndim
    return pl.BlockSpec(table.shape, lambda i: zeros)


def convolve(pairs, tables):
    blocks, chans, rows, _ = pairs.shape
    step = min(32, chans)
    outer = blocks * rows // 2
    spec = in_hbm((chans, outer, 2 * LANES), jnp.float32)
    spec_block = pl.BlockSpec((step, outer, 2 * LANES), lambda i: (i, 0, 0))
    return pl.pallas_call(
        convolve_kernel,
        grid=(chans // step,),
        in_specs=[pl.BlockSpec((blocks, step, rows, LANES), lambda i: (0, i, 0, 0))]
        + [whole(table) for table in tables],
        out_specs=[
            pl.BlockSpec((blocks, step // 2, rows, LANES), lambda i: (0, i, 0, 0)),
            spec_block,
            spec_block,
        ],
        out_shape=[in_hbm((blocks, chans // 2, rows, LANES)), spec, spec],
        scratch_shapes=[
            pltpu.VMEM((2 * step * outer, 2 * LANES), jnp.bfloat16),
            pltpu.VMEM((step * outer, 2 * LANES), jnp.float32),
        ],
        compiler_params=pltpu.CompilerParams(vmem_limit_bytes=VMEM_BYTES),
        name="convolve",
    )(pairs, *held_in_hbm(*tables))


def correlate(pairs, signal, kernel, tables):
    blocks, _, rows, _ = pairs.shape
    chans = signal.shape[0]
    step = min(16, chans)
    outer = blocks * rows // 2
    spec_block = pl.BlockSpec((step, outer, 2 * LANES), lambda i: (i, 0, 0))
    return pl.pallas_call(
        correlate_kernel,
        grid=(chans // step,),
        in_specs=[
            pl.BlockSpec((blocks, step // 2, rows, LANES), lambda i: (0, i, 0, 0)),
            spec_block,
            spec_block,
        ]
        + [whole(table) for table in tables],
        out_specs=pl.BlockSpec((blocks, step, rows, LANES), lambda i: (0, i, 0, 0)),
        out_shape=in_hbm((blocks, chans, rows, LANES)),
        scratch_shapes=[
            pltpu.VMEM((step * outer, 2 * LANES), jnp.bfloat16),
            pltpu.VMEM((2, step * outer, 2 * LANES), jnp.float32),
        ],
        compiler_params=pltpu.CompilerParams(vmem_limit_bytes=VMEM_BYTES),
        name="correlate",
    )(pairs, *held_in_hbm(signal, kernel, *tables))


def params():
    return pltpu.CompilerParams(vmem_limit_bytes=VMEM_BYTES)


def spread_lanes(target, rows, first, stride):
    count = rows.shape[0]
    for lane in range(rows.shape[1] // LANES):
        target[pl.ds(first + lane, count, stride=stride), :] = rows[:, lane * LANES : (lane + 1) * LANES]


def prepare_kernel(gate_ref, signal_ref, filter_ref, pair_ref, lines):
    per = gate_ref.shape[1] // LANES
    spread_lanes(lines, short(wide(gate_ref[...]) * wide(signal_ref[...])).astype(jnp.float32), 0, 2 * per)
    spread_lanes(lines, wide(filter_ref[...]), per, 2 * per)
    pair_ref[...] = short(lines[...]).reshape(pair_ref.shape)


def prepare(inner_gate, signal, long_filter):
    rows, length = signal.shape
    per = length // LANES
    step = rows // 2
    block = pl.BlockSpec((step, length), lambda i: (i, 0))
    return pl.pallas_call(
        prepare_kernel,
        grid=(2,),
        in_specs=[block] * 3,
        out_specs=pl.BlockSpec((step, 2 * per, LANES), lambda i: (i, 0, 0)),
        out_shape=in_hbm((rows, 2 * per, LANES)),
        scratch_shapes=[pltpu.VMEM((step * 2 * per, LANES), jnp.float32)],
        compiler_params=params(),
        name="prepare",
    )(*held_in_hbm(inner_gate, signal, long_filter))


def mix_kernel(parts, flag_ref, conv_ref, gate_ref, *refs):
    *share_refs, mixed_ref, outer_ref, grad_ref, lines, grads = refs
    rows, length = gate_ref.shape
    per = length // LANES
    lines[...] = wide(conv_ref[...].reshape(rows * per, LANES))
    groups = []
    for count in parts:
        groups.append(share_refs[:count])
        share_refs = share_refs[count:]
    for lane in range(per):
        cols = slice(lane * LANES, (lane + 1) * LANES)
        shares = []
        for group in groups:
            held = group[lane * len(group) // per]
            at = lane % (per // len(group)) * LANES
            shares.append(wide(held[:, at : at + LANES]))
        conv = lines[pl.ds(lane, rows, stride=per), :]
        gate = wide(gate_ref[:, cols])
        mixed_ref[:, cols] = short(conv * gate)
        grad_mix = shares[0]
        for share in shares[1:-1]:
            grad_mix = grad_mix + share
        grad_mix = grad_mix + jnp.where(flag_ref[0] != 0, shares[-1], jnp.zeros_like(shares[-1]))
        outer_ref[:, cols] = short(grad_mix * conv)
        grads[pl.ds(lane, rows, stride=per), :] = grad_mix * gate
    grad_ref[...] = short(grads[...]).reshape(grad_ref.shape)


def mix(conv, outer_gate, shares, flag):
    rows, length = outer_gate.shape
    parts = [len(share) for share in shares]
    cuts = [cut for share in shares for cut in share]
    per = length // LANES
    conv = conv.reshape(rows * per // 16, 16, LANES)
    step = rows // 2
    token_rows = pl.BlockSpec((step, length), lambda i, at: (i, 0))
    lane_rows = pl.BlockSpec((step * per // 16, 16, LANES), lambda i, at: (i, 0, 0))
    return pl.pallas_call(
        functools.partial(mix_kernel, parts),
        grid_spec=pltpu.PrefetchScalarGridSpec(
            num_scalar_prefetch=1,
            grid=(2,),
            in_specs=[lane_rows, token_rows]
            + [pl.BlockSpec((step, cut.shape[1]), lambda i, at: (i, 0)) for cut in cuts],
            out_specs=[token_rows, token_rows, lane_rows],
            scratch_shapes=[pltpu.VMEM((step * per, LANES), jnp.float32)] * 2,
        ),
        out_shape=[in_hbm((rows, length))] * 2 + [in_hbm((rows * per // 16, 16, LANES))],
        compiler_params=params(),
        name="mix",
    )(flag.astype(jnp.int32).reshape(1), conv, outer_gate, *cuts)


def finish_kernel(corr_ref, signal_ref, gate_ref, inner_ref, signal_out_ref, filter_ref, lines):
    rows, length = signal_ref.shape
    per = length // LANES
    lines[...] = wide(corr_ref[...].reshape(rows * 2 * per, LANES))
    for lane in range(per):
        cols = slice(lane * LANES, (lane + 1) * LANES)
        grad_prod = lines[pl.ds(lane, rows, stride=2 * per), :]
        filter_ref[:, cols] = lines[pl.ds(per + lane, rows, stride=2 * per), :]
        inner_ref[:, cols] = short(grad_prod * wide(signal_ref[:, cols]))
        signal_out_ref[:, cols] = short(grad_prod * wide(gate_ref[:, cols]))


def finish(corr, signal, inner_gate):
    rows, length = signal.shape
    per = length // LANES
    step = rows // 2
    block = pl.BlockSpec((step, length), lambda i: (i, 0))
    return pl.pallas_call(
        finish_kernel,
        grid=(2,),
        in_specs=[pl.BlockSpec((step, 2 * per, LANES), lambda i: (i, 0, 0)), block, block],
        out_specs=[block] * 3,
        out_shape=[jax.ShapeDtypeStruct((rows, length), jnp.bfloat16)] * 2
        + [jax.ShapeDtypeStruct((rows, length), jnp.float32)],
        scratch_shapes=[pltpu.VMEM((step * 2 * per, LANES), jnp.float32)],
        compiler_params=params(),
        name="finish",
    )(corr.reshape(rows, 2 * per, LANES), *held_in_hbm(signal, inner_gate))


def unproject_kernel(count, splits, add_from, place_ref, *refs):
    rows, width = refs[0].shape
    grad_ref, weights = refs[count], refs[-1]
    out_refs = refs[-1 - count * splits : -1]

    @pl.when(pl.program_id(0) == 0)
    def _():
        for row in range(count):
            weights[pl.ds(row * rows, rows), :] = refs[row][...]

    out = short(mxu(weights[...], grad_ref[...]))
    for row in range(count):
        part = out[row * rows : (row + 1) * rows]
        if add_from is not None:
            more = wide(refs[count + 1][...])
            part = short(wide(part) + jnp.where(place_ref[0] == add_from[row], more, jnp.zeros_like(more)))
        for split in range(splits):

            @pl.when(pl.program_id(0) * splits // pl.num_programs(0) == split)
            def _(part=part, ref=out_refs[row * splits + split]):
                ref[...] = part


def unproject(out_proj, grad_output, offsets, place, count, more=None, add_from=None, half=None, splits=1):
    width, length = grad_output.shape
    rows = out_proj.shape[0] // count
    step = 512 if half is None else 256
    length = length if half is None else length // 2
    first = 0 if half is None else half * (length // step)
    in_specs = [
        pl.BlockSpec((rows, width), lambda i, at, by=by: (lax.rem(at[0] + by, count), 0))
        for by in offsets
    ]
    out_block = pl.BlockSpec((rows, step), lambda i, at: (0, i if splits == 1 else 0))
    extra = [] if more is None else [more]
    return pl.pallas_call(
        functools.partial(unproject_kernel, len(offsets), splits, add_from),
        grid_spec=pltpu.PrefetchScalarGridSpec(
            num_scalar_prefetch=1,
            grid=(length // step,),
            in_specs=in_specs
            + [pl.BlockSpec((width, step), lambda i, at: (0, first + i))]
            + [out_block] * len(extra),
            out_specs=[out_block] * (len(offsets) * splits),
            scratch_shapes=[pltpu.VMEM((len(offsets) * rows, width), jnp.bfloat16)],
        ),
        out_shape=[in_hbm((rows, length // splits))] * (len(offsets) * splits),
        compiler_params=params(),
        cost_estimate=pl.CostEstimate(flops=40 * 10**9, bytes_accessed=10**8, transcendentals=0),
        name="unproject",
    )(place.reshape(1), *held_in_hbm(*[out_proj] * len(offsets), grad_output), *extra)


def project_kernel(core_ref, *refs):
    *piece_refs, grad_ref, other_ref, mine_ref, rows = refs
    count, small, _ = mine_ref.shape

    @pl.when(pl.program_id(0) == 0)
    def _():
        for place, which in enumerate((1 - core_ref[0], core_ref[0])):
            first = pl.multiple_of(which * small, small)
            for slot, piece in enumerate(piece_refs):
                rows[pl.ds((place * count + slot) * small, small), :] = piece[pl.ds(first, small), :]

    out = lax.dot_general(
        rows[...], grad_ref[...], (((1,), (1,)), ((), ())), preferred_element_type=jnp.float32
    )
    out = short(out).reshape(2, count, small, -1)
    other_ref[...] = out[0]
    mine_ref[...] = out[1]


def project(pieces, grad_output, core):
    width, length = grad_output.shape
    small = pieces[0].shape[0] // 2
    step = min(1024, width)
    out_block = pl.BlockSpec((len(pieces), small, step), lambda i, at: (0, 0, i))
    out = in_hbm((len(pieces), small, width))
    return pl.pallas_call(
        project_kernel,
        grid_spec=pltpu.PrefetchScalarGridSpec(
            num_scalar_prefetch=1,
            grid=(width // step,),
            in_specs=[pl.BlockSpec(pieces[0].shape, lambda i, at: (0, 0))] * len(pieces)
            + [pl.BlockSpec((step, length), lambda i, at: (i, 0))],
            out_specs=[out_block, out_block],
            scratch_shapes=[pltpu.VMEM((2 * len(pieces) * small, length), jnp.bfloat16)],
        ),
        out_shape=[out, out],
        compiler_params=params(),
        name="project",
    )(core.reshape(1), *pieces, *held_in_hbm(grad_output))


def swaps(count, bit):
    return [(place, place ^ bit) for place in range(count)]


def exchange(blocks):
    return lax.all_to_all(blocks, "seq", split_axis=0, concat_axis=0, tiled=True)


def tie(first, *others):
    return lax.optimization_barrier((first,) + others)[0]


def shift(block, by):
    count = lax.axis_size("chan")
    return lax.ppermute(block, "chan", [(i, (i + by) % count) for i in range(count)])


def gather_first(shard):
    count, place = lax.axis_size("chan"), lax.axis_index("chan")
    if count != 4:
        return [shard] + [shift(shard, by) for by in range(1, count)]
    return [shard, shift(shard, 1), shift(shard, 3)]


def both_cores(pieces, grad_output):
    count, core = lax.axis_size("seq"), lax.axis_index("seq") % 2
    rows = jnp.stack(pieces)
    sums = short(
        jnp.einsum("zct,dt->zcd", rows, grad_output, preferred_element_type=jnp.float32)
    ).reshape(len(pieces), 2, -1, grad_output.shape[0])
    got = lax.ppermute(lax.dynamic_index_in_dim(sums, 1 - core, 1, False), "seq", swaps(count, 1))
    return short(wide(lax.dynamic_index_in_dim(sums, core, 1, False)) + wide(got))


def scatter_chips(total):
    count, chips = lax.axis_size("seq"), lax.axis_size("chan")
    line, chip = lax.axis_index("chan"), lax.axis_index("seq") // 2

    def block(bit):
        return lax.dynamic_index_in_dim(total, (line - (chip ^ bit)) % chips, 0, False)

    bits = sorted(range(1, chips), key=lambda bit: (-bin(bit).count("1"), bit))
    return [lax.ppermute(block(bit), "seq", swaps(count, 2 * bit)) for bit in bits] + [block(0)]


def sum_of(parts):
    total = wide(parts[0])
    for part in parts[1:]:
        total = total + wide(part)
    return total


def body(outer_gate, inner_gate, signal, long_filter, grad_output, out_proj):
    seq_count, chan_count = lax.axis_size("seq"), lax.axis_size("chan")
    chan_rows, block_len = outer_gate.shape
    owned = chan_rows // seq_count
    per = block_len // LANES
    line = lax.axis_index("chan")
    tables = [jnp.asarray(t) for t in dft_tables(block_len * seq_count, seq_count)]

    if chan_count == 4:
        fars = unproject(out_proj, grad_output, [2], line, chan_count, splits=2)
        pair = prepare(inner_gate, signal, tie(long_filter, *fars))
        pair = pair.reshape(seq_count, owned, 2 * per, LANES)
        fars = [fars[0], tie(fars[1], pair)]
        fars = [lax.ppermute(far, "chan", [(2, 0), (1, 3), (3, 2), (0, 1)]) for far in fars]
        sent = exchange(pair)
        after, ups, downs = pair, [], []
        for half, far in enumerate(fars):
            near = unproject(
                tie(out_proj, after), grad_output, [1, 3], line, chan_count, far, [1, 2], half
            )
            ups.append(shift(near[0], 1))
            downs.append(shift(near[1], 3))
            after = near[1]
        sent = tie(sent, after)
        shares = [ups, downs, fars]
        flag = (line == 0) | (line == 3)
    else:
        pair = prepare(inner_gate, signal, long_filter)
        pair = pair.reshape(seq_count, owned, 2 * per, LANES)
        sent = exchange(pair)
        offsets = list(range(1, chan_count))
        blocks = unproject(out_proj, grad_output, offsets, line, chan_count)
        shares = [[shift(block, by)] for by, block in zip(offsets, blocks)]
        flag = line >= 0

    conv, spec_signal, spec_filter = convolve(sent, tables)
    own = unproject(tie(out_proj, conv), grad_output, [0], line, chan_count)
    shares = [held_in_hbm(*own), *shares]
    mixed, grad_outer, grad_conv = mix(exchange(conv), outer_gate, shares, flag)
    held = gather_first(mixed)
    grad_conv = grad_conv.reshape(seq_count, owned // 2, 2 * per, LANES)
    corr = correlate(exchange(grad_conv), spec_signal, spec_filter, tables)
    held = tie(held, corr)
    if chan_count == 4:
        passed = lax.select_n(line, held[0], held[2], held[1], held[0])
        middle = lax.ppermute(passed, "chan", [(0, 2), (3, 1), (2, 3), (1, 0)])
        corr = exchange(tie(corr, passed))
        held = tie(held, passed)
        core = lax.axis_index("seq") % 2
        other, mine = project([held[0], held[1], held[0], held[2]], grad_output, core)
        middle, other = lax.optimization_barrier((middle, other, corr))[:2]
        got = lax.ppermute(other, "seq", swaps(seq_count, 1))
        middle = both_cores([middle], grad_output)
        total = short(wide(mine) + wide(got))
        total = lax.dynamic_update_slice(total, middle, (2, 0, 0))
    else:
        corr = exchange(corr)
        total = both_cores(held, grad_output)
    parts = scatter_chips(total)
    grads = finish(tie(corr, parts[-1]), signal, inner_gate)
    return (grad_outer, *grads, sum_of(tie(parts, grads)))


def solution(mesh):
    tokens = P("chan", "seq")
    in_specs = (tokens, tokens, tokens, tokens, tokens, P(None, "chan"))
    out_specs = (tokens, tokens, tokens, tokens, P("seq", "chan"))
    return jax.shard_map(body, mesh=mesh, in_specs=in_specs, out_specs=out_specs, check_vma=False)
```

```python
import functools
import math

import jax
import jax.numpy as jnp
import numpy as np
from jax import lax
from jax.experimental import pallas as pl
from jax.experimental.pallas import tpu as pltpu
from jax.sharding import PartitionSpec as P

LANES = 128
VMEM_BYTES = 48 * 1024 * 1024


def wide(x):
    return x.astype(jnp.float32)


def short(x):
    return x.astype(jnp.bfloat16)


def held_in_hbm(*arrays):
    return [pltpu.with_memory_space_constraint(array, pltpu.HBM) for array in arrays]


def in_hbm(shape, dtype=jnp.bfloat16):
    return pltpu.HBM(shape, dtype)


def high_low(table, axis):
    high = table.astype(jnp.bfloat16)
    low = (table - high.astype(np.float64)).astype(jnp.bfloat16)
    return np.concatenate([high, low], axis=axis)


def dft_tables(tokens, blocks):
    outer = tokens // LANES
    per = outer // blocks
    freq = np.arange(outer) + 0.25
    angle = 2.0 * math.pi / outer * np.outer(freq, np.arange(outer))
    first = np.zeros((2, 2, outer, blocks, 2, per))
    last = np.zeros((blocks, 2, per, 2, 2, outer))
    for pair in range(2):
        first[pair, 0, :, :, pair, :] = np.cos(angle).reshape(outer, blocks, per)
        first[pair, 1, :, :, pair, :] = -np.sin(angle).reshape(outer, blocks, per)
        last[:, pair, :, pair, 0, :] = np.cos(angle.T).reshape(blocks, per, outer) / tokens
        last[:, pair, :, pair, 1, :] = -np.sin(angle.T).reshape(blocks, per, outer) / tokens
    first = high_low(first.reshape(4 * outer, 2 * outer), 1)
    last = high_low(last.reshape(2 * outer, 4 * outer), 1)
    turn = 2.0 * math.pi / tokens * np.outer(freq, np.arange(LANES))
    twiddle = np.stack([np.cos(turn), np.sin(turn)]).astype(np.float32)
    lane = 2.0 * math.pi / LANES * np.outer(np.arange(LANES), np.arange(LANES))
    cos, sin = np.cos(lane), np.sin(lane)
    forward = np.block([[cos, -sin], [sin, cos]]).astype(jnp.bfloat16)
    inverse = np.block([[cos, sin], [-sin, cos]]).astype(jnp.bfloat16)
    return first, forward, inverse, last, twiddle


def mxu(left, right):
    return jnp.dot(left, right, preferred_element_type=jnp.float32)


def forward_pair(pair_block, first, twiddle):
    outer = twiddle.shape[1]
    rows = pair_block.reshape(2 * outer, LANES)
    part = mxu(first, jnp.concatenate([rows, rows], axis=0))
    cos, sin = twiddle[0], twiddle[1]
    turned = []
    for pair in range(2):
        real = part[2 * pair * outer : (2 * pair + 1) * outer]
        imag = part[(2 * pair + 1) * outer : (2 * pair + 2) * outer]
        turned.append(
            jnp.concatenate([real * cos + imag * sin, imag * cos - real * sin], axis=1).astype(
                jnp.bfloat16
            )
        )
    return turned


def inverse_pair(spread, last, twiddle):
    cos, sin = twiddle[0], twiddle[1]
    parts = []
    for item in spread:
        real, imag = item[:, :LANES], item[:, LANES:]
        parts.append((real * cos - imag * sin).astype(jnp.bfloat16))
        parts.append((real * sin + imag * cos).astype(jnp.bfloat16))
    return mxu(last, jnp.concatenate(parts + parts, axis=0))


def lanes_dft(rows, table):
    return mxu(rows, table)


def convolve_kernel(pairs_ref, first_ref, forward_ref, inverse_ref, last_ref, twiddle_ref,
                    conv_ref, signal_ref, filter_ref, turned, spread):
    outer = twiddle_ref.shape[1]
    step = pairs_ref.shape[1]
    twiddle = twiddle_ref[...]
    for chan in range(step):
        pieces = forward_pair(pairs_ref[:, chan], first_ref[...], twiddle)
        for pair in range(2):
            turned[pl.ds((pair * step + chan) * outer, outer), :] = pieces[pair]
    half = step * outer
    signal = lanes_dft(turned[pl.ds(0, half), :], forward_ref[...])
    kernel = lanes_dft(turned[pl.ds(half, half), :], forward_ref[...])
    signal_ref[...] = signal.reshape(signal_ref.shape)
    filter_ref[...] = kernel.reshape(filter_ref.shape)
    sr, si = signal[:, :LANES], signal[:, LANES:]
    kr, ki = kernel[:, :LANES], kernel[:, LANES:]
    product = jnp.concatenate([kr * sr - ki * si, kr * si + ki * sr], axis=1).astype(jnp.bfloat16)
    spread[...] = lanes_dft(product, inverse_ref[...])
    for pair in range(step // 2):
        items = [spread[pl.ds((2 * pair + one) * outer, outer), :] for one in range(2)]
        out = inverse_pair(items, last_ref[...], twiddle)
        conv_ref[:, pair] = out.reshape(conv_ref.shape[0], -1, LANES).astype(jnp.bfloat16)


def correlate_kernel(pairs_ref, signal_ref, filter_ref, first_ref, forward_ref, inverse_ref,
                     last_ref, twiddle_ref, out_ref, turned, spread):
    outer = twiddle_ref.shape[1]
    step = signal_ref.shape[0]
    twiddle = twiddle_ref[...]
    for pair in range(step // 2):
        pieces = forward_pair(pairs_ref[:, pair], first_ref[...], twiddle)
        for one in range(2):
            turned[pl.ds((2 * pair + one) * outer, outer), :] = pieces[one]
    half = step * outer
    grad = lanes_dft(turned[...], forward_ref[...])
    gr, gi = grad[:, :LANES], grad[:, LANES:]
    for place, ref in enumerate((filter_ref, signal_ref)):
        other = ref[...].reshape(half, 2 * LANES)
        kr, ki = other[:, :LANES], other[:, LANES:]
        product = jnp.concatenate([kr * gr + ki * gi, kr * gi - ki * gr], axis=1)
        spread[place] = lanes_dft(product.astype(jnp.bfloat16), inverse_ref[...])
    for chan in range(step):
        items = [spread[place, pl.ds(chan * outer, outer), :] for place in range(2)]
        out = inverse_pair(items, last_ref[...], twiddle)
        out_ref[:, chan] = out.reshape(out_ref.shape[0], -1, LANES).astype(jnp.bfloat16)


def whole(table):
    zeros = (0,) * table.ndim
    return pl.BlockSpec(table.shape, lambda i: zeros)


def convolve(pairs, tables):
    blocks, chans, rows, _ = pairs.shape
    step = min(32, chans)
    outer = blocks * rows // 2
    spec = in_hbm((chans, outer, 2 * LANES), jnp.float32)
    spec_block = pl.BlockSpec((step, outer, 2 * LANES), lambda i: (i, 0, 0))
    return pl.pallas_call(
        convolve_kernel,
        grid=(chans // step,),
        in_specs=[pl.BlockSpec((blocks, step, rows, LANES), lambda i: (0, i, 0, 0))]
        + [whole(table) for table in tables],
        out_specs=[
            pl.BlockSpec((blocks, step // 2, rows, LANES), lambda i: (0, i, 0, 0)),
            spec_block,
            spec_block,
        ],
        out_shape=[in_hbm((blocks, chans // 2, rows, LANES)), spec, spec],
        scratch_shapes=[
            pltpu.VMEM((2 * step * outer, 2 * LANES), jnp.bfloat16),
            pltpu.VMEM((step * outer, 2 * LANES), jnp.float32),
        ],
        compiler_params=pltpu.CompilerParams(vmem_limit_bytes=VMEM_BYTES),
        name="convolve",
    )(pairs, *held_in_hbm(*tables))


def correlate(pairs, signal, kernel, tables):
    blocks, _, rows, _ = pairs.shape
    chans = signal.shape[0]
    step = min(16, chans)
    outer = blocks * rows // 2
    spec_block = pl.BlockSpec((step, outer, 2 * LANES), lambda i: (i, 0, 0))
    return pl.pallas_call(
        correlate_kernel,
        grid=(chans // step,),
        in_specs=[
            pl.BlockSpec((blocks, step // 2, rows, LANES), lambda i: (0, i, 0, 0)),
            spec_block,
            spec_block,
        ]
        + [whole(table) for table in tables],
        out_specs=pl.BlockSpec((blocks, step, rows, LANES), lambda i: (0, i, 0, 0)),
        out_shape=in_hbm((blocks, chans, rows, LANES)),
        scratch_shapes=[
            pltpu.VMEM((step * outer, 2 * LANES), jnp.bfloat16),
            pltpu.VMEM((2, step * outer, 2 * LANES), jnp.float32),
        ],
        compiler_params=pltpu.CompilerParams(vmem_limit_bytes=VMEM_BYTES),
        name="correlate",
    )(pairs, *held_in_hbm(signal, kernel, *tables))


def params():
    return pltpu.CompilerParams(vmem_limit_bytes=VMEM_BYTES)


def spread_lanes(target, rows, first, stride):
    count = rows.shape[0]
    for lane in range(rows.shape[1] // LANES):
        target[pl.ds(first + lane, count, stride=stride), :] = rows[:, lane * LANES : (lane + 1) * LANES]


def prepare_kernel(gate_ref, signal_ref, filter_ref, pair_ref, lines):
    per = gate_ref.shape[1] // LANES
    spread_lanes(lines, short(wide(gate_ref[...]) * wide(signal_ref[...])).astype(jnp.float32), 0, 2 * per)
    spread_lanes(lines, wide(filter_ref[...]), per, 2 * per)
    pair_ref[...] = short(lines[...]).reshape(pair_ref.shape)


def prepare(inner_gate, signal, long_filter):
    rows, length = signal.shape
    per = length // LANES
    step = rows // 2
    block = pl.BlockSpec((step, length), lambda i: (i, 0))
    return pl.pallas_call(
        prepare_kernel,
        grid=(2,),
        in_specs=[block] * 3,
        out_specs=pl.BlockSpec((step, 2 * per, LANES), lambda i: (i, 0, 0)),
        out_shape=in_hbm((rows, 2 * per, LANES)),
        scratch_shapes=[pltpu.VMEM((step * 2 * per, LANES), jnp.float32)],
        compiler_params=params(),
        name="prepare",
    )(*held_in_hbm(inner_gate, signal, long_filter))


def regard_kernel(parts, flag_ref, gate_ref, *refs):
    *share_refs, sum_ref, grad_ref, grads = refs
    rows, length = gate_ref.shape
    per = length // LANES
    groups = []
    for count in parts:
        groups.append(share_refs[:count])
        share_refs = share_refs[count:]
    for lane in range(per):
        cols = slice(lane * LANES, (lane + 1) * LANES)
        shares = []
        for group in groups:
            held = group[lane * len(group) // per]
            at = lane % (per // len(group)) * LANES
            shares.append(wide(held[:, at : at + LANES]))
        grad_mix = shares[0]
        for share in shares[1:-1]:
            grad_mix = grad_mix + share
        grad_mix = grad_mix + jnp.where(flag_ref[0] != 0, shares[-1], jnp.zeros_like(shares[-1]))
        sum_ref[:, cols] = grad_mix
        grads[pl.ds(lane, rows, stride=per), :] = grad_mix * wide(gate_ref[:, cols])
    grad_ref[...] = short(grads[...]).reshape(grad_ref.shape)


def regard(outer_gate, shares, flag):
    rows, length = outer_gate.shape
    parts = [len(share) for share in shares]
    cuts = [cut for share in shares for cut in share]
    per = length // LANES
    step = rows // 2
    token_rows = pl.BlockSpec((step, length), lambda i, at: (i, 0))
    return pl.pallas_call(
        functools.partial(regard_kernel, parts),
        grid_spec=pltpu.PrefetchScalarGridSpec(
            num_scalar_prefetch=1,
            grid=(2,),
            in_specs=[token_rows]
            + [pl.BlockSpec((step, cut.shape[1]), lambda i, at: (i, 0)) for cut in cuts],
            out_specs=[token_rows, pl.BlockSpec((step * per // 16, 16, LANES), lambda i, at: (i, 0, 0))],
            scratch_shapes=[pltpu.VMEM((step * per, LANES), jnp.float32)],
        ),
        out_shape=[in_hbm((rows, length), jnp.float32), in_hbm((rows * per // 16, 16, LANES))],
        compiler_params=params(),
        name="regard",
    )(flag.astype(jnp.int32).reshape(1), outer_gate, *cuts)


def mix_kernel(conv_ref, gate_ref, mixed_ref, out_ref, lines):
    rows, length = gate_ref.shape
    per = length // LANES
    lines[...] = wide(conv_ref[...].reshape(rows * per, LANES))
    for lane in range(per):
        cols = slice(lane * LANES, (lane + 1) * LANES)
        conv = lines[pl.ds(lane, rows, stride=per), :]
        out_ref[:, cols] = short(conv)
        mixed_ref[:, cols] = short(conv * wide(gate_ref[:, cols]))


def mix(conv, outer_gate):
    rows, length = outer_gate.shape
    per = length // LANES
    conv = conv.reshape(rows * per // 16, 16, LANES)
    step = rows // 2
    token_rows = pl.BlockSpec((step, length), lambda i: (i, 0))
    return pl.pallas_call(
        mix_kernel,
        grid=(2,),
        in_specs=[pl.BlockSpec((step * per // 16, 16, LANES), lambda i: (i, 0, 0)), token_rows],
        out_specs=[token_rows, token_rows],
        out_shape=[in_hbm((rows, length))] * 2,
        scratch_shapes=[pltpu.VMEM((step * per, LANES), jnp.float32)],
        compiler_params=params(),
        name="mix",
    )(conv, outer_gate)


def finish_kernel(corr_ref, signal_ref, gate_ref, inner_ref, signal_out_ref, filter_ref, lines):
    rows, length = signal_ref.shape
    per = length // LANES
    lines[...] = wide(corr_ref[...].reshape(rows * 2 * per, LANES))
    for lane in range(per):
        cols = slice(lane * LANES, (lane + 1) * LANES)
        grad_prod = lines[pl.ds(lane, rows, stride=2 * per), :]
        filter_ref[:, cols] = lines[pl.ds(per + lane, rows, stride=2 * per), :]
        inner_ref[:, cols] = short(grad_prod * wide(signal_ref[:, cols]))
        signal_out_ref[:, cols] = short(grad_prod * wide(gate_ref[:, cols]))


def finish(corr, signal, inner_gate):
    rows, length = signal.shape
    per = length // LANES
    step = rows // 2
    block = pl.BlockSpec((step, length), lambda i: (i, 0))
    return pl.pallas_call(
        finish_kernel,
        grid=(2,),
        in_specs=[pl.BlockSpec((step, 2 * per, LANES), lambda i: (i, 0, 0)), block, block],
        out_specs=[block] * 3,
        out_shape=[jax.ShapeDtypeStruct((rows, length), jnp.bfloat16)] * 2
        + [jax.ShapeDtypeStruct((rows, length), jnp.float32)],
        scratch_shapes=[pltpu.VMEM((step * 2 * per, LANES), jnp.float32)],
        compiler_params=params(),
        name="finish",
    )(corr.reshape(rows, 2 * per, LANES), *held_in_hbm(signal, inner_gate))


def unproject_kernel(count, splits, add_from, place_ref, *refs):
    rows, width = refs[0].shape
    grad_ref, weights = refs[count], refs[-1]
    out_refs = refs[-1 - count * splits : -1]

    @pl.when(pl.program_id(0) == 0)
    def _():
        for row in range(count):
            weights[pl.ds(row * rows, rows), :] = refs[row][...]

    out = short(mxu(weights[...], grad_ref[...]))
    for row in range(count):
        part = out[row * rows : (row + 1) * rows]
        if add_from is not None:
            more = wide(refs[count + 1][...])
            part = short(wide(part) + jnp.where(place_ref[0] == add_from[row], more, jnp.zeros_like(more)))
        for split in range(splits):

            @pl.when(pl.program_id(0) * splits // pl.num_programs(0) == split)
            def _(part=part, ref=out_refs[row * splits + split]):
                ref[...] = part


def unproject(out_proj, grad_output, offsets, place, count, more=None, add_from=None, half=None, splits=1):
    width, length = grad_output.shape
    rows = out_proj.shape[0] // count
    step = 512 if half is None else 256
    length = length if half is None else length // 2
    first = 0 if half is None else half * (length // step)
    in_specs = [
        pl.BlockSpec((rows, width), lambda i, at, by=by: (lax.rem(at[0] + by, count), 0))
        for by in offsets
    ]
    out_block = pl.BlockSpec((rows, step), lambda i, at: (0, i if splits == 1 else 0))
    extra = [] if more is None else [more]
    return pl.pallas_call(
        functools.partial(unproject_kernel, len(offsets), splits, add_from),
        grid_spec=pltpu.PrefetchScalarGridSpec(
            num_scalar_prefetch=1,
            grid=(length // step,),
            in_specs=in_specs
            + [pl.BlockSpec((width, step), lambda i, at: (0, first + i))]
            + [out_block] * len(extra),
            out_specs=[out_block] * (len(offsets) * splits),
            scratch_shapes=[pltpu.VMEM((len(offsets) * rows, width), jnp.bfloat16)],
        ),
        out_shape=[in_hbm((rows, length // splits))] * (len(offsets) * splits),
        compiler_params=params(),
        cost_estimate=pl.CostEstimate(flops=40 * 10**9, bytes_accessed=10**8, transcendentals=0),
        name="unproject",
    )(place.reshape(1), *held_in_hbm(*[out_proj] * len(offsets), grad_output), *extra)


def project_kernel(core_ref, *refs):
    *piece_refs, grad_ref, other_ref, mine_ref, rows = refs
    count, small, _ = mine_ref.shape

    @pl.when(pl.program_id(0) == 0)
    def _():
        for place, which in enumerate((1 - core_ref[0], core_ref[0])):
            first = pl.multiple_of(which * small, small)
            for slot, piece in enumerate(piece_refs):
                rows[pl.ds((place * count + slot) * small, small), :] = piece[pl.ds(first, small), :]

    out = lax.dot_general(
        rows[...], grad_ref[...], (((1,), (1,)), ((), ())), preferred_element_type=jnp.float32
    )
    out = short(out).reshape(2, count, small, -1)
    other_ref[...] = out[0]
    mine_ref[...] = out[1]


def project(pieces, grad_output, core):
    width, length = grad_output.shape
    small = pieces[0].shape[0] // 2
    step = min(1024, width)
    out_block = pl.BlockSpec((len(pieces), small, step), lambda i, at: (0, 0, i))
    out = in_hbm((len(pieces), small, width))
    return pl.pallas_call(
        project_kernel,
        grid_spec=pltpu.PrefetchScalarGridSpec(
            num_scalar_prefetch=1,
            grid=(width // step,),
            in_specs=[pl.BlockSpec(pieces[0].shape, lambda i, at: (0, 0))] * len(pieces)
            + [pl.BlockSpec((step, length), lambda i, at: (i, 0))],
            out_specs=[out_block, out_block],
            scratch_shapes=[pltpu.VMEM((2 * len(pieces) * small, length), jnp.bfloat16)],
        ),
        out_shape=[out, out],
        compiler_params=params(),
        name="project",
    )(core.reshape(1), *pieces, *held_in_hbm(grad_output))


def swaps(count, bit):
    return [(place, place ^ bit) for place in range(count)]


def exchange(blocks):
    return lax.all_to_all(blocks, "seq", split_axis=0, concat_axis=0, tiled=True)


def tie(first, *others):
    return lax.optimization_barrier((first,) + others)[0]


def shift(block, by):
    count = lax.axis_size("chan")
    return lax.ppermute(block, "chan", [(i, (i + by) % count) for i in range(count)])


def gather_first(shard):
    count, place = lax.axis_size("chan"), lax.axis_index("chan")
    if count != 4:
        return [shard] + [shift(shard, by) for by in range(1, count)]
    return [shard, shift(shard, 1), shift(shard, 3)]


def both_cores(pieces, grad_output):
    count, core = lax.axis_size("seq"), lax.axis_index("seq") % 2
    rows = jnp.stack(pieces)
    sums = short(
        jnp.einsum("zct,dt->zcd", rows, grad_output, preferred_element_type=jnp.float32)
    ).reshape(len(pieces), 2, -1, grad_output.shape[0])
    got = lax.ppermute(lax.dynamic_index_in_dim(sums, 1 - core, 1, False), "seq", swaps(count, 1))
    return short(wide(lax.dynamic_index_in_dim(sums, core, 1, False)) + wide(got))


def scatter_chips(total):
    count, chips = lax.axis_size("seq"), lax.axis_size("chan")
    line, chip = lax.axis_index("chan"), lax.axis_index("seq") // 2

    def block(bit):
        return lax.dynamic_index_in_dim(total, (line - (chip ^ bit)) % chips, 0, False)

    bits = sorted(range(1, chips), key=lambda bit: (-bin(bit).count("1"), bit))
    return [lax.ppermute(block(bit), "seq", swaps(count, 2 * bit)) for bit in bits] + [block(0)]


def sum_of(parts):
    total = wide(parts[0])
    for part in parts[1:]:
        total = total + wide(part)
    return total


def body(outer_gate, inner_gate, signal, long_filter, grad_output, out_proj):
    seq_count, chan_count = lax.axis_size("seq"), lax.axis_size("chan")
    chan_rows, block_len = outer_gate.shape
    owned = chan_rows // seq_count
    per = block_len // LANES
    line = lax.axis_index("chan")
    tables = [jnp.asarray(t) for t in dft_tables(block_len * seq_count, seq_count)]

    if chan_count == 4:
        fars = unproject(out_proj, grad_output, [2], line, chan_count, splits=2)
        pair = prepare(inner_gate, signal, tie(long_filter, *fars))
        pair = pair.reshape(seq_count, owned, 2 * per, LANES)
        fars = [fars[0], tie(fars[1], pair)]
        fars = [lax.ppermute(far, "chan", [(2, 0), (1, 3), (3, 2), (0, 1)]) for far in fars]
        sent = exchange(pair)
        after, ups, downs = pair, [], []
        for half, far in enumerate(fars):
            near = unproject(
                tie(out_proj, after), grad_output, [1, 3], line, chan_count, far, [1, 2], half
            )
            ups.append(shift(near[0], 1))
            downs.append(shift(near[1], 3))
            after = near[1]
        sent = tie(sent, after)
        shares = [ups, downs, fars]
        flag = (line == 0) | (line == 3)
    else:
        pair = prepare(inner_gate, signal, long_filter)
        pair = pair.reshape(seq_count, owned, 2 * per, LANES)
        sent = exchange(pair)
        offsets = list(range(1, chan_count))
        blocks = unproject(out_proj, grad_output, offsets, line, chan_count)
        shares = [[shift(block, by)] for by, block in zip(offsets, blocks)]
        flag = line >= 0

    conv, spec_signal, spec_filter = convolve(sent, tables)
    own = unproject(tie(out_proj, conv), grad_output, [0], line, chan_count)
    shares = [held_in_hbm(*own), *shares]
    grad_mix, grad_conv = regard(outer_gate, shares, flag)
    mixed, conv_out = mix(tie(exchange(conv), grad_conv), outer_gate)
    held = gather_first(mixed)
    grad_conv = tie(grad_conv, mixed).reshape(seq_count, owned // 2, 2 * per, LANES)
    corr = correlate(exchange(grad_conv), spec_signal, spec_filter, tables)
    held = tie(held, corr)
    if chan_count == 4:
        passed = lax.select_n(line, held[0], held[2], held[1], held[0])
        middle = lax.ppermute(passed, "chan", [(0, 2), (3, 1), (2, 3), (1, 0)])
        corr = exchange(corr)
        held = tie(held, passed)
        core = lax.axis_index("seq") % 2
        other, mine = project([held[0], held[1], held[0], held[2]], grad_output, core)
        middle, other = lax.optimization_barrier((middle, other, corr))[:2]
        got = lax.ppermute(other, "seq", swaps(seq_count, 1))
        middle = both_cores([middle], grad_output)
        total = short(wide(mine) + wide(got))
        total = lax.dynamic_update_slice(total, middle, (2, 0, 0))
    else:
        corr = exchange(corr)
        total = both_cores(held, grad_output)
    parts = scatter_chips(total)
    grads = finish(tie(corr, parts[-1]), signal, inner_gate)
    grad_outer = short(tie(grad_mix, corr) * wide(conv_out))
    return (grad_outer, *grads, sum_of(tie(parts, grads)))


def solution(mesh):
    tokens = P("chan", "seq")
    in_specs = (tokens, tokens, tokens, tokens, tokens, P(None, "chan"))
    out_specs = (tokens, tokens, tokens, tokens, P("seq", "chan"))
    return jax.shard_map(body, mesh=mesh, in_specs=in_specs, out_specs=out_specs, check_vma=False)
```

```python
import functools
import math

import jax
import jax.numpy as jnp
import numpy as np
from jax import lax
from jax.experimental import pallas as pl
from jax.experimental.pallas import tpu as pltpu
from jax.sharding import PartitionSpec as P

LANES = 128
VMEM_BYTES = 48 * 1024 * 1024


def wide(x):
    return x.astype(jnp.float32)


def short(x):
    return x.astype(jnp.bfloat16)


def held_in_hbm(*arrays):
    return [pltpu.with_memory_space_constraint(array, pltpu.HBM) for array in arrays]


def in_hbm(shape, dtype=jnp.bfloat16):
    return pltpu.HBM(shape, dtype)


def high_low(table, axis):
    high = table.astype(jnp.bfloat16)
    low = (table - high.astype(np.float64)).astype(jnp.bfloat16)
    return np.concatenate([high, low], axis=axis)


def dft_tables(tokens, blocks):
    outer = tokens // LANES
    per = outer // blocks
    freq = np.arange(outer) + 0.25
    angle = 2.0 * math.pi / outer * np.outer(freq, np.arange(outer))
    first = np.zeros((2, 2, outer, blocks, 2, per))
    last = np.zeros((blocks, 2, per, 2, 2, outer))
    for pair in range(2):
        first[pair, 0, :, :, pair, :] = np.cos(angle).reshape(outer, blocks, per)
        first[pair, 1, :, :, pair, :] = -np.sin(angle).reshape(outer, blocks, per)
        last[:, pair, :, pair, 0, :] = np.cos(angle.T).reshape(blocks, per, outer) / tokens
        last[:, pair, :, pair, 1, :] = -np.sin(angle.T).reshape(blocks, per, outer) / tokens
    first = high_low(first.reshape(4 * outer, 2 * outer), 1)
    last = high_low(last.reshape(2 * outer, 4 * outer), 1)
    turn = 2.0 * math.pi / tokens * np.outer(freq, np.arange(LANES))
    twiddle = np.stack([np.cos(turn), np.sin(turn)]).astype(np.float32)
    lane = 2.0 * math.pi / LANES * np.outer(np.arange(LANES), np.arange(LANES))
    cos, sin = np.cos(lane), np.sin(lane)
    forward = np.block([[cos, -sin], [sin, cos]]).astype(jnp.bfloat16)
    inverse = np.block([[cos, sin], [-sin, cos]]).astype(jnp.bfloat16)
    return first, forward, inverse, last, twiddle


def mxu(left, right):
    return jnp.dot(left, right, preferred_element_type=jnp.float32)


def forward_pair(pair_block, first, twiddle):
    outer = twiddle.shape[1]
    rows = pair_block.reshape(2 * outer, LANES)
    part = mxu(first, jnp.concatenate([rows, rows], axis=0))
    cos, sin = twiddle[0], twiddle[1]
    turned = []
    for pair in range(2):
        real = part[2 * pair * outer : (2 * pair + 1) * outer]
        imag = part[(2 * pair + 1) * outer : (2 * pair + 2) * outer]
        turned.append(
            jnp.concatenate([real * cos + imag * sin, imag * cos - real * sin], axis=1).astype(
                jnp.bfloat16
            )
        )
    return turned


def inverse_pair(spread, last, twiddle):
    cos, sin = twiddle[0], twiddle[1]
    parts = []
    for item in spread:
        real, imag = item[:, :LANES], item[:, LANES:]
        parts.append((real * cos - imag * sin).astype(jnp.bfloat16))
        parts.append((real * sin + imag * cos).astype(jnp.bfloat16))
    return mxu(last, jnp.concatenate(parts + parts, axis=0))


def lanes_dft(rows, table):
    return mxu(rows, table)


def convolve_kernel(pairs_ref, first_ref, forward_ref, inverse_ref, last_ref, twiddle_ref,
                    conv_ref, signal_ref, filter_ref, turned, spread):
    outer = twiddle_ref.shape[1]
    step = pairs_ref.shape[1]
    twiddle = twiddle_ref[...]
    for chan in range(step):
        pieces = forward_pair(pairs_ref[:, chan], first_ref[...], twiddle)
        for pair in range(2):
            turned[pl.ds((pair * step + chan) * outer, outer), :] = pieces[pair]
    half = step * outer
    signal = lanes_dft(turned[pl.ds(0, half), :], forward_ref[...])
    kernel = lanes_dft(turned[pl.ds(half, half), :], forward_ref[...])
    signal_ref[...] = signal.reshape(signal_ref.shape)
    filter_ref[...] = kernel.reshape(filter_ref.shape)
    sr, si = signal[:, :LANES], signal[:, LANES:]
    kr, ki = kernel[:, :LANES], kernel[:, LANES:]
    product = jnp.concatenate([kr * sr - ki * si, kr * si + ki * sr], axis=1).astype(jnp.bfloat16)
    spread[...] = lanes_dft(product, inverse_ref[...])
    for pair in range(step // 2):
        items = [spread[pl.ds((2 * pair + one) * outer, outer), :] for one in range(2)]
        out = inverse_pair(items, last_ref[...], twiddle)
        conv_ref[:, pair] = out.reshape(conv_ref.shape[0], -1, LANES).astype(jnp.bfloat16)


def correlate_kernel(pairs_ref, signal_ref, filter_ref, first_ref, forward_ref, inverse_ref,
                     last_ref, twiddle_ref, out_ref, turned, spread):
    outer = twiddle_ref.shape[1]
    step = signal_ref.shape[0]
    twiddle = twiddle_ref[...]
    for pair in range(step // 2):
        pieces = forward_pair(pairs_ref[:, pair], first_ref[...], twiddle)
        for one in range(2):
            turned[pl.ds((2 * pair + one) * outer, outer), :] = pieces[one]
    half = step * outer
    grad = lanes_dft(turned[...], forward_ref[...])
    gr, gi = grad[:, :LANES], grad[:, LANES:]
    for place, ref in enumerate((filter_ref, signal_ref)):
        other = ref[...].reshape(half, 2 * LANES)
        kr, ki = other[:, :LANES], other[:, LANES:]
        product = jnp.concatenate([kr * gr + ki * gi, kr * gi - ki * gr], axis=1)
        spread[place] = lanes_dft(product.astype(jnp.bfloat16), inverse_ref[...])
    for chan in range(step):
        items = [spread[place, pl.ds(chan * outer, outer), :] for place in range(2)]
        out = inverse_pair(items, last_ref[...], twiddle)
        out_ref[:, chan] = out.reshape(out_ref.shape[0], -1, LANES).astype(jnp.bfloat16)


def whole(table):
    zeros = (0,) * table.ndim
    return pl.BlockSpec(table.shape, lambda i: zeros)


def convolve(pairs, tables):
    blocks, chans, rows, _ = pairs.shape
    step = min(32, chans)
    outer = blocks * rows // 2
    spec = in_hbm((chans, outer, 2 * LANES), jnp.float32)
    spec_block = pl.BlockSpec((step, outer, 2 * LANES), lambda i: (i, 0, 0))
    return pl.pallas_call(
        convolve_kernel,
        grid=(chans // step,),
        in_specs=[pl.BlockSpec((blocks, step, rows, LANES), lambda i: (0, i, 0, 0))]
        + [whole(table) for table in tables],
        out_specs=[
            pl.BlockSpec((blocks, step // 2, rows, LANES), lambda i: (0, i, 0, 0)),
            spec_block,
            spec_block,
        ],
        out_shape=[in_hbm((blocks, chans // 2, rows, LANES)), spec, spec],
        scratch_shapes=[
            pltpu.VMEM((2 * step * outer, 2 * LANES), jnp.bfloat16),
            pltpu.VMEM((step * outer, 2 * LANES), jnp.float32),
        ],
        compiler_params=pltpu.CompilerParams(vmem_limit_bytes=VMEM_BYTES),
        name="convolve",
    )(pairs, *held_in_hbm(*tables))


def correlate(pairs, signal, kernel, tables):
    blocks, _, rows, _ = pairs.shape
    chans = signal.shape[0]
    step = min(16, chans)
    outer = blocks * rows // 2
    spec_block = pl.BlockSpec((step, outer, 2 * LANES), lambda i: (i, 0, 0))
    return pl.pallas_call(
        correlate_kernel,
        grid=(chans // step,),
        in_specs=[
            pl.BlockSpec((blocks, step // 2, rows, LANES), lambda i: (0, i, 0, 0)),
            spec_block,
            spec_block,
        ]
        + [whole(table) for table in tables],
        out_specs=pl.BlockSpec((blocks, step, rows, LANES), lambda i: (0, i, 0, 0)),
        out_shape=in_hbm((blocks, chans, rows, LANES)),
        scratch_shapes=[
            pltpu.VMEM((step * outer, 2 * LANES), jnp.bfloat16),
            pltpu.VMEM((2, step * outer, 2 * LANES), jnp.float32),
        ],
        compiler_params=pltpu.CompilerParams(vmem_limit_bytes=VMEM_BYTES),
        name="correlate",
    )(pairs, *held_in_hbm(signal, kernel, *tables))


def params():
    return pltpu.CompilerParams(vmem_limit_bytes=VMEM_BYTES)


def spread_lanes(target, rows, first, stride):
    count = rows.shape[0]
    for lane in range(rows.shape[1] // LANES):
        target[pl.ds(first + lane, count, stride=stride), :] = rows[:, lane * LANES : (lane + 1) * LANES]


def prepare_kernel(gate_ref, signal_ref, filter_ref, pair_ref, lines):
    per = gate_ref.shape[1] // LANES
    spread_lanes(lines, short(wide(gate_ref[...]) * wide(signal_ref[...])).astype(jnp.float32), 0, 2 * per)
    spread_lanes(lines, wide(filter_ref[...]), per, 2 * per)
    held = lines[pl.ds(0, gate_ref.shape[0] * 2 * per), :]
    pair_ref[...] = short(held).reshape(pair_ref.shape)


def prepare(inner_gate, signal, long_filter):
    rows, length = signal.shape
    per = length // LANES
    step = rows // 2
    block = pl.BlockSpec((step, length), lambda i: (i, 0))
    return pl.pallas_call(
        prepare_kernel,
        grid=(2,),
        in_specs=[block] * 3,
        out_specs=pl.BlockSpec((step, 2 * per, LANES), lambda i: (i, 0, 0)),
        out_shape=in_hbm((rows, 2 * per, LANES)),
        scratch_shapes=[pltpu.VMEM(((step + 1) * 2 * per, LANES), jnp.float32)],
        compiler_params=params(),
        name="prepare",
    )(*held_in_hbm(inner_gate, signal, long_filter))


def regard_kernel(parts, flag_ref, gate_ref, *refs):
    *share_refs, sum_ref, grad_ref, grads = refs
    rows, length = gate_ref.shape
    per = length // LANES
    groups = []
    for count in parts:
        groups.append(share_refs[:count])
        share_refs = share_refs[count:]
    for lane in range(per):
        cols = slice(lane * LANES, (lane + 1) * LANES)
        shares = []
        for group in groups:
            held = group[lane * len(group) // per]
            at = lane % (per // len(group)) * LANES
            shares.append(wide(held[:, at : at + LANES]))
        grad_mix = shares[0]
        for share in shares[1:-1]:
            grad_mix = grad_mix + share
        grad_mix = grad_mix + jnp.where(flag_ref[0] != 0, shares[-1], jnp.zeros_like(shares[-1]))
        sum_ref[:, cols] = grad_mix
        grads[pl.ds(lane, rows, stride=per), :] = grad_mix * wide(gate_ref[:, cols])
    grad_ref[...] = short(grads[pl.ds(0, rows * per), :]).reshape(grad_ref.shape)


def regard(outer_gate, shares, flag):
    rows, length = outer_gate.shape
    parts = [len(share) for share in shares]
    cuts = [cut for share in shares for cut in share]
    per = length // LANES
    step = rows // 2
    token_rows = pl.BlockSpec((step, length), lambda i, at: (i, 0))
    return pl.pallas_call(
        functools.partial(regard_kernel, parts),
        grid_spec=pltpu.PrefetchScalarGridSpec(
            num_scalar_prefetch=1,
            grid=(2,),
            in_specs=[token_rows]
            + [pl.BlockSpec((step, cut.shape[1]), lambda i, at: (i, 0)) for cut in cuts],
            out_specs=[token_rows, pl.BlockSpec((step * per // 16, 16, LANES), lambda i, at: (i, 0, 0))],
            scratch_shapes=[pltpu.VMEM(((step + 1) * per, LANES), jnp.float32)],
        ),
        out_shape=[in_hbm((rows, length), jnp.float32), in_hbm((rows * per // 16, 16, LANES))],
        compiler_params=params(),
        name="regard",
    )(flag.astype(jnp.int32).reshape(1), outer_gate, *cuts)


def mix_kernel(conv_ref, gate_ref, mixed_ref, out_ref, lines):
    rows, length = gate_ref.shape
    per = length // LANES
    lines[pl.ds(0, rows * per), :] = wide(conv_ref[...].reshape(rows * per, LANES))
    for lane in range(per):
        cols = slice(lane * LANES, (lane + 1) * LANES)
        conv = lines[pl.ds(lane, rows, stride=per), :]
        out_ref[:, cols] = short(conv)
        mixed_ref[:, cols] = short(conv * wide(gate_ref[:, cols]))


def mix(conv, outer_gate):
    rows, length = outer_gate.shape
    per = length // LANES
    conv = conv.reshape(rows * per // 16, 16, LANES)
    step = rows // 2
    token_rows = pl.BlockSpec((step, length), lambda i: (i, 0))
    return pl.pallas_call(
        mix_kernel,
        grid=(2,),
        in_specs=[pl.BlockSpec((step * per // 16, 16, LANES), lambda i: (i, 0, 0)), token_rows],
        out_specs=[token_rows, token_rows],
        out_shape=[in_hbm((rows, length))] * 2,
        scratch_shapes=[pltpu.VMEM(((step + 1) * per, LANES), jnp.float32)],
        compiler_params=params(),
        name="mix",
    )(conv, outer_gate)


def finish_kernel(corr_ref, signal_ref, gate_ref, inner_ref, signal_out_ref, filter_ref, lines):
    rows, length = signal_ref.shape
    per = length // LANES
    lines[pl.ds(0, rows * 2 * per), :] = wide(corr_ref[...].reshape(rows * 2 * per, LANES))
    for lane in range(per):
        cols = slice(lane * LANES, (lane + 1) * LANES)
        grad_prod = lines[pl.ds(lane, rows, stride=2 * per), :]
        filter_ref[:, cols] = lines[pl.ds(per + lane, rows, stride=2 * per), :]
        inner_ref[:, cols] = short(grad_prod * wide(signal_ref[:, cols]))
        signal_out_ref[:, cols] = short(grad_prod * wide(gate_ref[:, cols]))


def finish(corr, signal, inner_gate):
    rows, length = signal.shape
    per = length // LANES
    step = rows // 2
    block = pl.BlockSpec((step, length), lambda i: (i, 0))
    return pl.pallas_call(
        finish_kernel,
        grid=(2,),
        in_specs=[pl.BlockSpec((step, 2 * per, LANES), lambda i: (i, 0, 0)), block, block],
        out_specs=[block] * 3,
        out_shape=[jax.ShapeDtypeStruct((rows, length), jnp.bfloat16)] * 2
        + [jax.ShapeDtypeStruct((rows, length), jnp.float32)],
        scratch_shapes=[pltpu.VMEM(((step + 1) * 2 * per, LANES), jnp.float32)],
        compiler_params=params(),
        name="finish",
    )(corr.reshape(rows, 2 * per, LANES), *held_in_hbm(signal, inner_gate))


def unproject_kernel(count, splits, add_from, place_ref, *refs):
    rows, width = refs[0].shape
    grad_ref, weights = refs[count], refs[-1]
    out_refs = refs[-1 - count * splits : -1]

    @pl.when(pl.program_id(0) == 0)
    def _():
        for row in range(count):
            weights[pl.ds(row * rows, rows), :] = refs[row][...]

    out = short(mxu(weights[...], grad_ref[...]))
    for row in range(count):
        part = out[row * rows : (row + 1) * rows]
        if add_from is not None:
            more = wide(refs[count + 1][...])
            part = short(wide(part) + jnp.where(place_ref[0] == add_from[row], more, jnp.zeros_like(more)))
        for split in range(splits):

            @pl.when(pl.program_id(0) * splits // pl.num_programs(0) == split)
            def _(part=part, ref=out_refs[row * splits + split]):
                ref[...] = part


def unproject(out_proj, grad_output, offsets, place, count, more=None, add_from=None, half=None, splits=1):
    width, length = grad_output.shape
    rows = out_proj.shape[0] // count
    step = 512 if half is None else 256
    length = length if half is None else length // 2
    first = 0 if half is None else half * (length // step)
    in_specs = [
        pl.BlockSpec((rows, width), lambda i, at, by=by: (lax.rem(at[0] + by, count), 0))
        for by in offsets
    ]
    out_block = pl.BlockSpec((rows, step), lambda i, at: (0, i if splits == 1 else 0))
    extra = [] if more is None else [more]
    return pl.pallas_call(
        functools.partial(unproject_kernel, len(offsets), splits, add_from),
        grid_spec=pltpu.PrefetchScalarGridSpec(
            num_scalar_prefetch=1,
            grid=(length // step,),
            in_specs=in_specs
            + [pl.BlockSpec((width, step), lambda i, at: (0, first + i))]
            + [out_block] * len(extra),
            out_specs=[out_block] * (len(offsets) * splits),
            scratch_shapes=[pltpu.VMEM((len(offsets) * rows, width), jnp.bfloat16)],
        ),
        out_shape=[in_hbm((rows, length // splits))] * (len(offsets) * splits),
        compiler_params=params(),
        cost_estimate=pl.CostEstimate(flops=40 * 10**9, bytes_accessed=10**8, transcendentals=0),
        name="unproject",
    )(place.reshape(1), *held_in_hbm(*[out_proj] * len(offsets), grad_output), *extra)


def project_kernel(core_ref, *refs):
    *piece_refs, grad_ref, other_ref, mine_ref, rows = refs
    count, small, _ = mine_ref.shape

    @pl.when(pl.program_id(0) == 0)
    def _():
        for place, which in enumerate((1 - core_ref[0], core_ref[0])):
            first = pl.multiple_of(which * small, small)
            for slot, piece in enumerate(piece_refs):
                rows[pl.ds((place * count + slot) * small, small), :] = piece[pl.ds(first, small), :]

    out = lax.dot_general(
        rows[...], grad_ref[...], (((1,), (1,)), ((), ())), preferred_element_type=jnp.float32
    )
    out = short(out).reshape(2, count, small, -1)
    other_ref[...] = out[0]
    mine_ref[...] = out[1]


def project(pieces, grad_output, core):
    width, length = grad_output.shape
    small = pieces[0].shape[0] // 2
    step = min(1024, width)
    out_block = pl.BlockSpec((len(pieces), small, step), lambda i, at: (0, 0, i))
    out = in_hbm((len(pieces), small, width))
    return pl.pallas_call(
        project_kernel,
        grid_spec=pltpu.PrefetchScalarGridSpec(
            num_scalar_prefetch=1,
            grid=(width // step,),
            in_specs=[pl.BlockSpec(pieces[0].shape, lambda i, at: (0, 0))] * len(pieces)
            + [pl.BlockSpec((step, length), lambda i, at: (i, 0))],
            out_specs=[out_block, out_block],
            scratch_shapes=[pltpu.VMEM((2 * len(pieces) * small, length), jnp.bfloat16)],
        ),
        out_shape=[out, out],
        compiler_params=params(),
        name="project",
    )(core.reshape(1), *pieces, *held_in_hbm(grad_output))


def swaps(count, bit):
    return [(place, place ^ bit) for place in range(count)]


def exchange(blocks):
    return lax.all_to_all(blocks, "seq", split_axis=0, concat_axis=0, tiled=True)


def tie(first, *others):
    return lax.optimization_barrier((first,) + others)[0]


def shift(block, by):
    count = lax.axis_size("chan")
    return lax.ppermute(block, "chan", [(i, (i + by) % count) for i in range(count)])


def gather_first(shard):
    count, place = lax.axis_size("chan"), lax.axis_index("chan")
    if count != 4:
        return [shard] + [shift(shard, by) for by in range(1, count)]
    return [shard, shift(shard, 1), shift(shard, 3)]


def both_cores(pieces, grad_output):
    count, core = lax.axis_size("seq"), lax.axis_index("seq") % 2
    rows = jnp.stack(pieces)
    sums = short(
        jnp.einsum("zct,dt->zcd", rows, grad_output, preferred_element_type=jnp.float32)
    ).reshape(len(pieces), 2, -1, grad_output.shape[0])
    got = lax.ppermute(lax.dynamic_index_in_dim(sums, 1 - core, 1, False), "seq", swaps(count, 1))
    return short(wide(lax.dynamic_index_in_dim(sums, core, 1, False)) + wide(got))


def scatter_chips(total):
    count, chips = lax.axis_size("seq"), lax.axis_size("chan")
    line, chip = lax.axis_index("chan"), lax.axis_index("seq") // 2

    def block(bit):
        return lax.dynamic_index_in_dim(total, (line - (chip ^ bit)) % chips, 0, False)

    bits = sorted(range(1, chips), key=lambda bit: (-bin(bit).count("1"), bit))
    return [lax.ppermute(block(bit), "seq", swaps(count, 2 * bit)) for bit in bits] + [block(0)]


def sum_of(parts):
    total = wide(parts[0])
    for part in parts[1:]:
        total = total + wide(part)
    return total


def body(outer_gate, inner_gate, signal, long_filter, grad_output, out_proj):
    seq_count, chan_count = lax.axis_size("seq"), lax.axis_size("chan")
    chan_rows, block_len = outer_gate.shape
    owned = chan_rows // seq_count
    per = block_len // LANES
    line = lax.axis_index("chan")
    tables = [jnp.asarray(t) for t in dft_tables(block_len * seq_count, seq_count)]

    if chan_count == 4:
        fars = unproject(out_proj, grad_output, [2], line, chan_count, splits=2)
        pair = prepare(inner_gate, signal, tie(long_filter, *fars))
        pair = pair.reshape(seq_count, owned, 2 * per, LANES)
        fars = [fars[0], tie(fars[1], pair)]
        fars = [lax.ppermute(far, "chan", [(2, 0), (1, 3), (3, 2), (0, 1)]) for far in fars]
        sent = exchange(pair)
        after, ups, downs = pair, [], []
        for half, far in enumerate(fars):
            near = unproject(
                tie(out_proj, after), grad_output, [1, 3], line, chan_count, far, [1, 2], half
            )
            ups.append(shift(near[0], 1))
            downs.append(shift(near[1], 3))
            after = near[1]
        sent = tie(sent, after)
        shares = [ups, downs, fars]
        flag = (line == 0) | (line == 3)
    else:
        pair = prepare(inner_gate, signal, long_filter)
        pair = pair.reshape(seq_count, owned, 2 * per, LANES)
        sent = exchange(pair)
        offsets = list(range(1, chan_count))
        blocks = unproject(out_proj, grad_output, offsets, line, chan_count)
        shares = [[shift(block, by)] for by, block in zip(offsets, blocks)]
        flag = line >= 0

    conv, spec_signal, spec_filter = convolve(sent, tables)
    own = unproject(tie(out_proj, conv), grad_output, [0], line, chan_count)
    shares = [held_in_hbm(*own), *shares]
    grad_mix, grad_conv = regard(outer_gate, shares, flag)
    mixed, conv_out = mix(tie(exchange(conv), grad_conv), outer_gate)
    held = gather_first(mixed)
    grad_conv = tie(grad_conv, mixed).reshape(seq_count, owned // 2, 2 * per, LANES)
    corr = correlate(exchange(grad_conv), spec_signal, spec_filter, tables)
    held = tie(held, corr)
    if chan_count == 4:
        passed = lax.select_n(line, held[0], held[2], held[1], held[0])
        middle = lax.ppermute(passed, "chan", [(0, 2), (3, 1), (2, 3), (1, 0)])
        corr = exchange(corr)
        held = tie(held, passed)
        core = lax.axis_index("seq") % 2
        other, mine = project([held[0], held[1], held[0], held[2]], grad_output, core)
        middle, other = lax.optimization_barrier((middle, other, corr))[:2]
        got = lax.ppermute(other, "seq", swaps(seq_count, 1))
        middle = both_cores([middle], grad_output)
        total = short(wide(mine) + wide(got))
        total = lax.dynamic_update_slice(total, middle, (2, 0, 0))
    else:
        corr = exchange(corr)
        total = both_cores(held, grad_output)
    parts = scatter_chips(total)
    grads = finish(tie(corr, parts[-1]), signal, inner_gate)
    grad_outer = short(tie(grad_mix, corr) * wide(conv_out))
    return (grad_outer, *grads, sum_of(tie(parts, grads)))


def solution(mesh):
    tokens = P("chan", "seq")
    in_specs = (tokens, tokens, tokens, tokens, tokens, P(None, "chan"))
    out_specs = (tokens, tokens, tokens, tokens, P("seq", "chan"))
    return jax.shard_map(body, mesh=mesh, in_specs=in_specs, out_specs=out_specs, check_vma=False)
```

```python
import functools
import math

import jax
import jax.numpy as jnp
import numpy as np
from jax import lax
from jax.experimental import pallas as pl
from jax.experimental.pallas import tpu as pltpu
from jax.sharding import PartitionSpec as P

LANES = 128
VMEM_BYTES = 48 * 1024 * 1024


def wide(x):
    return x.astype(jnp.float32)


def short(x):
    return x.astype(jnp.bfloat16)


def held_in_hbm(*arrays):
    return [pltpu.with_memory_space_constraint(array, pltpu.HBM) for array in arrays]


def in_hbm(shape, dtype=jnp.bfloat16):
    return pltpu.HBM(shape, dtype)


def high_low(table, axis):
    high = table.astype(jnp.bfloat16)
    low = (table - high.astype(np.float64)).astype(jnp.bfloat16)
    return np.concatenate([high, low], axis=axis)


def dft_tables(tokens, blocks):
    outer = tokens // LANES
    per = outer // blocks
    freq = np.arange(outer) + 0.25
    angle = 2.0 * math.pi / outer * np.outer(freq, np.arange(outer))
    first = np.zeros((2, 2, outer, blocks, 2, per))
    last = np.zeros((blocks, 2, per, 2, 2, outer))
    for pair in range(2):
        first[pair, 0, :, :, pair, :] = np.cos(angle).reshape(outer, blocks, per)
        first[pair, 1, :, :, pair, :] = -np.sin(angle).reshape(outer, blocks, per)
        last[:, pair, :, pair, 0, :] = np.cos(angle.T).reshape(blocks, per, outer) / tokens
        last[:, pair, :, pair, 1, :] = -np.sin(angle.T).reshape(blocks, per, outer) / tokens
    first = high_low(first.reshape(4 * outer, 2 * outer), 1)
    last = high_low(last.reshape(2 * outer, 4 * outer), 1)
    turn = 2.0 * math.pi / tokens * np.outer(freq, np.arange(LANES))
    twiddle = np.stack([np.cos(turn), np.sin(turn)]).astype(np.float32)
    lane = 2.0 * math.pi / LANES * np.outer(np.arange(LANES), np.arange(LANES))
    cos, sin = np.cos(lane), np.sin(lane)
    forward = np.block([[cos, -sin], [sin, cos]]).astype(jnp.bfloat16)
    inverse = np.block([[cos, sin], [-sin, cos]]).astype(jnp.bfloat16)
    return first, forward, inverse, last, twiddle


def mxu(left, right):
    return jnp.dot(left, right, preferred_element_type=jnp.float32)


def forward_pair(pair_block, first, twiddle):
    outer = twiddle.shape[1]
    rows = pair_block.reshape(2 * outer, LANES)
    part = mxu(first, jnp.concatenate([rows, rows], axis=0))
    cos, sin = twiddle[0], twiddle[1]
    turned = []
    for pair in range(2):
        real = part[2 * pair * outer : (2 * pair + 1) * outer]
        imag = part[(2 * pair + 1) * outer : (2 * pair + 2) * outer]
        turned.append(
            jnp.concatenate([real * cos + imag * sin, imag * cos - real * sin], axis=1).astype(
                jnp.bfloat16
            )
        )
    return turned


def inverse_pair(spread, last, twiddle):
    cos, sin = twiddle[0], twiddle[1]
    parts = []
    for item in spread:
        real, imag = item[:, :LANES], item[:, LANES:]
        parts.append((real * cos - imag * sin).astype(jnp.bfloat16))
        parts.append((real * sin + imag * cos).astype(jnp.bfloat16))
    return mxu(last, jnp.concatenate(parts + parts, axis=0))


def lanes_dft(rows, table):
    return mxu(rows, table)


def convolve_kernel(pairs_ref, first_ref, forward_ref, inverse_ref, last_ref, twiddle_ref,
                    conv_ref, signal_ref, filter_ref, turned, spread):
    outer = twiddle_ref.shape[1]
    step = pairs_ref.shape[1]
    twiddle = twiddle_ref[...]
    for chan in range(step):
        pieces = forward_pair(pairs_ref[:, chan], first_ref[...], twiddle)
        for pair in range(2):
            turned[pl.ds((pair * step + chan) * outer, outer), :] = pieces[pair]
    half = step * outer
    signal = lanes_dft(turned[pl.ds(0, half), :], forward_ref[...])
    kernel = lanes_dft(turned[pl.ds(half, half), :], forward_ref[...])
    signal_ref[...] = signal.reshape(signal_ref.shape)
    filter_ref[...] = kernel.reshape(filter_ref.shape)
    sr, si = signal[:, :LANES], signal[:, LANES:]
    kr, ki = kernel[:, :LANES], kernel[:, LANES:]
    product = jnp.concatenate([kr * sr - ki * si, kr * si + ki * sr], axis=1).astype(jnp.bfloat16)
    spread[...] = lanes_dft(product, inverse_ref[...])
    for pair in range(step // 2):
        items = [spread[pl.ds((2 * pair + one) * outer, outer), :] for one in range(2)]
        out = inverse_pair(items, last_ref[...], twiddle)
        conv_ref[:, pair] = out.reshape(conv_ref.shape[0], -1, LANES).astype(jnp.bfloat16)


def correlate_kernel(pairs_ref, signal_ref, filter_ref, first_ref, forward_ref, inverse_ref,
                     last_ref, twiddle_ref, out_ref, turned, spread):
    outer = twiddle_ref.shape[1]
    step = signal_ref.shape[0]
    twiddle = twiddle_ref[...]
    for pair in range(step // 2):
        pieces = forward_pair(pairs_ref[:, pair], first_ref[...], twiddle)
        for one in range(2):
            turned[pl.ds((2 * pair + one) * outer, outer), :] = pieces[one]
    half = step * outer
    grad = lanes_dft(turned[...], forward_ref[...])
    gr, gi = grad[:, :LANES], grad[:, LANES:]
    for place, ref in enumerate((filter_ref, signal_ref)):
        other = ref[...].reshape(half, 2 * LANES)
        kr, ki = other[:, :LANES], other[:, LANES:]
        product = jnp.concatenate([kr * gr + ki * gi, kr * gi - ki * gr], axis=1)
        spread[place] = lanes_dft(product.astype(jnp.bfloat16), inverse_ref[...])
    for chan in range(step):
        items = [spread[place, pl.ds(chan * outer, outer), :] for place in range(2)]
        out = inverse_pair(items, last_ref[...], twiddle)
        out_ref[:, chan] = out.reshape(out_ref.shape[0], -1, LANES).astype(jnp.bfloat16)


def whole(table):
    zeros = (0,) * table.ndim
    return pl.BlockSpec(table.shape, lambda i: zeros)


def convolve(pairs, tables):
    blocks, chans, rows, _ = pairs.shape
    step = min(32, chans)
    outer = blocks * rows // 2
    spec = in_hbm((chans, outer, 2 * LANES), jnp.float32)
    spec_block = pl.BlockSpec((step, outer, 2 * LANES), lambda i: (i, 0, 0))
    return pl.pallas_call(
        convolve_kernel,
        grid=(chans // step,),
        in_specs=[pl.BlockSpec((blocks, step, rows, LANES), lambda i: (0, i, 0, 0))]
        + [whole(table) for table in tables],
        out_specs=[
            pl.BlockSpec((blocks, step // 2, rows, LANES), lambda i: (0, i, 0, 0)),
            spec_block,
            spec_block,
        ],
        out_shape=[in_hbm((blocks, chans // 2, rows, LANES)), spec, spec],
        scratch_shapes=[
            pltpu.VMEM((2 * step * outer, 2 * LANES), jnp.bfloat16),
            pltpu.VMEM((step * outer, 2 * LANES), jnp.float32),
        ],
        compiler_params=pltpu.CompilerParams(vmem_limit_bytes=VMEM_BYTES),
        name="convolve",
    )(pairs, *held_in_hbm(*tables))


def correlate(pairs, signal, kernel, tables):
    blocks, _, rows, _ = pairs.shape
    chans = signal.shape[0]
    step = min(16, chans)
    outer = blocks * rows // 2
    spec_block = pl.BlockSpec((step, outer, 2 * LANES), lambda i: (i, 0, 0))
    return pl.pallas_call(
        correlate_kernel,
        grid=(chans // step,),
        in_specs=[
            pl.BlockSpec((blocks, step // 2, rows, LANES), lambda i: (0, i, 0, 0)),
            spec_block,
            spec_block,
        ]
        + [whole(table) for table in tables],
        out_specs=pl.BlockSpec((blocks, step, rows, LANES), lambda i: (0, i, 0, 0)),
        out_shape=in_hbm((blocks, chans, rows, LANES)),
        scratch_shapes=[
            pltpu.VMEM((step * outer, 2 * LANES), jnp.bfloat16),
            pltpu.VMEM((2, step * outer, 2 * LANES), jnp.float32),
        ],
        compiler_params=pltpu.CompilerParams(vmem_limit_bytes=VMEM_BYTES),
        name="correlate",
    )(pairs, *held_in_hbm(signal, kernel, *tables))


def params():
    return pltpu.CompilerParams(vmem_limit_bytes=VMEM_BYTES)


def spread_lanes(target, rows, first, stride):
    count = rows.shape[0]
    for lane in range(rows.shape[1] // LANES):
        target[pl.ds(first + lane, count, stride=stride), :] = rows[:, lane * LANES : (lane + 1) * LANES]


def prepare_kernel(gate_ref, signal_ref, filter_ref, pair_ref, lines):
    per = gate_ref.shape[1] // LANES
    spread_lanes(lines, short(wide(gate_ref[...]) * wide(signal_ref[...])).astype(jnp.float32), 0, 2 * per)
    spread_lanes(lines, wide(filter_ref[...]), per, 2 * per)
    held = lines[pl.ds(0, gate_ref.shape[0] * 2 * per), :]
    pair_ref[...] = short(held).reshape(pair_ref.shape)


def prepare(inner_gate, signal, long_filter):
    rows, length = signal.shape
    per = length // LANES
    step = rows // 2
    block = pl.BlockSpec((step, length), lambda i: (i, 0))
    return pl.pallas_call(
        prepare_kernel,
        grid=(2,),
        in_specs=[block] * 3,
        out_specs=pl.BlockSpec((step, 2 * per, LANES), lambda i: (i, 0, 0)),
        out_shape=in_hbm((rows, 2 * per, LANES)),
        scratch_shapes=[pltpu.VMEM(((step + 1) * 2 * per, LANES), jnp.float32)],
        compiler_params=params(),
        name="prepare",
    )(*held_in_hbm(inner_gate, signal, long_filter))


def regard_kernel(parts, flag_ref, gate_ref, *refs):
    *share_refs, sum_ref, grad_ref, grads = refs
    rows, length = gate_ref.shape
    per = length // LANES
    groups = []
    for count in parts:
        groups.append(share_refs[:count])
        share_refs = share_refs[count:]
    for lane in range(per):
        cols = slice(lane * LANES, (lane + 1) * LANES)
        shares = []
        for group in groups:
            held = group[lane * len(group) // per]
            at = lane % (per // len(group)) * LANES
            shares.append(wide(held[:, at : at + LANES]))
        grad_mix = shares[0]
        for share in shares[1:-1]:
            grad_mix = grad_mix + share
        grad_mix = grad_mix + jnp.where(flag_ref[0] != 0, shares[-1], jnp.zeros_like(shares[-1]))
        sum_ref[:, cols] = grad_mix
        grads[pl.ds(lane, rows, stride=per), :] = grad_mix * wide(gate_ref[:, cols])
    grad_ref[...] = short(grads[pl.ds(0, rows * per), :]).reshape(grad_ref.shape)


def regard(outer_gate, shares, flag):
    rows, length = outer_gate.shape
    parts = [len(share) for share in shares]
    cuts = [cut for share in shares for cut in share]
    per = length // LANES
    step = rows // 2
    token_rows = pl.BlockSpec((step, length), lambda i, at: (i, 0))
    return pl.pallas_call(
        functools.partial(regard_kernel, parts),
        grid_spec=pltpu.PrefetchScalarGridSpec(
            num_scalar_prefetch=1,
            grid=(2,),
            in_specs=[token_rows]
            + [pl.BlockSpec((step, cut.shape[1]), lambda i, at: (i, 0)) for cut in cuts],
            out_specs=[token_rows, pl.BlockSpec((step * per // 16, 16, LANES), lambda i, at: (i, 0, 0))],
            scratch_shapes=[pltpu.VMEM(((step + 1) * per, LANES), jnp.float32)],
        ),
        out_shape=[in_hbm((rows, length), jnp.float32), in_hbm((rows * per // 16, 16, LANES))],
        compiler_params=params(),
        name="regard",
    )(flag.astype(jnp.int32).reshape(1), outer_gate, *cuts)


def mix_kernel(conv_ref, gate_ref, mixed_ref, out_ref, lines):
    rows, length = gate_ref.shape
    per = length // LANES
    lines[pl.ds(0, rows * per), :] = wide(conv_ref[...].reshape(rows * per, LANES))
    for lane in range(per):
        cols = slice(lane * LANES, (lane + 1) * LANES)
        conv = lines[pl.ds(lane, rows, stride=per), :]
        out_ref[:, cols] = short(conv)
        mixed_ref[:, cols] = short(conv * wide(gate_ref[:, cols]))


def mix(conv, outer_gate):
    rows, length = outer_gate.shape
    per = length // LANES
    conv = conv.reshape(rows * per // 16, 16, LANES)
    step = rows // 2
    token_rows = pl.BlockSpec((step, length), lambda i: (i, 0))
    return pl.pallas_call(
        mix_kernel,
        grid=(2,),
        in_specs=[pl.BlockSpec((step * per // 16, 16, LANES), lambda i: (i, 0, 0)), token_rows],
        out_specs=[token_rows, token_rows],
        out_shape=[in_hbm((rows, length))] * 2,
        scratch_shapes=[pltpu.VMEM(((step + 1) * per, LANES), jnp.float32)],
        compiler_params=params(),
        name="mix",
    )(conv, outer_gate)


def finish_kernel(corr_ref, signal_ref, gate_ref, inner_ref, signal_out_ref, filter_ref, lines):
    rows, length = signal_ref.shape
    per = length // LANES
    lines[pl.ds(0, rows * 2 * per), :] = wide(corr_ref[...].reshape(rows * 2 * per, LANES))
    for lane in range(per):
        cols = slice(lane * LANES, (lane + 1) * LANES)
        grad_prod = lines[pl.ds(lane, rows, stride=2 * per), :]
        filter_ref[:, cols] = lines[pl.ds(per + lane, rows, stride=2 * per), :]
        inner_ref[:, cols] = short(grad_prod * wide(signal_ref[:, cols]))
        signal_out_ref[:, cols] = short(grad_prod * wide(gate_ref[:, cols]))


def finish(corr, signal, inner_gate):
    rows, length = signal.shape
    per = length // LANES
    step = rows // 2
    block = pl.BlockSpec((step, length), lambda i: (i, 0))
    return pl.pallas_call(
        finish_kernel,
        grid=(2,),
        in_specs=[pl.BlockSpec((step, 2 * per, LANES), lambda i: (i, 0, 0)), block, block],
        out_specs=[block] * 3,
        out_shape=[jax.ShapeDtypeStruct((rows, length), jnp.bfloat16)] * 2
        + [jax.ShapeDtypeStruct((rows, length), jnp.float32)],
        scratch_shapes=[pltpu.VMEM(((step + 1) * 2 * per, LANES), jnp.float32)],
        compiler_params=params(),
        name="finish",
    )(corr.reshape(rows, 2 * per, LANES), *held_in_hbm(signal, inner_gate))


def unproject_kernel(count, splits, add_from, place_ref, *refs):
    rows, width = refs[0].shape
    grad_ref, weights = refs[count], refs[-1]
    out_refs = refs[-1 - count * splits : -1]

    @pl.when(pl.program_id(0) == 0)
    def _():
        for row in range(count):
            weights[pl.ds(row * rows, rows), :] = refs[row][...]

    out = short(mxu(weights[...], grad_ref[...]))
    for row in range(count):
        part = out[row * rows : (row + 1) * rows]
        if add_from is not None:
            more = wide(refs[count + 1][...])
            part = short(wide(part) + jnp.where(place_ref[0] == add_from[row], more, jnp.zeros_like(more)))
        for split in range(splits):

            @pl.when(pl.program_id(0) * splits // pl.num_programs(0) == split)
            def _(part=part, ref=out_refs[row * splits + split]):
                ref[...] = part


def unproject(out_proj, grad_output, offsets, place, count, more=None, add_from=None, half=None, splits=1):
    width, length = grad_output.shape
    rows = out_proj.shape[0] // count
    step = 512 if half is None else 256
    length = length if half is None else length // 2
    first = 0 if half is None else half * (length // step)
    in_specs = [
        pl.BlockSpec((rows, width), lambda i, at, by=by: (lax.rem(at[0] + by, count), 0))
        for by in offsets
    ]
    out_block = pl.BlockSpec((rows, step), lambda i, at: (0, i if splits == 1 else 0))
    extra = [] if more is None else [more]
    return pl.pallas_call(
        functools.partial(unproject_kernel, len(offsets), splits, add_from),
        grid_spec=pltpu.PrefetchScalarGridSpec(
            num_scalar_prefetch=1,
            grid=(length // step,),
            in_specs=in_specs
            + [pl.BlockSpec((width, step), lambda i, at: (0, first + i))]
            + [out_block] * len(extra),
            out_specs=[out_block] * (len(offsets) * splits),
            scratch_shapes=[pltpu.VMEM((len(offsets) * rows, width), jnp.bfloat16)],
        ),
        out_shape=[in_hbm((rows, length // splits))] * (len(offsets) * splits),
        compiler_params=params(),
        cost_estimate=pl.CostEstimate(flops=40 * 10**9, bytes_accessed=10**8, transcendentals=0),
        name="unproject",
    )(place.reshape(1), *held_in_hbm(*[out_proj] * len(offsets), grad_output), *extra)


def project_kernel(core_ref, *refs):
    *piece_refs, grad_ref, other_ref, mine_ref, rows = refs
    count, small, _ = mine_ref.shape

    @pl.when(pl.program_id(0) == 0)
    def _():
        for place, which in enumerate((1 - core_ref[0], core_ref[0])):
            first = pl.multiple_of(which * small, small)
            for slot, piece in enumerate(piece_refs):
                rows[pl.ds((place * count + slot) * small, small), :] = piece[pl.ds(first, small), :]

    out = lax.dot_general(
        rows[...], grad_ref[...], (((1,), (1,)), ((), ())), preferred_element_type=jnp.float32
    )
    out = short(out).reshape(2, count, small, -1)
    other_ref[...] = out[0]
    mine_ref[...] = out[1]


def project(pieces, grad_output, core):
    width, length = grad_output.shape
    small = pieces[0].shape[0] // 2
    step = min(1024, width)
    out_block = pl.BlockSpec((len(pieces), small, step), lambda i, at: (0, 0, i))
    out = in_hbm((len(pieces), small, width))
    return pl.pallas_call(
        project_kernel,
        grid_spec=pltpu.PrefetchScalarGridSpec(
            num_scalar_prefetch=1,
            grid=(width // step,),
            in_specs=[pl.BlockSpec(pieces[0].shape, lambda i, at: (0, 0))] * len(pieces)
            + [pl.BlockSpec((step, length), lambda i, at: (i, 0))],
            out_specs=[out_block, out_block],
            scratch_shapes=[pltpu.VMEM((2 * len(pieces) * small, length), jnp.bfloat16)],
        ),
        out_shape=[out, out],
        compiler_params=params(),
        name="project",
    )(core.reshape(1), *pieces, *held_in_hbm(grad_output))


def swaps(count, bit):
    return [(place, place ^ bit) for place in range(count)]


def exchange(blocks):
    return lax.all_to_all(blocks, "seq", split_axis=0, concat_axis=0, tiled=True)


def tie(first, *others):
    return lax.optimization_barrier((first,) + others)[0]


def shift(block, by):
    count = lax.axis_size("chan")
    return lax.ppermute(block, "chan", [(i, (i + by) % count) for i in range(count)])


def gather_first(shard):
    count, place = lax.axis_size("chan"), lax.axis_index("chan")
    if count != 4:
        return [shard] + [shift(shard, by) for by in range(1, count)]
    return [shard, shift(shard, 1), shift(shard, 3)]


def both_cores(pieces, grad_output):
    count, core = lax.axis_size("seq"), lax.axis_index("seq") % 2
    rows = jnp.stack(pieces)
    sums = short(
        jnp.einsum("zct,dt->zcd", rows, grad_output, preferred_element_type=jnp.float32)
    ).reshape(len(pieces), 2, -1, grad_output.shape[0])
    got = lax.ppermute(lax.dynamic_index_in_dim(sums, 1 - core, 1, False), "seq", swaps(count, 1))
    return short(wide(lax.dynamic_index_in_dim(sums, core, 1, False)) + wide(got))


def scatter_chips(total, meanwhile):
    count, chips = lax.axis_size("seq"), lax.axis_size("chan")
    line, chip = lax.axis_index("chan"), lax.axis_index("seq") // 2
    rows, width = total.shape[1:]

    def block(bit):
        return lax.dynamic_index_in_dim(total, (line - (chip ^ bit)) % chips, 0, False)

    if chips != 4:
        bits = sorted(range(1, chips), key=lambda bit: (-bin(bit).count("1"), bit))
        parts = [lax.ppermute(block(bit), "seq", swaps(count, 2 * bit)) for bit in bits] + [block(0)]
        grads = meanwhile(parts[-1])
        return sum_of(parts), grads

    def part(bit, half):
        at = ((line - (chip ^ bit)) % chips, half * (rows // 2), 0)
        return lax.dynamic_slice(total, at, (1, rows // 2, width))[0]

    along_x = lax.ppermute(jnp.stack([part(1, 0), part(3, 0)]), "seq", swaps(count, 2))
    along_y = lax.ppermute(jnp.stack([part(2, 1), part(3, 1)]), "seq", swaps(count, 4))
    grads = meanwhile(total)
    along_x, along_y = tie((along_x, along_y), grads)
    then_y = lax.ppermute(short(wide(part(2, 0)) + wide(along_x[1])), "seq", swaps(count, 4))
    then_x = lax.ppermute(short(wide(part(1, 1)) + wide(along_y[1])), "seq", swaps(count, 2))
    halves = [
        sum_of([part(0, 0), along_x[0], then_y]),
        sum_of([part(0, 1), along_y[0], then_x]),
    ]
    return jnp.concatenate(halves, axis=0), grads


def sum_of(parts):
    total = wide(parts[0])
    for part in parts[1:]:
        total = total + wide(part)
    return total


def body(outer_gate, inner_gate, signal, long_filter, grad_output, out_proj):
    seq_count, chan_count = lax.axis_size("seq"), lax.axis_size("chan")
    chan_rows, block_len = outer_gate.shape
    owned = chan_rows // seq_count
    per = block_len // LANES
    line = lax.axis_index("chan")
    tables = [jnp.asarray(t) for t in dft_tables(block_len * seq_count, seq_count)]

    if chan_count == 4:
        fars = unproject(out_proj, grad_output, [2], line, chan_count, splits=2)
        pair = prepare(inner_gate, signal, tie(long_filter, *fars))
        pair = pair.reshape(seq_count, owned, 2 * per, LANES)
        fars = [fars[0], tie(fars[1], pair)]
        fars = [lax.ppermute(far, "chan", [(2, 0), (1, 3), (3, 2), (0, 1)]) for far in fars]
        sent = exchange(pair)
        after, ups, downs = pair, [], []
        for half, far in enumerate(fars):
            near = unproject(
                tie(out_proj, after), grad_output, [1, 3], line, chan_count, far, [1, 2], half
            )
            ups.append(shift(near[0], 1))
            downs.append(shift(near[1], 3))
            after = near[1]
        sent = tie(sent, after)
        shares = [ups, downs, fars]
        flag = (line == 0) | (line == 3)
    else:
        pair = prepare(inner_gate, signal, long_filter)
        pair = pair.reshape(seq_count, owned, 2 * per, LANES)
        sent = exchange(pair)
        offsets = list(range(1, chan_count))
        blocks = unproject(out_proj, grad_output, offsets, line, chan_count)
        shares = [[shift(block, by)] for by, block in zip(offsets, blocks)]
        flag = line >= 0

    conv, spec_signal, spec_filter = convolve(sent, tables)
    own = unproject(tie(out_proj, conv), grad_output, [0], line, chan_count)
    shares = [held_in_hbm(*own), *shares]
    grad_mix, grad_conv = regard(outer_gate, shares, flag)
    mixed, conv_out = mix(tie(exchange(conv), grad_conv), outer_gate)
    held = gather_first(mixed)
    grad_conv = tie(grad_conv, mixed).reshape(seq_count, owned // 2, 2 * per, LANES)
    corr = correlate(exchange(grad_conv), spec_signal, spec_filter, tables)
    held = tie(held, corr)
    if chan_count == 4:
        passed = lax.select_n(line, held[0], held[2], held[1], held[0])
        middle = lax.ppermute(passed, "chan", [(0, 2), (3, 1), (2, 3), (1, 0)])
        corr = exchange(corr)
        held = tie(held, passed)
        core = lax.axis_index("seq") % 2
        other, mine = project([held[0], held[1], held[0], held[2]], grad_output, core)
        middle, other = lax.optimization_barrier((middle, other, corr))[:2]
        got = lax.ppermute(other, "seq", swaps(seq_count, 1))
        middle = both_cores([middle], grad_output)
        total = short(wide(mine) + wide(got))
        total = lax.dynamic_update_slice(total, middle, (2, 0, 0))
    else:
        corr = exchange(corr)
        total = both_cores(held, grad_output)
    grad_proj, grads = scatter_chips(
        total, lambda before: finish(tie(corr, before), signal, inner_gate)
    )
    grad_outer = short(tie(grad_mix, corr) * wide(conv_out))
    return (grad_outer, *grads, grad_proj)


def solution(mesh):
    tokens = P("chan", "seq")
    in_specs = (tokens, tokens, tokens, tokens, tokens, P(None, "chan"))
    out_specs = (tokens, tokens, tokens, tokens, P("seq", "chan"))
    return jax.shard_map(body, mesh=mesh, in_specs=in_specs, out_specs=out_specs, check_vma=False)
```

```python
import functools
import math

import jax
import jax.numpy as jnp
import numpy as np
from jax import lax
from jax.experimental import pallas as pl
from jax.experimental.pallas import tpu as pltpu
from jax.sharding import PartitionSpec as P

LANES = 128
VMEM_BYTES = 48 * 1024 * 1024


def wide(x):
    return x.astype(jnp.float32)


def short(x):
    return x.astype(jnp.bfloat16)


def held_in_hbm(*arrays):
    return [pltpu.with_memory_space_constraint(array, pltpu.HBM) for array in arrays]


def in_hbm(shape, dtype=jnp.bfloat16):
    return pltpu.HBM(shape, dtype)


def high_low(table, axis):
    high = table.astype(jnp.bfloat16)
    low = (table - high.astype(np.float64)).astype(jnp.bfloat16)
    return np.concatenate([high, low], axis=axis)


def dft_tables(tokens, blocks):
    outer = tokens // LANES
    per = outer // blocks
    freq = np.arange(outer) + 0.25
    angle = 2.0 * math.pi / outer * np.outer(freq, np.arange(outer))
    first = np.zeros((2, 2, outer, blocks, 2, per))
    last = np.zeros((blocks, 2, per, 2, 2, outer))
    for pair in range(2):
        first[pair, 0, :, :, pair, :] = np.cos(angle).reshape(outer, blocks, per)
        first[pair, 1, :, :, pair, :] = -np.sin(angle).reshape(outer, blocks, per)
        last[:, pair, :, pair, 0, :] = np.cos(angle.T).reshape(blocks, per, outer) / tokens
        last[:, pair, :, pair, 1, :] = -np.sin(angle.T).reshape(blocks, per, outer) / tokens
    first = first.reshape(4 * outer, 2 * outer).astype(jnp.bfloat16)
    last = high_low(last.reshape(2 * outer, 4 * outer), 1)
    turn = 2.0 * math.pi / tokens * np.outer(freq, np.arange(LANES))
    twiddle = np.stack([np.cos(turn), np.sin(turn)]).astype(np.float32)
    lane = 2.0 * math.pi / LANES * np.outer(np.arange(LANES), np.arange(LANES))
    cos, sin = np.cos(lane), np.sin(lane)
    forward = np.block([[cos, -sin], [sin, cos]]).astype(jnp.bfloat16)
    inverse = np.block([[cos, sin], [-sin, cos]]).astype(jnp.bfloat16)
    return first, forward, inverse, last, twiddle


def mxu(left, right):
    return jnp.dot(left, right, preferred_element_type=jnp.float32)


def forward_pair(pair_block, first, twiddle):
    outer = twiddle.shape[1]
    rows = pair_block.reshape(2 * outer, LANES)
    part = mxu(first, rows)
    cos, sin = twiddle[0], twiddle[1]
    turned = []
    for pair in range(2):
        real = part[2 * pair * outer : (2 * pair + 1) * outer]
        imag = part[(2 * pair + 1) * outer : (2 * pair + 2) * outer]
        turned.append(
            jnp.concatenate([real * cos + imag * sin, imag * cos - real * sin], axis=1).astype(
                jnp.bfloat16
            )
        )
    return turned


def inverse_pair(spread, last, twiddle):
    cos, sin = twiddle[0], twiddle[1]
    parts = []
    for item in spread:
        real, imag = item[:, :LANES], item[:, LANES:]
        parts.append((real * cos - imag * sin).astype(jnp.bfloat16))
        parts.append((real * sin + imag * cos).astype(jnp.bfloat16))
    return mxu(last, jnp.concatenate(parts + parts, axis=0))


def lanes_dft(rows, table):
    return mxu(rows, table)


def convolve_kernel(pairs_ref, first_ref, forward_ref, inverse_ref, last_ref, twiddle_ref,
                    conv_ref, signal_ref, filter_ref, turned, spread):
    outer = twiddle_ref.shape[1]
    step = pairs_ref.shape[1]
    twiddle = twiddle_ref[...]
    for chan in range(step):
        pieces = forward_pair(pairs_ref[:, chan], first_ref[...], twiddle)
        for pair in range(2):
            turned[pl.ds((pair * step + chan) * outer, outer), :] = pieces[pair]
    half = step * outer
    signal = lanes_dft(turned[pl.ds(0, half), :], forward_ref[...])
    kernel = lanes_dft(turned[pl.ds(half, half), :], forward_ref[...])
    signal_ref[...] = signal.reshape(signal_ref.shape)
    filter_ref[...] = kernel.reshape(filter_ref.shape)
    sr, si = signal[:, :LANES], signal[:, LANES:]
    kr, ki = kernel[:, :LANES], kernel[:, LANES:]
    product = jnp.concatenate([kr * sr - ki * si, kr * si + ki * sr], axis=1).astype(jnp.bfloat16)
    spread[...] = lanes_dft(product, inverse_ref[...])
    for pair in range(step // 2):
        items = [spread[pl.ds((2 * pair + one) * outer, outer), :] for one in range(2)]
        out = inverse_pair(items, last_ref[...], twiddle)
        conv_ref[:, pair] = out.reshape(conv_ref.shape[0], -1, LANES).astype(jnp.bfloat16)


def correlate_kernel(pairs_ref, signal_ref, filter_ref, first_ref, forward_ref, inverse_ref,
                     last_ref, twiddle_ref, out_ref, turned, spread):
    outer = twiddle_ref.shape[1]
    step = signal_ref.shape[0]
    twiddle = twiddle_ref[...]
    for pair in range(step // 2):
        pieces = forward_pair(pairs_ref[:, pair], first_ref[...], twiddle)
        for one in range(2):
            turned[pl.ds((2 * pair + one) * outer, outer), :] = pieces[one]
    half = step * outer
    grad = lanes_dft(turned[...], forward_ref[...])
    gr, gi = grad[:, :LANES], grad[:, LANES:]
    for place, ref in enumerate((filter_ref, signal_ref)):
        other = ref[...].reshape(half, 2 * LANES)
        kr, ki = other[:, :LANES], other[:, LANES:]
        product = jnp.concatenate([kr * gr + ki * gi, kr * gi - ki * gr], axis=1)
        spread[place] = lanes_dft(product.astype(jnp.bfloat16), inverse_ref[...])
    for chan in range(step):
        items = [spread[place, pl.ds(chan * outer, outer), :] for place in range(2)]
        out = inverse_pair(items, last_ref[...], twiddle)
        out_ref[:, chan] = out.reshape(out_ref.shape[0], -1, LANES).astype(jnp.bfloat16)


def whole(table):
    zeros = (0,) * table.ndim
    return pl.BlockSpec(table.shape, lambda i: zeros)


def convolve(pairs, tables):
    blocks, chans, rows, _ = pairs.shape
    step = min(32, chans)
    outer = blocks * rows // 2
    spec = in_hbm((chans, outer, 2 * LANES), jnp.float32)
    spec_block = pl.BlockSpec((step, outer, 2 * LANES), lambda i: (i, 0, 0))
    return pl.pallas_call(
        convolve_kernel,
        grid=(chans // step,),
        in_specs=[pl.BlockSpec((blocks, step, rows, LANES), lambda i: (0, i, 0, 0))]
        + [whole(table) for table in tables],
        out_specs=[
            pl.BlockSpec((blocks, step // 2, rows, LANES), lambda i: (0, i, 0, 0)),
            spec_block,
            spec_block,
        ],
        out_shape=[in_hbm((blocks, chans // 2, rows, LANES)), spec, spec],
        scratch_shapes=[
            pltpu.VMEM((2 * step * outer, 2 * LANES), jnp.bfloat16),
            pltpu.VMEM((step * outer, 2 * LANES), jnp.float32),
        ],
        compiler_params=pltpu.CompilerParams(vmem_limit_bytes=VMEM_BYTES),
        name="convolve",
    )(pairs, *held_in_hbm(*tables))


def correlate(pairs, signal, kernel, tables):
    blocks, _, rows, _ = pairs.shape
    chans = signal.shape[0]
    step = min(16, chans)
    outer = blocks * rows // 2
    spec_block = pl.BlockSpec((step, outer, 2 * LANES), lambda i: (i, 0, 0))
    return pl.pallas_call(
        correlate_kernel,
        grid=(chans // step,),
        in_specs=[
            pl.BlockSpec((blocks, step // 2, rows, LANES), lambda i: (0, i, 0, 0)),
            spec_block,
            spec_block,
        ]
        + [whole(table) for table in tables],
        out_specs=pl.BlockSpec((blocks, step, rows, LANES), lambda i: (0, i, 0, 0)),
        out_shape=in_hbm((blocks, chans, rows, LANES)),
        scratch_shapes=[
            pltpu.VMEM((step * outer, 2 * LANES), jnp.bfloat16),
            pltpu.VMEM((2, step * outer, 2 * LANES), jnp.float32),
        ],
        compiler_params=pltpu.CompilerParams(vmem_limit_bytes=VMEM_BYTES),
        name="correlate",
    )(pairs, *held_in_hbm(signal, kernel, *tables))


def params():
    return pltpu.CompilerParams(vmem_limit_bytes=VMEM_BYTES)


def spread_lanes(target, rows, first, stride):
    count = rows.shape[0]
    for lane in range(rows.shape[1] // LANES):
        target[pl.ds(first + lane, count, stride=stride), :] = rows[:, lane * LANES : (lane + 1) * LANES]


def prepare_kernel(gate_ref, signal_ref, filter_ref, pair_ref, lines):
    per = gate_ref.shape[1] // LANES
    spread_lanes(lines, short(wide(gate_ref[...]) * wide(signal_ref[...])).astype(jnp.float32), 0, 2 * per)
    spread_lanes(lines, wide(filter_ref[...]), per, 2 * per)
    held = lines[pl.ds(0, gate_ref.shape[0] * 2 * per), :]
    pair_ref[...] = short(held).reshape(pair_ref.shape)


def prepare(inner_gate, signal, long_filter):
    rows, length = signal.shape
    per = length // LANES
    step = rows // 2
    block = pl.BlockSpec((step, length), lambda i: (i, 0))
    return pl.pallas_call(
        prepare_kernel,
        grid=(2,),
        in_specs=[block] * 3,
        out_specs=pl.BlockSpec((step, 2 * per, LANES), lambda i: (i, 0, 0)),
        out_shape=in_hbm((rows, 2 * per, LANES)),
        scratch_shapes=[pltpu.VMEM(((step + 1) * 2 * per, LANES), jnp.float32)],
        compiler_params=params(),
        name="prepare",
    )(*held_in_hbm(inner_gate, signal, long_filter))


def regard_kernel(parts, flag_ref, gate_ref, *refs):
    *share_refs, sum_ref, grad_ref, grads = refs
    rows, length = gate_ref.shape
    per = length // LANES
    groups = []
    for count in parts:
        groups.append(share_refs[:count])
        share_refs = share_refs[count:]
    for lane in range(per):
        cols = slice(lane * LANES, (lane + 1) * LANES)
        shares = []
        for group in groups:
            held = group[lane * len(group) // per]
            at = lane % (per // len(group)) * LANES
            shares.append(wide(held[:, at : at + LANES]))
        grad_mix = shares[0]
        for share in shares[1:-1]:
            grad_mix = grad_mix + share
        grad_mix = grad_mix + jnp.where(flag_ref[0] != 0, shares[-1], jnp.zeros_like(shares[-1]))
        sum_ref[:, cols] = grad_mix
        grads[pl.ds(lane, rows, stride=per), :] = grad_mix * wide(gate_ref[:, cols])
    grad_ref[...] = short(grads[pl.ds(0, rows * per), :]).reshape(grad_ref.shape)


def regard(outer_gate, shares, flag):
    rows, length = outer_gate.shape
    parts = [len(share) for share in shares]
    cuts = [cut for share in shares for cut in share]
    per = length // LANES
    step = rows // 2
    token_rows = pl.BlockSpec((step, length), lambda i, at: (i, 0))
    return pl.pallas_call(
        functools.partial(regard_kernel, parts),
        grid_spec=pltpu.PrefetchScalarGridSpec(
            num_scalar_prefetch=1,
            grid=(2,),
            in_specs=[token_rows]
            + [pl.BlockSpec((step, cut.shape[1]), lambda i, at: (i, 0)) for cut in cuts],
            out_specs=[token_rows, pl.BlockSpec((step * per // 16, 16, LANES), lambda i, at: (i, 0, 0))],
            scratch_shapes=[pltpu.VMEM(((step + 1) * per, LANES), jnp.float32)],
        ),
        out_shape=[in_hbm((rows, length), jnp.float32), in_hbm((rows * per // 16, 16, LANES))],
        compiler_params=params(),
        name="regard",
    )(flag.astype(jnp.int32).reshape(1), outer_gate, *cuts)


def mix_kernel(conv_ref, gate_ref, mixed_ref, out_ref, lines):
    rows, length = gate_ref.shape
    per = length // LANES
    lines[pl.ds(0, rows * per), :] = wide(conv_ref[...].reshape(rows * per, LANES))
    for lane in range(per):
        cols = slice(lane * LANES, (lane + 1) * LANES)
        conv = lines[pl.ds(lane, rows, stride=per), :]
        out_ref[:, cols] = short(conv)
        mixed_ref[:, cols] = short(conv * wide(gate_ref[:, cols]))


def mix(conv, outer_gate):
    rows, length = outer_gate.shape
    per = length // LANES
    conv = conv.reshape(rows * per // 16, 16, LANES)
    step = rows // 2
    token_rows = pl.BlockSpec((step, length), lambda i: (i, 0))
    return pl.pallas_call(
        mix_kernel,
        grid=(2,),
        in_specs=[pl.BlockSpec((step * per // 16, 16, LANES), lambda i: (i, 0, 0)), token_rows],
        out_specs=[token_rows, token_rows],
        out_shape=[in_hbm((rows, length))] * 2,
        scratch_shapes=[pltpu.VMEM(((step + 1) * per, LANES), jnp.float32)],
        compiler_params=params(),
        name="mix",
    )(conv, outer_gate)


def finish_kernel(corr_ref, signal_ref, gate_ref, inner_ref, signal_out_ref, filter_ref, lines):
    rows, length = signal_ref.shape
    per = length // LANES
    lines[pl.ds(0, rows * 2 * per), :] = wide(corr_ref[...].reshape(rows * 2 * per, LANES))
    for lane in range(per):
        cols = slice(lane * LANES, (lane + 1) * LANES)
        grad_prod = lines[pl.ds(lane, rows, stride=2 * per), :]
        filter_ref[:, cols] = lines[pl.ds(per + lane, rows, stride=2 * per), :]
        inner_ref[:, cols] = short(grad_prod * wide(signal_ref[:, cols]))
        signal_out_ref[:, cols] = short(grad_prod * wide(gate_ref[:, cols]))


def finish(corr, signal, inner_gate):
    rows, length = signal.shape
    per = length // LANES
    step = rows // 2
    block = pl.BlockSpec((step, length), lambda i: (i, 0))
    return pl.pallas_call(
        finish_kernel,
        grid=(2,),
        in_specs=[pl.BlockSpec((step, 2 * per, LANES), lambda i: (i, 0, 0)), block, block],
        out_specs=[block] * 3,
        out_shape=[jax.ShapeDtypeStruct((rows, length), jnp.bfloat16)] * 2
        + [jax.ShapeDtypeStruct((rows, length), jnp.float32)],
        scratch_shapes=[pltpu.VMEM(((step + 1) * 2 * per, LANES), jnp.float32)],
        compiler_params=params(),
        name="finish",
    )(corr.reshape(rows, 2 * per, LANES), *held_in_hbm(signal, inner_gate))


def unproject_kernel(count, splits, add_from, place_ref, *refs):
    rows, width = refs[0].shape
    grad_ref, weights = refs[count], refs[-1]
    out_refs = refs[-1 - count * splits : -1]

    @pl.when(pl.program_id(0) == 0)
    def _():
        for row in range(count):
            weights[pl.ds(row * rows, rows), :] = refs[row][...]

    out = short(mxu(weights[...], grad_ref[...]))
    for row in range(count):
        part = out[row * rows : (row + 1) * rows]
        if add_from is not None:
            more = wide(refs[count + 1][...])
            part = short(wide(part) + jnp.where(place_ref[0] == add_from[row], more, jnp.zeros_like(more)))
        for split in range(splits):

            @pl.when(pl.program_id(0) * splits // pl.num_programs(0) == split)
            def _(part=part, ref=out_refs[row * splits + split]):
                ref[...] = part


def unproject(out_proj, grad_output, offsets, place, count, more=None, add_from=None, half=None, splits=1):
    width, length = grad_output.shape
    rows = out_proj.shape[0] // count
    step = 512 if half is None else 256
    length = length if half is None else length // 2
    first = 0 if half is None else half * (length // step)
    in_specs = [
        pl.BlockSpec((rows, width), lambda i, at, by=by: (lax.rem(at[0] + by, count), 0))
        for by in offsets
    ]
    out_block = pl.BlockSpec((rows, step), lambda i, at: (0, i if splits == 1 else 0))
    extra = [] if more is None else [more]
    return pl.pallas_call(
        functools.partial(unproject_kernel, len(offsets), splits, add_from),
        grid_spec=pltpu.PrefetchScalarGridSpec(
            num_scalar_prefetch=1,
            grid=(length // step,),
            in_specs=in_specs
            + [pl.BlockSpec((width, step), lambda i, at: (0, first + i))]
            + [out_block] * len(extra),
            out_specs=[out_block] * (len(offsets) * splits),
            scratch_shapes=[pltpu.VMEM((len(offsets) * rows, width), jnp.bfloat16)],
        ),
        out_shape=[in_hbm((rows, length // splits))] * (len(offsets) * splits),
        compiler_params=params(),
        cost_estimate=pl.CostEstimate(flops=40 * 10**9, bytes_accessed=10**8, transcendentals=0),
        name="unproject",
    )(place.reshape(1), *held_in_hbm(*[out_proj] * len(offsets), grad_output), *extra)


def project_kernel(core_ref, *refs):
    *piece_refs, grad_ref, other_ref, mine_ref, rows = refs
    count, small, _ = mine_ref.shape

    @pl.when(pl.program_id(0) == 0)
    def _():
        for place, which in enumerate((1 - core_ref[0], core_ref[0])):
            first = pl.multiple_of(which * small, small)
            for slot, piece in enumerate(piece_refs):
                rows[pl.ds((place * count + slot) * small, small), :] = piece[pl.ds(first, small), :]

    out = lax.dot_general(
        rows[...], grad_ref[...], (((1,), (1,)), ((), ())), preferred_element_type=jnp.float32
    )
    out = short(out).reshape(2, count, small, -1)
    other_ref[...] = out[0]
    mine_ref[...] = out[1]


def project(pieces, grad_output, core):
    width, length = grad_output.shape
    small = pieces[0].shape[0] // 2
    step = min(1024, width)
    out_block = pl.BlockSpec((len(pieces), small, step), lambda i, at: (0, 0, i))
    out = in_hbm((len(pieces), small, width))
    return pl.pallas_call(
        project_kernel,
        grid_spec=pltpu.PrefetchScalarGridSpec(
            num_scalar_prefetch=1,
            grid=(width // step,),
            in_specs=[pl.BlockSpec(pieces[0].shape, lambda i, at: (0, 0))] * len(pieces)
            + [pl.BlockSpec((step, length), lambda i, at: (i, 0))],
            out_specs=[out_block, out_block],
            scratch_shapes=[pltpu.VMEM((2 * len(pieces) * small, length), jnp.bfloat16)],
        ),
        out_shape=[out, out],
        compiler_params=params(),
        name="project",
    )(core.reshape(1), *pieces, *held_in_hbm(grad_output))


def swaps(count, bit):
    return [(place, place ^ bit) for place in range(count)]


def exchange(blocks):
    return lax.all_to_all(blocks, "seq", split_axis=0, concat_axis=0, tiled=True)


def tie(first, *others):
    return lax.optimization_barrier((first,) + others)[0]


def shift(block, by):
    count = lax.axis_size("chan")
    return lax.ppermute(block, "chan", [(i, (i + by) % count) for i in range(count)])


def gather_first(shard):
    count, place = lax.axis_size("chan"), lax.axis_index("chan")
    if count != 4:
        return [shard] + [shift(shard, by) for by in range(1, count)]
    return [shard, shift(shard, 1), shift(shard, 3)]


def both_cores(pieces, grad_output):
    count, core = lax.axis_size("seq"), lax.axis_index("seq") % 2
    rows = jnp.stack(pieces)
    sums = short(
        jnp.einsum("zct,dt->zcd", rows, grad_output, preferred_element_type=jnp.float32)
    ).reshape(len(pieces), 2, -1, grad_output.shape[0])
    got = lax.ppermute(lax.dynamic_index_in_dim(sums, 1 - core, 1, False), "seq", swaps(count, 1))
    return short(wide(lax.dynamic_index_in_dim(sums, core, 1, False)) + wide(got))


def scatter_chips(total, meanwhile):
    count, chips = lax.axis_size("seq"), lax.axis_size("chan")
    line, chip = lax.axis_index("chan"), lax.axis_index("seq") // 2
    rows, width = total.shape[1:]

    def block(bit):
        return lax.dynamic_index_in_dim(total, (line - (chip ^ bit)) % chips, 0, False)

    if chips != 4:
        bits = sorted(range(1, chips), key=lambda bit: (-bin(bit).count("1"), bit))
        parts = [lax.ppermute(block(bit), "seq", swaps(count, 2 * bit)) for bit in bits] + [block(0)]
        grads = meanwhile(parts[-1])
        return sum_of(parts), grads

    def part(bit, half):
        at = ((line - (chip ^ bit)) % chips, half * (rows // 2), 0)
        return lax.dynamic_slice(total, at, (1, rows // 2, width))[0]

    along_x = lax.ppermute(jnp.stack([part(1, 0), part(3, 0)]), "seq", swaps(count, 2))
    along_y = lax.ppermute(jnp.stack([part(2, 1), part(3, 1)]), "seq", swaps(count, 4))
    grads = meanwhile(total)
    along_x, along_y = tie((along_x, along_y), grads)
    then_y = lax.ppermute(short(wide(part(2, 0)) + wide(along_x[1])), "seq", swaps(count, 4))
    then_x = lax.ppermute(short(wide(part(1, 1)) + wide(along_y[1])), "seq", swaps(count, 2))
    halves = [
        sum_of([part(0, 0), along_x[0], then_y]),
        sum_of([part(0, 1), along_y[0], then_x]),
    ]
    return jnp.concatenate(halves, axis=0), grads


def sum_of(parts):
    total = wide(parts[0])
    for part in parts[1:]:
        total = total + wide(part)
    return total


def body(outer_gate, inner_gate, signal, long_filter, grad_output, out_proj):
    seq_count, chan_count = lax.axis_size("seq"), lax.axis_size("chan")
    chan_rows, block_len = outer_gate.shape
    owned = chan_rows // seq_count
    per = block_len // LANES
    line = lax.axis_index("chan")
    tables = [jnp.asarray(t) for t in dft_tables(block_len * seq_count, seq_count)]

    if chan_count == 4:
        fars = unproject(out_proj, grad_output, [2], line, chan_count, splits=2)
        pair = prepare(inner_gate, signal, tie(long_filter, *fars))
        pair = pair.reshape(seq_count, owned, 2 * per, LANES)
        fars = [fars[0], tie(fars[1], pair)]
        fars = [lax.ppermute(far, "chan", [(2, 0), (1, 3), (3, 2), (0, 1)]) for far in fars]
        sent = exchange(pair)
        after, ups, downs = pair, [], []
        for half, far in enumerate(fars):
            near = unproject(
                tie(out_proj, after), grad_output, [1, 3], line, chan_count, far, [1, 2], half
            )
            ups.append(shift(near[0], 1))
            downs.append(shift(near[1], 3))
            after = near[1]
        sent = tie(sent, after)
        shares = [ups, downs, fars]
        flag = (line == 0) | (line == 3)
    else:
        pair = prepare(inner_gate, signal, long_filter)
        pair = pair.reshape(seq_count, owned, 2 * per, LANES)
        sent = exchange(pair)
        offsets = list(range(1, chan_count))
        blocks = unproject(out_proj, grad_output, offsets, line, chan_count)
        shares = [[shift(block, by)] for by, block in zip(offsets, blocks)]
        flag = line >= 0

    conv, spec_signal, spec_filter = convolve(sent, tables)
    own = unproject(tie(out_proj, conv), grad_output, [0], line, chan_count)
    shares = [held_in_hbm(*own), *shares]
    grad_mix, grad_conv = regard(outer_gate, shares, flag)
    mixed, conv_out = mix(exchange(conv), outer_gate)
    held = gather_first(mixed)
    grad_conv = tie(grad_conv, mixed).reshape(seq_count, owned // 2, 2 * per, LANES)
    corr = correlate(exchange(grad_conv), spec_signal, spec_filter, tables)
    held = tie(held, corr)
    if chan_count == 4:
        passed = lax.select_n(line, held[0], held[2], held[1], held[0])
        middle = lax.ppermute(passed, "chan", [(0, 2), (3, 1), (2, 3), (1, 0)])
        corr = exchange(corr)
        held = tie(held, passed)
        core = lax.axis_index("seq") % 2
        other, mine = project([held[0], held[1], held[0], held[2]], grad_output, core)
        middle, other = lax.optimization_barrier((middle, other, corr))[:2]
        got = lax.ppermute(other, "seq", swaps(seq_count, 1))
        middle = both_cores([middle], grad_output)
        total = short(wide(mine) + wide(got))
        total = lax.dynamic_update_slice(total, middle, (2, 0, 0))
    else:
        corr = exchange(corr)
        total = both_cores(held, grad_output)
    grad_proj, grads = scatter_chips(
        total, lambda before: finish(tie(corr, before), signal, inner_gate)
    )
    grad_outer = short(tie(grad_mix, corr) * wide(conv_out))
    return (grad_outer, *grads, grad_proj)


def solution(mesh):
    tokens = P("chan", "seq")
    in_specs = (tokens, tokens, tokens, tokens, tokens, P(None, "chan"))
    out_specs = (tokens, tokens, tokens, tokens, P("seq", "chan"))
    return jax.shard_map(body, mesh=mesh, in_specs=in_specs, out_specs=out_specs, check_vma=False)
```
